32 devices in a mesh: wide: 16 (over z, y, x), narrow: 2 (over core).
Axes of the slice: x: 2, y: 2, z: 4, core: 2. Of those that a mesh axis runs over, the one named last changes fastest.
Arguments:
- tokens: bfloat16 [16, 12288, 512], P('narrow', 'wide')
- cotangent: bfloat16 [16, 12288, 512], P('narrow', 'wide'), may hold values from -6 to 6
- owner_list: int32 [12], replicated, may hold values from 0 to 15, as said below
- master: float32 [16, 512, 512], P('wide', 'narrow')
- moment_one: float32 [16, 512, 512], P('wide', 'narrow'), may hold values from -112 to 112
- moment_two: float32 [16, 512, 512], P('wide', 'narrow'), may hold values from 825.7536 to 13172.736
- small_params: float32 [4608], replicated
- small_one: float32 [4608], replicated, may hold values from -128 to 128
- small_two: float32 [4608], replicated, may hold values from 1297.6128 to 20643.84
Outputs:
- block_out: bfloat16 [16, 12288, 512], P('narrow', 'wide')
- grad_tokens: float32 [16, 12288, 512], P('narrow', 'wide')
- new_master: float32 [16, 512, 512], P('wide', 'narrow')
- new_one: float32 [16, 512, 512], P('wide', 'narrow')
- new_two: float32 [16, 512, 512], P('wide', 'narrow')
- small_new: float32 [4608], replicated
- small_one_new: float32 [4608], replicated
- small_two_new: float32 [4608], replicated
The draws below stay inside these ranges and needn't reach their ends.
Inputs may be any that keep to these rules, and one draw needn't show every extreme that they name: `owner_list`: 12 different slot indices; 0 and 15 are always among them.
All inputs are finite; a program needn't handle non-finite values.
Results may differ from the reference program's by a relative error of at most 0.025.
Values may be sent and summed in bfloat16 or wider, within the bound.
No kernel may reach another device: no remote copies, remote signals or barrier semaphores. Data moves between devices by JAX's collectives and lax.ppermute only.
A program may use at most 512 MiB of HBM per device.

```python
import math
import jax
import jax.numpy as jnp
from jax import lax

D = 512
HEADS = 8
HD = 64
FF = 2048
ROW = 192
ROWS_IMG = 64
STEP = 10
SEQ = 12288
IMAGES = 16
TOKENS = 196608
NF = 4
NBLK = 12
SLOTS = 16
SMALL = 4608


def owner_draw(key):
    middle_key, order_key = jax.random.split(jax.random.fold_in(key, 5))
    middle = jax.random.permutation(middle_key, SLOTS - 2)[:NBLK - 2] + 1
    chosen = jnp.concatenate([jnp.array([0, SLOTS - 1], jnp.int32), middle.astype(jnp.int32)])
    return jax.random.permutation(order_key, chosen).astype(jnp.int32)


def draw_owner_list(key, part):
    return owner_draw(key)


def draw_master(key, part):
    owners = owner_draw(key)
    key = jax.random.fold_in(key, 7)
    numbers = jnp.arange(NBLK, dtype=jnp.int32)
    block_std = jnp.where(numbers == 3, 4.0 * D ** (-0.5), jnp.where(numbers >= 4 + FF // D, FF ** (-0.5), D ** (-0.5)))
    slot_std = jnp.full((SLOTS,), D ** (-0.5), jnp.float32).at[owners].set(block_std.astype(jnp.float32))
    entries = jnp.clip(jax.random.normal(key, (SLOTS, D, D), jnp.float32), -4.0, 4.0)
    return entries * slot_std[:, None, None]


def draw_tokens(key, part):
    key = jax.random.fold_in(key, 11)
    common_key, noise_key = jax.random.split(key)
    common = jax.random.normal(common_key, (IMAGES, ROWS_IMG, 1, D), jnp.float32)
    noise = jax.random.normal(noise_key, (IMAGES, ROWS_IMG, ROW, D), jnp.float32)
    mixed = jnp.clip(0.8 * common + 0.6 * noise, -6.0, 6.0)
    return mixed.reshape(IMAGES, SEQ, D).astype(jnp.bfloat16)


def draw_small_params(key, part):
    key = jax.random.fold_in(key, 13)
    gain_key, shift_key, bias_key = jax.random.split(key, 3)
    gains = 1.0 + 0.3 * jax.random.uniform(gain_key, (2, D), jnp.float32, -1.0, 1.0)
    shifts = 0.1 * jax.random.normal(shift_key, (2, D), jnp.float32)
    biases = 0.1 * jax.random.normal(bias_key, (FF + D,), jnp.float32)
    return jnp.concatenate([gains[0], shifts[0], gains[1], shifts[1], biases])


def levels(own_key, dims, cuts, smallest, high):
    def one(position, parts):
        draws = jax.random.uniform(jax.random.fold_in(jax.random.fold_in(own_key, 6), position), (parts,), jnp.float32, smallest / len(cuts), high / len(cuts))
        return jnp.repeat(jnp.exp(draws), dims[position] // parts).reshape((-1,) + (1,) * (len(dims) - position - 1))

    level = one(*cuts[0])
    for cut in cuts[1:]:
        level = level * one(*cut)
    return level


def scatter_about(stream_key, dims, width, bound, cuts=(), kind=jnp.bfloat16):
    values = width * jax.random.normal(stream_key, dims, jnp.float32)
    if cuts:
        values = values * levels(stream_key, dims, cuts, -0.22, 0.18)
    return jnp.clip(values, -bound, bound).astype(kind)


def setup_inputs(seed: int = 0) -> dict:
    key_of = jax.random.split(jax.random.key(seed), 10)
    return {
        "tokens": draw_tokens(jax.random.fold_in(key_of[9], 71), 0),
        "cotangent": scatter_about(key_of[1], (IMAGES, SEQ, D), 1.0, 6.0, ((0, 2), (1, 16))),
        "owner_list": draw_owner_list(jax.random.fold_in(key_of[9], 71), 0),
        "master": draw_master(jax.random.fold_in(key_of[9], 71), 0),
        "moment_one": scatter_about(key_of[4], (SLOTS, D, D), (0.044 * TOKENS ** 0.5), 112.0, ((0, 16), (1, 2)), jnp.float32),
        "moment_two": jnp.clip(jnp.exp(math.log(13172.736) - 2.769608 * jax.random.uniform(key_of[5], (SLOTS, D, D), jnp.float32) ** levels(key_of[5], (SLOTS, D, D), ((0, 16), (1, 2)), -0.2, 0.2)), 825.7536, 13172.736),
        "small_params": draw_small_params(jax.random.fold_in(key_of[9], 71), 0),
        "small_one": scatter_about(key_of[7], (SMALL,), (0.055 * TOKENS ** 0.5), 128.0, (), jnp.float32),
        "small_two": jnp.clip(jnp.exp(jax.random.uniform(key_of[8], (SMALL,), jnp.float32, math.log(1297.6128), math.log(20643.84))), 1297.6128, 20643.84),
    }


RATE = 0.03
GAIN_RATE = 0.4

@jax.custom_vjp
def low(v):
    return lax.optimization_barrier(v.astype(jnp.bfloat16)).astype(jnp.float32)

@jax.custom_vjp
def low_back(v):
    return v

def low_keep(v):
    return (low(v), None)

def low_pass(kept, grad):
    return (grad,)

def back_keep(v):
    return (v, None)

def back_low(kept, grad):
    return (low(grad),)
low.defvjp(low_keep, low_pass)
low_back.defvjp(back_keep, back_low)

def layer_norm(values, gain, shift):
    centre = lax.optimization_barrier(jnp.mean(values, -1, keepdims=True))
    centred = values - centre
    spread = lax.optimization_barrier(jnp.mean(centred * centred, -1, keepdims=True))
    return centred * lax.rsqrt(spread + 1e-05) * gain + shift

def matmul(left, right):
    return jnp.dot(left, right, precision=lax.Precision.HIGHEST)

def attend_image(pieces):
    queries, key_rows, value_rows = pieces
    query_five = queries.reshape(ROWS_IMG, ROW, HEADS, HD)
    key_five = key_rows.reshape(ROWS_IMG, ROW, HEADS, HD)
    value_five = value_rows.reshape(ROWS_IMG, ROW, HEADS, HD)
    sum_keys = low(lax.optimization_barrier(jnp.mean(key_rows.reshape(ROWS_IMG, ROW, D), axis=1))).reshape(ROWS_IMG, HEADS, HD)
    sum_values = low(lax.optimization_barrier(jnp.mean(value_rows.reshape(ROWS_IMG, ROW, D), axis=1))).reshape(ROWS_IMG, HEADS, HD)
    score_scale = 1.0 / math.sqrt(HD)
    local_scores = low_back(jnp.einsum('rqhd,rkhd->rhqk', query_five, key_five, precision=lax.Precision.HIGHEST) * score_scale)
    columns = jnp.arange(ROW, dtype=jnp.int32)
    local_scores = jnp.where(columns[None, :] <= columns[:, None], local_scores, -1e+30)
    summ_scores = low_back(jnp.einsum('rqhd,shd->rhqs', query_five, sum_keys, precision=lax.Precision.HIGHEST) * score_scale) + math.log(ROW)
    row_ids = jnp.arange(ROWS_IMG, dtype=jnp.int32)
    earlier = row_ids[None, :] < row_ids[:, None]
    summ_scores = jnp.where(earlier[:, None, None, :], summ_scores, -1e+30)
    log_total = jnp.logaddexp(jax.nn.logsumexp(local_scores, -1), jax.nn.logsumexp(summ_scores, -1))
    local_probs = low(jnp.exp(local_scores - log_total[..., None]))
    summ_probs = low(jnp.exp(summ_scores - log_total[..., None]))
    mixed = jnp.einsum('rhqk,rkhd->rqhd', local_probs, value_five, precision=lax.Precision.HIGHEST)
    mixed = mixed + jnp.einsum('rhqs,shd->rqhd', summ_probs, sum_values, precision=lax.Precision.HIGHEST)
    return mixed.reshape(SEQ, D)

def forward(inputs, master, small_params, owner_list):
    blocks = low(jnp.take(master, owner_list, axis=0))
    w_up = jnp.concatenate([blocks[4 + number] for number in range(NF)], axis=1)
    w_down = blocks[4 + NF:].reshape(FF, D)
    gain_one = small_params[0:D]
    shift_one = small_params[D:2 * D]
    gain_two = small_params[2 * D:3 * D]
    shift_two = small_params[3 * D:4 * D]
    bias_up = small_params[4 * D:4 * D + FF]
    bias_down = small_params[4 * D + FF:]
    rows_flat = inputs.reshape(-1, D)
    normed_one = low(layer_norm(rows_flat, gain_one, shift_one))
    queries = low(low_back(matmul(normed_one, blocks[0])))
    key_rows = low(low_back(matmul(normed_one, blocks[1])))
    value_rows = low(low_back(matmul(normed_one, blocks[2])))
    attended = lax.map(jax.checkpoint(attend_image), (queries.reshape(IMAGES, SEQ, D), key_rows.reshape(IMAGES, SEQ, D), value_rows.reshape(IMAGES, SEQ, D)))
    attended = low(low_back(attended.reshape(-1, D)))
    hidden_one = rows_flat + low_back(matmul(attended, blocks[3]))
    normed_two = low(layer_norm(hidden_one, gain_two, shift_two))
    pre_act = low_back(matmul(normed_two, w_up) + bias_up)
    activated = low(jax.nn.gelu(pre_act))
    result = hidden_one + matmul(activated, w_down) + bias_down
    return result.reshape(inputs.shape)

def adamw_update(weight_now, gradient, first_moment, second_moment, decay_rate, step_rate):
    first_new = 0.9 * first_moment + 0.1 * gradient
    second_new = 0.95 * second_moment + 0.05 * gradient * gradient
    direction = first_new / (1.0 - 0.9 ** STEP) / (jnp.sqrt(second_new / (1.0 - 0.95 ** STEP)) + 1e-08)
    return (weight_now - step_rate * (direction + decay_rate * weight_now), first_new, second_new)

def reference(tokens, cotangent, owner_list, master, moment_one, moment_two, small_params, small_one, small_two):
    inputs = tokens.astype(jnp.float32)
    result, backward = jax.vjp(lambda first, second, third: forward(first, second, third, owner_list), inputs, master, small_params)
    grad_tokens, grad_slots, grad_small = backward(cotangent.astype(jnp.float32))
    owns_slot = jnp.any(owner_list[None, :] == jnp.arange(SLOTS, dtype=jnp.int32)[:, None], axis=1)[:, None, None]
    slot_weight, slot_first, slot_second = adamw_update(master, grad_slots, moment_one, moment_two, 0.1, RATE)
    new_master = jnp.where(owns_slot, slot_weight, master)
    new_one = jnp.where(owns_slot, slot_first, moment_one)
    new_two = jnp.where(owns_slot, slot_second, moment_two)
    small_new, small_one_new, small_two_new = adamw_update(small_params, grad_small, small_one, small_two, 0.0, GAIN_RATE)
    return (result.astype(jnp.bfloat16), grad_tokens, new_master, new_one, new_two, small_new, small_one_new, small_two_new)
```

```python
import functools
import math

import jax
import jax.numpy as jnp
from jax import lax
from jax.experimental import pallas as pl
from jax.experimental.pallas import tpu as pltpu
from jax.sharding import PartitionSpec as P

D = 512
HEADS = 8
HD = 64
PAIR = 2 * HD
PAIRS = HEADS // 2
FF = 2048
NF = FF // D
ROW = 192
ROWS_IMG = 64
KEYS = ROW + ROWS_IMG
STEP = 10
RATE = 0.03
GAIN_RATE = 0.4
EPS = 1e-05
LOG2E = math.log2(math.e)
F32 = jnp.float32
BF16 = jnp.bfloat16
MIB = 1024 * 1024


def dot(left, right):
    return jnp.dot(left, right, preferred_element_type=F32)


def dot_nt(left, right):
    return lax.dot_general(left, right, (((1,), (1,)), ((), ())), preferred_element_type=F32)


def normalize(values):
    centred = values - jnp.mean(values, -1, keepdims=True)
    scale = lax.rsqrt(jnp.mean(centred * centred, -1, keepdims=True) + EPS)
    return centred * scale, scale


def head_masks(dtype):
    lane = lax.broadcasted_iota(jnp.int32, (1, PAIR), 1)
    first = (lane < HD).astype(F32)
    return first.astype(dtype), (1.0 - first).astype(dtype)


def tile_spec(*tail, buffers=None):
    zeros = (0,) * len(tail)
    return pl.BlockSpec((1,) + tail, lambda step, *_: (step,) + zeros)


def whole_spec(shape):
    zeros = (0,) * len(shape)
    return pl.BlockSpec(shape, lambda step, *_: zeros, pipeline_mode=pl.Buffered(1))


def weight_spec(block):
    return pl.BlockSpec(
        (1, D, D), lambda step, owner, *_: (owner[block], 0, 0), pipeline_mode=pl.Buffered(1)
    )


def out_whole(shape):
    zeros = (0,) * len(shape)
    return pl.BlockSpec(shape, lambda step, *_: zeros)


def norm_kernel(x_ref, cot_ref, g_ref, s_ref, a_ref, xh_ref, mean_ref, csum_ref):
    normal, _ = normalize(x_ref[0].astype(F32))
    a_ref[0] = (normal * g_ref[...] + s_ref[...]).astype(BF16)
    xh_ref[0] = normal.astype(BF16)
    for row in range(mean_ref.shape[1]):
        part = normal[row * ROW : (row + 1) * ROW]
        mean_ref[0, row : row + 1, :] = jnp.mean(part, 0, keepdims=True)
    total = jnp.sum(cot_ref[0].astype(F32), 0, keepdims=True)

    @pl.when(pl.program_id(0) == 0)
    def _():
        csum_ref[...] = total

    @pl.when(pl.program_id(0) > 0)
    def _():
        csum_ref[...] += total


def norm_call(tokens, cotangent, gain, shift):
    images, count, _ = tokens.shape
    rows = count // ROW
    return pl.pallas_call(
        norm_kernel,
        grid=(images,),
        in_specs=[tile_spec(count, D), tile_spec(count, D), whole_spec((1, D)), whole_spec((1, D))],
        out_specs=[tile_spec(count, D), tile_spec(count, D), tile_spec(rows, D), out_whole((1, D))],
        out_shape=[
            jax.ShapeDtypeStruct((images, count, D), BF16),
            jax.ShapeDtypeStruct((images, count, D), BF16),
            jax.ShapeDtypeStruct((images, rows, D), F32),
            jax.ShapeDtypeStruct((1, D), F32),
        ],
        compiler_params=pltpu.CompilerParams(vmem_limit_bytes=40 * MIB),
        cost_estimate=pl.CostEstimate(
            flops=images * count * D * 20, bytes_accessed=images * count * D * 8, transcendentals=0
        ),
        name="norm_one",
    )(tokens, cotangent, gain, shift)


def attend_kernel(
    owner, first_row, a_ref, mean_ref, g_ref, s_ref, wq_ref, wk_ref, wv_ref,
    q_ref, k_ref, v_ref, e_ref, o_ref, li_ref, bias_ref, sk_ref, sv_ref,
):
    rows = a_ref.shape[1] // ROW

    @pl.when(pl.program_id(0) == 0)
    def _():
        query = lax.broadcasted_iota(jnp.int32, (ROW, KEYS), 0)
        key = lax.broadcasted_iota(jnp.int32, (ROW, KEYS), 1)
        for row in range(rows):
            own = jnp.where(key <= query, 0.0, -1e30)
            earlier = jnp.where(key - ROW < first_row[0] + row, math.log2(ROW), -1e30)
            bias_ref[row] = jnp.where(key < ROW, own, earlier)

    a1 = a_ref[0]
    q_ref[0] = dot(a1, wq_ref[0]).astype(BF16)
    k_ref[0] = dot(a1, wk_ref[0]).astype(BF16)
    v_ref[0] = dot(a1, wv_ref[0]).astype(BF16)
    mean_a = (mean_ref[0].astype(F32) * g_ref[...] + s_ref[...]).astype(BF16)
    sk_ref[...] = dot(mean_a, wk_ref[0]).astype(BF16)
    sv_ref[...] = dot(mean_a, wv_ref[0]).astype(BF16)
    masks = head_masks(BF16)
    ones = [jnp.broadcast_to(mask, (KEYS, PAIR)) for mask in masks]
    scale = LOG2E / math.sqrt(HD)

    def one_row(row, carry):
        here = pl.ds(pl.multiple_of(row * ROW, ROW), ROW)
        for pair in range(PAIRS):
            lanes = slice(pair * PAIR, (pair + 1) * PAIR)
            query = q_ref[0, here, lanes]
            keys = jnp.concatenate([k_ref[0, here, lanes], sk_ref[:, lanes]], 0)
            values = jnp.concatenate([v_ref[0, here, lanes], sv_ref[:, lanes]], 0)
            total = None
            for half in range(2):
                score = dot_nt(query, keys * masks[half]) * scale + bias_ref[row]
                weight = jnp.exp2(score - jnp.max(score, -1, keepdims=True)).astype(BF16)
                e_ref[0, row, 2 * pair + half] = weight
                part = dot(weight, jnp.concatenate([values * masks[half], ones[half]], 1))
                total = part if total is None else total + part
            inverse = 1.0 / total[:, PAIR:]
            o_ref[0, here, lanes] = (total[:, :PAIR] * inverse).astype(BF16)
            li_ref[0, here, lanes] = inverse.astype(BF16)
        return carry

    lax.fori_loop(0, rows, one_row, 0)


def attend_call(owner, first_row, a1, mean_all, gain, shift, slots):
    images, count, _ = a1.shape
    rows = count // ROW
    tokens_shape = jax.ShapeDtypeStruct((images, count, D), BF16)
    return pl.pallas_call(
        attend_kernel,
        grid_spec=pltpu.PrefetchScalarGridSpec(
            num_scalar_prefetch=2,
            grid=(images,),
            in_specs=[
                tile_spec(count, D), tile_spec(ROWS_IMG, D), whole_spec((1, D)), whole_spec((1, D)),
                weight_spec(0), weight_spec(1), weight_spec(2),
            ],
            out_specs=[tile_spec(count, D)] * 3
            + [tile_spec(rows, HEADS, ROW, KEYS)]
            + [tile_spec(count, D)] * 2,
            scratch_shapes=[
                pltpu.VMEM((rows, ROW, KEYS), F32),
                pltpu.VMEM((ROWS_IMG, D), BF16),
                pltpu.VMEM((ROWS_IMG, D), BF16),
            ],
        ),
        out_shape=[tokens_shape] * 3
        + [jax.ShapeDtypeStruct((images, rows, HEADS, ROW, KEYS), BF16)]
        + [tokens_shape] * 2,
        compiler_params=pltpu.CompilerParams(vmem_limit_bytes=56 * MIB),
        cost_estimate=pl.CostEstimate(
            flops=images * count * D * D * 10, bytes_accessed=images * count * D * 20, transcendentals=0
        ),
        name="attend",
    )(owner, first_row, a1, mean_all, gain, shift, slots, slots, slots)


def ff_kernel(
    owner, x_ref, o_ref, cot_ref, li_ref, g_ref, s_ref, bu_ref, bd_ref,
    wo_ref, u0_ref, u1_ref, u2_ref, u3_ref, d0_ref, d1_ref, d2_ref, d3_ref,
    out_ref, dr_ref, do_ref, grads_ref, gg_ref, gs_ref, gbu_ref,
    acc_ref, h_ref, xh_ref, da_ref,
):
    step = pl.program_id(0)
    ups = (u0_ref, u1_ref, u2_ref, u3_ref)
    downs = (d0_ref, d1_ref, d2_ref, d3_ref)

    @pl.when(step == 0)
    def _():
        acc_ref[...] = jnp.zeros_like(acc_ref)
        gg_ref[...] = jnp.zeros_like(gg_ref)
        gs_ref[...] = jnp.zeros_like(gs_ref)
        gbu_ref[...] = jnp.zeros_like(gbu_ref)

    hidden = x_ref[0].astype(F32) + dot(o_ref[0], wo_ref[0])
    normal, spread = normalize(hidden)
    xh_ref[...] = normal
    h_ref[...] = hidden + bd_ref[...]
    a2 = (normal * g_ref[...] + s_ref[...]).astype(BF16)
    a2_t = a2.T
    cot = cot_ref[0]
    cot_t = cot.T
    c_one = math.sqrt(2.0 / math.pi)
    c_two = c_one * 0.044715
    for block in range(NF):
        w_up = ups[block][0]
        w_down = downs[block][0]
        pre = dot(a2, w_up) + bu_ref[:, block * D : (block + 1) * D]
        d_act = dot_nt(cot, w_down)
        square = pre * pre
        half = 0.5 + 0.5 * jnp.tanh(pre * (c_one + c_two * square))
        act = pre * half
        slope = half + act * (1.0 - half) * (2.0 * c_one + (6.0 * c_two) * square)
        act = act.astype(BF16)
        d_pre = d_act * slope
        gbu_ref[:, block * D : (block + 1) * D] += jnp.sum(d_pre, 0, keepdims=True)
        d_pre = d_pre.astype(BF16)
        h_ref[...] += dot(act, w_down)
        part = dot_nt(d_pre, w_up)
        if block == 0:
            da_ref[...] = part
        else:
            da_ref[...] += part
        acc_ref[1 + block] += dot(a2_t, d_pre)
        acc_ref[1 + NF + block] += dot(cot_t, act)
    out_ref[0] = h_ref[...].astype(BF16)
    d_a2 = da_ref[...]
    normal = xh_ref[...]
    gs_ref[...] += jnp.sum(d_a2, 0, keepdims=True)
    gg_ref[...] += jnp.sum(d_a2 * normal, 0, keepdims=True)
    d_normal = d_a2 * g_ref[...]
    middle = jnp.mean(d_normal, -1, keepdims=True)
    along = jnp.mean(d_normal * normal, -1, keepdims=True)
    d_hidden = cot.astype(F32) + spread * (d_normal - middle - normal * along)
    branch = d_hidden.astype(BF16)
    dr_ref[0] = branch
    acc_ref[0] += dot(o_ref[0].T, branch)
    do_ref[0] = (dot_nt(branch, wo_ref[0]) * li_ref[0].astype(F32)).astype(BF16)

    @pl.when(step == pl.num_programs(0) - 1)
    def _():
        for block in range(1 + NF):
            grads_ref[block] = acc_ref[block].astype(BF16)
        for block in range(1 + NF, 1 + 2 * NF):
            grads_ref[block] = acc_ref[block].T.astype(BF16)


def ff_call(owner, tokens, attended, cotangent, inverse, gain, shift, bias_up, bias_down, slots):
    images, count, _ = tokens.shape
    tokens_shape = jax.ShapeDtypeStruct((images, count, D), BF16)
    blocks = 1 + 2 * NF
    return pl.pallas_call(
        ff_kernel,
        grid_spec=pltpu.PrefetchScalarGridSpec(
            num_scalar_prefetch=1,
            grid=(images,),
            in_specs=[tile_spec(count, D)] * 4
            + [whole_spec((1, D)), whole_spec((1, D)), whole_spec((1, FF)), whole_spec((1, D))]
            + [weight_spec(3 + block) for block in range(blocks)],
            out_specs=[tile_spec(count, D)] * 3
            + [out_whole((blocks, D, D)), out_whole((1, D)), out_whole((1, D)), out_whole((1, FF))],
            scratch_shapes=[
                pltpu.VMEM((blocks, D, D), F32),
                pltpu.VMEM((count, D), F32),
                pltpu.VMEM((count, D), F32),
                pltpu.VMEM((count, D), F32),
            ],
        ),
        out_shape=[tokens_shape] * 3
        + [
            jax.ShapeDtypeStruct((blocks, D, D), BF16),
            jax.ShapeDtypeStruct((1, D), F32),
            jax.ShapeDtypeStruct((1, D), F32),
            jax.ShapeDtypeStruct((1, FF), F32),
        ],
        compiler_params=pltpu.CompilerParams(vmem_limit_bytes=60 * MIB),
        cost_estimate=pl.CostEstimate(
            flops=images * count * D * D * 54, bytes_accessed=images * count * D * 14, transcendentals=0
        ),
        name="feed_forward",
    )(owner, tokens, attended, cotangent, inverse, gain, shift, bias_up, bias_down, *([slots] * blocks))


def back_kernel(
    owner, q_ref, k_ref, v_ref, o_ref, do_ref, e_ref, xh_ref, mean_ref, g_ref, s_ref,
    wq_ref, wk_ref, wv_ref,
    dlow_ref, dm_ref, grads_ref, gg_ref, gs_ref,
    acc_ref, dt_ref, sk_ref, sv_ref, dsk_ref, dsv_ref, skt_ref,
):
    step = pl.program_id(0)
    rows = q_ref.shape[1] // ROW
    scale = 1.0 / math.sqrt(HD)

    @pl.when(step == 0)
    def _():
        acc_ref[...] = jnp.zeros_like(acc_ref)
        gg_ref[...] = jnp.zeros_like(gg_ref)
        gs_ref[...] = jnp.zeros_like(gs_ref)

    mean_x = mean_ref[0].astype(F32)
    mean_a = (mean_x * g_ref[...] + s_ref[...]).astype(BF16)
    sum_k = dot(mean_a, wk_ref[0]).astype(BF16)
    sk_ref[...] = sum_k
    skt_ref[...] = (sum_k * scale).T
    sv_ref[...] = dot(mean_a, wv_ref[0]).astype(BF16)
    dsk_ref[...] = jnp.zeros_like(dsk_ref)
    dsv_ref[...] = jnp.zeros_like(dsv_ref)
    masks = head_masks(BF16)
    minus = [jnp.broadcast_to(-mask, (KEYS, PAIR)) for mask in masks]

    def one_row(row, carry):
        here = pl.ds(pl.multiple_of(row * ROW, ROW), ROW)
        d_out = do_ref[0, here, :]
        d_out_o = d_out * o_ref[0, here, :]
        q_t = (q_ref[0, here, :] * scale).T
        d_out_t = d_out.T
        k_t = jnp.concatenate([(k_ref[0, here, :] * scale).T, skt_ref[...]], 1)
        for pair in range(PAIRS):
            lanes = slice(pair * PAIR, (pair + 1) * PAIR)
            values = jnp.concatenate([v_ref[0, here, lanes], sv_ref[:, lanes]], 0)
            left = jnp.concatenate([d_out[:, lanes], d_out_o[:, lanes]], 1)
            for half in range(2):
                head = 2 * pair + half
                mine = slice(head * HD, (head + 1) * HD)
                right = jnp.concatenate([values * masks[half], minus[half]], 1)
                weight = e_ref[0, row, head]
                d_score = weight * dot_nt(left, right).astype(BF16)
                d_v = dot(d_out_t[mine], weight)
                d_k = dot(q_t[mine], d_score)
                d_q = dot_nt(k_t[mine], d_score)
                dt_ref[mine, :] = d_q.astype(BF16)
                dt_ref[D + head * HD : D + (head + 1) * HD, :] = d_k[:, :ROW].astype(BF16)
                dt_ref[2 * D + head * HD : 2 * D + (head + 1) * HD, :] = d_v[:, :ROW].astype(BF16)
                dsk_ref[mine, :] += d_k[:, PAIR:]
                dsv_ref[mine, :] += d_v[:, PAIR:]
        normal = xh_ref[0, here, :].astype(F32)
        a1 = (normal * g_ref[...] + s_ref[...]).astype(BF16)
        acc_ref[...] += dot(dt_ref[...], a1)
        low = (
            dot(wq_ref[0], dt_ref[0:D, :])
            + dot(wk_ref[0], dt_ref[D : 2 * D, :])
            + dot(wv_ref[0], dt_ref[2 * D : 3 * D, :])
        ).T
        dlow_ref[0, here, :] = low.astype(BF16)
        gs_ref[...] += jnp.sum(low, 0, keepdims=True)
        gg_ref[...] += jnp.sum(low * normal, 0, keepdims=True)
        return carry

    lax.fori_loop(0, rows, one_row, 0)
    d_sum_k = dsk_ref[:, ROW - PAIR :].astype(BF16)
    d_sum_v = dsv_ref[:, ROW - PAIR :].astype(BF16)
    acc_ref[D : 2 * D, :] += dot(d_sum_k, mean_a)
    acc_ref[2 * D : 3 * D, :] += dot(d_sum_v, mean_a)
    d_mean = (dot(wk_ref[0], d_sum_k) + dot(wv_ref[0], d_sum_v)).T
    dm_ref[0] = d_mean.astype(BF16)
    gs_ref[...] += jnp.sum(d_mean, 0, keepdims=True)
    gg_ref[...] += jnp.sum(d_mean * mean_x, 0, keepdims=True)

    @pl.when(step == pl.num_programs(0) - 1)
    def _():
        for block in range(3):
            grads_ref[block] = acc_ref[block * D : (block + 1) * D, :].T.astype(BF16)


def back_call(owner, queries, keys, values, attended, d_out, weights, normal, mean_all, gain, shift, slots):
    images, count, _ = queries.shape
    rows = count // ROW
    return pl.pallas_call(
        back_kernel,
        grid_spec=pltpu.PrefetchScalarGridSpec(
            num_scalar_prefetch=1,
            grid=(images,),
            in_specs=[tile_spec(count, D)] * 5
            + [tile_spec(rows, HEADS, ROW, KEYS), tile_spec(count, D), tile_spec(ROWS_IMG, D)]
            + [whole_spec((1, D)), whole_spec((1, D))]
            + [weight_spec(block) for block in range(3)],
            out_specs=[
                tile_spec(count, D), tile_spec(ROWS_IMG, D), out_whole((3, D, D)),
                out_whole((1, D)), out_whole((1, D)),
            ],
            scratch_shapes=[
                pltpu.VMEM((3 * D, D), F32),
                pltpu.VMEM((3 * D, ROW), BF16),
                pltpu.VMEM((ROWS_IMG, D), BF16),
                pltpu.VMEM((ROWS_IMG, D), BF16),
                pltpu.VMEM((D, PAIR), F32),
                pltpu.VMEM((D, PAIR), F32),
                pltpu.VMEM((D, ROWS_IMG), BF16),
            ],
        ),
        out_shape=[
            jax.ShapeDtypeStruct((images, count, D), BF16),
            jax.ShapeDtypeStruct((images, ROWS_IMG, D), BF16),
            jax.ShapeDtypeStruct((3, D, D), BF16),
            jax.ShapeDtypeStruct((1, D), F32),
            jax.ShapeDtypeStruct((1, D), F32),
        ],
        compiler_params=pltpu.CompilerParams(vmem_limit_bytes=56 * MIB),
        cost_estimate=pl.CostEstimate(
            flops=images * count * D * D * 20, bytes_accessed=images * count * D * 24, transcendentals=0
        ),
        name="attend_back",
    )(owner, queries, keys, values, attended, d_out, weights, normal, mean_all, gain, shift, slots, slots, slots)


def last_kernel(x_ref, low_ref, dr_ref, dm_ref, g_ref, out_ref):
    for row in range(dm_ref.shape[1]):
        here = slice(row * ROW, (row + 1) * ROW)
        normal, spread = normalize(x_ref[0, here, :].astype(F32))
        total = low_ref[0, here, :].astype(F32) + dm_ref[0, row : row + 1, :] * (1.0 / ROW)
        d_normal = total * g_ref[...]
        middle = jnp.mean(d_normal, -1, keepdims=True)
        along = jnp.mean(d_normal * normal, -1, keepdims=True)
        out_ref[0, here, :] = dr_ref[0, here, :].astype(F32) + spread * (d_normal - middle - normal * along)


def last_call(tokens, d_low, d_branch, d_mean, gain):
    images, count, _ = tokens.shape
    return pl.pallas_call(
        last_kernel,
        grid=(images,),
        in_specs=[tile_spec(count, D)] * 3 + [tile_spec(count // ROW, D), whole_spec((1, D))],
        out_specs=tile_spec(count, D),
        out_shape=jax.ShapeDtypeStruct((images, count, D), F32),
        compiler_params=pltpu.CompilerParams(vmem_limit_bytes=40 * MIB),
        cost_estimate=pl.CostEstimate(
            flops=images * count * D * 20, bytes_accessed=images * count * D * 10, transcendentals=0
        ),
        name="norm_one_back",
    )(tokens, d_low, d_branch, d_mean, gain)


def adamw_update(weight_now, gradient, first_moment, second_moment, decay_rate, step_rate):
    first_new = 0.9 * first_moment + 0.1 * gradient
    second_new = 0.95 * second_moment + 0.05 * gradient * gradient
    direction = first_new / (1.0 - 0.9**STEP) / (jnp.sqrt(second_new / (1.0 - 0.95**STEP)) + 1e-08)
    return (weight_now - step_rate * (direction + decay_rate * weight_now), first_new, second_new)


def sum_everywhere(value):
    for axis in ("narrow", "wide"):
        size = lax.axis_size(axis)
        bit = 1
        while bit < size:
            value = value + lax.ppermute(value, axis, [(index, index ^ bit) for index in range(size)])
            bit *= 2
    return value


def share_sums(grads):
    blocks = grads.shape[0]
    narrow = lax.axis_size("narrow")
    wide = lax.axis_size("wide")
    parts = lax.all_to_all(grads.reshape(blocks, narrow, D // narrow, D), "narrow", 1, 1, tiled=True)
    rows = jnp.sum(parts.astype(F32), 1).astype(BF16)
    pieces = rows.reshape(blocks, wide, -1, D).swapaxes(0, 1)
    parts = lax.all_to_all(pieces, "wide", 0, 0, tiled=True)
    return jnp.sum(parts.astype(F32), 0).astype(BF16)


def to_slots(shares, owner_list):
    wide = lax.axis_size("wide")
    slotted = jnp.zeros((wide,) + shares.shape[1:], BF16).at[owner_list].set(shares)
    parts = lax.all_to_all(slotted, "wide", 0, 0, tiled=True)
    return parts.reshape(1, -1, D).astype(F32)


def per_device(
    tokens, cotangent, owner_list, master, moment_one, moment_two, small_params, small_one, small_two
):
    images, count, _ = tokens.shape
    rows = count // ROW
    wide = lax.axis_size("wide")
    small = small_params.reshape(1, -1)
    gain_one = small[:, 0:D]
    shift_one = small[:, D : 2 * D]
    gain_two = small[:, 2 * D : 3 * D]
    shift_two = small[:, 3 * D : 4 * D]
    bias_up = small[:, 4 * D : 4 * D + FF]
    bias_down = small[:, 4 * D + FF :]
    low_master = master.astype(BF16)
    slots = lax.all_gather(low_master.reshape(-1, D), ("wide", "narrow"), axis=0, tiled=True)
    slots = slots.reshape(-1, D, D)
    a1, normal, means, bias_down_grad = norm_call(tokens, cotangent, gain_one, shift_one)
    gathered = lax.all_gather(means.astype(BF16).reshape(-1, D), "wide", axis=0, tiled=True)
    mean_all = gathered.reshape(wide, images, rows, D).swapaxes(0, 1).reshape(images, ROWS_IMG, D)
    first_row = (lax.axis_index("wide") * rows).astype(jnp.int32).reshape(1)
    queries, keys, values, weights, attended, inverse = attend_call(
        owner_list, first_row, a1, mean_all, gain_one, shift_one, slots
    )
    block_out, d_branch, d_out, grads_late, gain_two_grad, shift_two_grad, bias_up_grad = ff_call(
        owner_list, tokens, attended, cotangent, inverse, gain_two, shift_two, bias_up, bias_down, slots
    )
    d_low, d_mean, grads_early, gain_one_grad, shift_one_grad = back_call(
        owner_list, queries, keys, values, attended, d_out, weights, normal, mean_all, gain_one, shift_one, slots
    )
    pieces = d_mean.reshape(images, wide, rows, D).swapaxes(0, 1)
    own_mean = jnp.sum(lax.all_to_all(pieces, "wide", 0, 0, tiled=True).astype(F32), 0)
    grad_tokens = last_call(tokens, d_low, d_branch, own_mean, gain_one)
    own_grad = to_slots(share_sums(grads_late), owner_list[3:]) + to_slots(
        share_sums(grads_early), owner_list[:3]
    )
    small_grad = sum_everywhere(
        jnp.concatenate(
            [gain_one_grad, shift_one_grad, gain_two_grad, shift_two_grad, bias_up_grad, bias_down_grad], 1
        )
    ).reshape(-1)
    owns_slot = jnp.any(owner_list == lax.axis_index("wide"))
    slot_weight, slot_first, slot_second = adamw_update(
        master, own_grad, moment_one, moment_two, 0.1, RATE
    )
    new_master = jnp.where(owns_slot, slot_weight, master)
    new_one = jnp.where(owns_slot, slot_first, moment_one)
    new_two = jnp.where(owns_slot, slot_second, moment_two)
    small_new, small_one_new, small_two_new = adamw_update(
        small_params, small_grad, small_one, small_two, 0.0, GAIN_RATE
    )
    return (block_out, grad_tokens, new_master, new_one, new_two, small_new, small_one_new, small_two_new)


def solution(mesh):
    split = P("narrow", "wide", None)
    slot = P("wide", "narrow", None)
    return jax.shard_map(
        per_device,
        mesh=mesh,
        in_specs=(split, split, P(), slot, slot, slot, P(), P(), P()),
        out_specs=(split, split, slot, slot, slot, P(), P(), P()),
        check_vma=False,
    )
```

```python
import functools
import functools
import math

import jax
import jax.numpy as jnp
from jax import lax
from jax.experimental import pallas as pl
from jax.experimental.pallas import tpu as pltpu
from jax.sharding import PartitionSpec as P

D = 512
HEADS = 8
HD = 64
PAIR = 2 * HD
PAIRS = HEADS // 2
FF = 2048
NF = FF // D
ROW = 192
ROWS_IMG = 64
KEYS = ROW + ROWS_IMG
STEP = 10
RATE = 0.03
GAIN_RATE = 0.4
EPS = 1e-05
LOG2E = math.log2(math.e)
F32 = jnp.float32
BF16 = jnp.bfloat16
MIB = 1024 * 1024


def dot(left, right):
    return jnp.dot(left, right, preferred_element_type=F32)


def dot_nt(left, right):
    return lax.dot_general(left, right, (((1,), (1,)), ((), ())), preferred_element_type=F32)


def normalize(values):
    centred = values - jnp.mean(values, -1, keepdims=True)
    scale = lax.rsqrt(jnp.mean(centred * centred, -1, keepdims=True) + EPS)
    return centred * scale, scale


def head_masks(dtype):
    lane = lax.broadcasted_iota(jnp.int32, (1, PAIR), 1)
    first = (lane < HD).astype(F32)
    return first.astype(dtype), (1.0 - first).astype(dtype)


def tile_spec(*tail, buffers=None):
    zeros = (0,) * len(tail)
    return pl.BlockSpec((1,) + tail, lambda step, *_: (step,) + zeros)


def whole_spec(shape):
    zeros = (0,) * len(shape)
    return pl.BlockSpec(shape, lambda step, *_: zeros, pipeline_mode=pl.Buffered(1))


def weight_spec(block):
    return pl.BlockSpec(
        (1, D, D), lambda step, owner, *_: (owner[block], 0, 0), pipeline_mode=pl.Buffered(1)
    )


def plain_weight_spec(block):
    return pl.BlockSpec((1, D, D), lambda step, *_: (block, 0, 0), pipeline_mode=pl.Buffered(1))


def out_whole(shape):
    zeros = (0,) * len(shape)
    return pl.BlockSpec(shape, lambda step, *_: zeros)


def norm_kernel(x_ref, cot_ref, g_ref, s_ref, a_ref, xh_ref, mean_ref, csum_ref):
    normal, _ = normalize(x_ref[0].astype(F32))
    a_ref[0] = (normal * g_ref[...] + s_ref[...]).astype(BF16)
    xh_ref[0] = normal.astype(BF16)
    for row in range(mean_ref.shape[1]):
        part = normal[row * ROW : (row + 1) * ROW]
        mean_ref[0, row : row + 1, :] = jnp.mean(part, 0, keepdims=True)
    total = jnp.sum(cot_ref[0].astype(F32), 0, keepdims=True)

    @pl.when(pl.program_id(0) == 0)
    def _():
        csum_ref[...] = total

    @pl.when(pl.program_id(0) > 0)
    def _():
        csum_ref[...] += total


def norm_call(tokens, cotangent, gain, shift):
    images, count, _ = tokens.shape
    rows = count // ROW
    return pl.pallas_call(
        norm_kernel,
        grid=(images,),
        in_specs=[tile_spec(count, D), tile_spec(count, D), whole_spec((1, D)), whole_spec((1, D))],
        out_specs=[tile_spec(count, D), tile_spec(count, D), tile_spec(rows, D), out_whole((1, D))],
        out_shape=[
            jax.ShapeDtypeStruct((images, count, D), BF16),
            jax.ShapeDtypeStruct((images, count, D), BF16),
            jax.ShapeDtypeStruct((images, rows, D), F32),
            jax.ShapeDtypeStruct((1, D), F32),
        ],
        compiler_params=pltpu.CompilerParams(vmem_limit_bytes=40 * MIB),
        cost_estimate=pl.CostEstimate(
            flops=images * count * D * 20, bytes_accessed=images * count * D * 8, transcendentals=0
        ),
        name="norm_one",
    )(tokens, cotangent, gain, shift)


def attend_kernel(
    first_row, a_ref, mean_ref, g_ref, s_ref, wq_ref, wk_ref, wv_ref,
    q_ref, k_ref, v_ref, e_ref, o_ref, li_ref, bias_ref, sk_ref, sv_ref,
):
    rows = a_ref.shape[1] // ROW

    @pl.when(pl.program_id(0) == 0)
    def _():
        query = lax.broadcasted_iota(jnp.int32, (ROW, KEYS), 0)
        key = lax.broadcasted_iota(jnp.int32, (ROW, KEYS), 1)
        for row in range(rows):
            own = jnp.where(key <= query, 0.0, -1e30)
            earlier = jnp.where(key - ROW < first_row[0] + row, math.log2(ROW), -1e30)
            bias_ref[row] = jnp.where(key < ROW, own, earlier)

    a1 = a_ref[0]
    q_ref[0] = dot(a1, wq_ref[0]).astype(BF16)
    k_ref[0] = dot(a1, wk_ref[0]).astype(BF16)
    v_ref[0] = dot(a1, wv_ref[0]).astype(BF16)
    mean_a = (mean_ref[0].astype(F32) * g_ref[...] + s_ref[...]).astype(BF16)
    sk_ref[...] = dot(mean_a, wk_ref[0]).astype(BF16)
    sv_ref[...] = dot(mean_a, wv_ref[0]).astype(BF16)
    masks = head_masks(BF16)
    ones = [jnp.broadcast_to(mask, (KEYS, PAIR)) for mask in masks]
    scale = LOG2E / math.sqrt(HD)

    def one_row(row, carry):
        here = pl.ds(pl.multiple_of(row * ROW, ROW), ROW)
        for pair in range(PAIRS):
            lanes = slice(pair * PAIR, (pair + 1) * PAIR)
            query = q_ref[0, here, lanes]
            keys = jnp.concatenate([k_ref[0, here, lanes], sk_ref[:, lanes]], 0)
            values = jnp.concatenate([v_ref[0, here, lanes], sv_ref[:, lanes]], 0)
            total = None
            for half in range(2):
                score = dot_nt(query, keys * masks[half]) * scale + bias_ref[row]
                weight = jnp.exp2(score - jnp.max(score, -1, keepdims=True)).astype(BF16)
                e_ref[0, row, 2 * pair + half] = weight
                part = dot(weight, jnp.concatenate([values * masks[half], ones[half]], 1))
                total = part if total is None else total + part
            inverse = 1.0 / total[:, PAIR:]
            o_ref[0, here, lanes] = (total[:, :PAIR] * inverse).astype(BF16)
            li_ref[0, here, lanes] = inverse.astype(BF16)
        return carry

    lax.fori_loop(0, rows, one_row, 0)


def attend_call(first_row, a1, mean_all, gain, shift, blocks):
    images, count, _ = a1.shape
    rows = count // ROW
    tokens_shape = jax.ShapeDtypeStruct((images, count, D), BF16)
    return pl.pallas_call(
        attend_kernel,
        grid_spec=pltpu.PrefetchScalarGridSpec(
            num_scalar_prefetch=1,
            grid=(images,),
            in_specs=[
                tile_spec(count, D), tile_spec(ROWS_IMG, D), whole_spec((1, D)), whole_spec((1, D)),
            ]
            + [plain_weight_spec(block) for block in range(3)],
            out_specs=[tile_spec(count, D)] * 3
            + [tile_spec(rows, HEADS, ROW, KEYS)]
            + [tile_spec(count, D)] * 2,
            scratch_shapes=[
                pltpu.VMEM((rows, ROW, KEYS), F32),
                pltpu.VMEM((ROWS_IMG, D), BF16),
                pltpu.VMEM((ROWS_IMG, D), BF16),
            ],
        ),
        out_shape=[tokens_shape] * 3
        + [jax.ShapeDtypeStruct((images, rows, HEADS, ROW, KEYS), BF16)]
        + [tokens_shape] * 2,
        compiler_params=pltpu.CompilerParams(vmem_limit_bytes=56 * MIB),
        cost_estimate=pl.CostEstimate(
            flops=images * count * D * D * 10, bytes_accessed=images * count * D * 20, transcendentals=0
        ),
        name="attend",
    )(first_row, a1, mean_all, gain, shift, blocks, blocks, blocks)


def ff_kernel(
    owner, x_ref, o_ref, cot_ref, li_ref, g_ref, s_ref, bu_ref, bd_ref,
    wo_ref, u0_ref, u1_ref, u2_ref, u3_ref, d0_ref, d1_ref, d2_ref, d3_ref,
    out_ref, dr_ref, do_ref, grads_ref, gg_ref, gs_ref, gbu_ref,
    acc_ref, h_ref, xh_ref, da_ref,
):
    step = pl.program_id(0)
    ups = (u0_ref, u1_ref, u2_ref, u3_ref)
    downs = (d0_ref, d1_ref, d2_ref, d3_ref)

    @pl.when(step == 0)
    def _():
        acc_ref[...] = jnp.zeros_like(acc_ref)
        gg_ref[...] = jnp.zeros_like(gg_ref)
        gs_ref[...] = jnp.zeros_like(gs_ref)
        gbu_ref[...] = jnp.zeros_like(gbu_ref)

    hidden = x_ref[0].astype(F32) + dot(o_ref[0], wo_ref[0])
    normal, spread = normalize(hidden)
    xh_ref[...] = normal
    h_ref[...] = hidden + bd_ref[...]
    a2 = (normal * g_ref[...] + s_ref[...]).astype(BF16)
    a2_t = a2.T
    cot = cot_ref[0]
    cot_t = cot.T
    c_one = math.sqrt(2.0 / math.pi)
    c_two = c_one * 0.044715
    for block in range(NF):
        w_up = ups[block][0]
        w_down = downs[block][0]
        pre = dot(a2, w_up) + bu_ref[:, block * D : (block + 1) * D]
        d_act = dot_nt(cot, w_down)
        square = pre * pre
        half = 0.5 + 0.5 * jnp.tanh(pre * (c_one + c_two * square))
        act = pre * half
        slope = half + act * (1.0 - half) * (2.0 * c_one + (6.0 * c_two) * square)
        act = act.astype(BF16)
        d_pre = d_act * slope
        gbu_ref[:, block * D : (block + 1) * D] += jnp.sum(d_pre, 0, keepdims=True)
        d_pre = d_pre.astype(BF16)
        h_ref[...] += dot(act, w_down)
        part = dot_nt(d_pre, w_up)
        if block == 0:
            da_ref[...] = part
        else:
            da_ref[...] += part
        acc_ref[1 + block] += dot(a2_t, d_pre)
        acc_ref[1 + NF + block] += dot(cot_t, act)
    out_ref[0] = h_ref[...].astype(BF16)
    d_a2 = da_ref[...]
    normal = xh_ref[...]
    gs_ref[...] += jnp.sum(d_a2, 0, keepdims=True)
    gg_ref[...] += jnp.sum(d_a2 * normal, 0, keepdims=True)
    d_normal = d_a2 * g_ref[...]
    middle = jnp.mean(d_normal, -1, keepdims=True)
    along = jnp.mean(d_normal * normal, -1, keepdims=True)
    d_hidden = cot.astype(F32) + spread * (d_normal - middle - normal * along)
    branch = d_hidden.astype(BF16)
    dr_ref[0] = branch
    acc_ref[0] += dot(o_ref[0].T, branch)
    do_ref[0] = (dot_nt(branch, wo_ref[0]) * li_ref[0].astype(F32)).astype(BF16)

    @pl.when(step == pl.num_programs(0) - 1)
    def _():
        for block in range(1 + NF):
            grads_ref[block] = acc_ref[block].astype(BF16)
        for block in range(1 + NF, 1 + 2 * NF):
            grads_ref[block] = acc_ref[block].T.astype(BF16)


def ff_call(owner, tokens, attended, cotangent, inverse, gain, shift, bias_up, bias_down, slots):
    images, count, _ = tokens.shape
    tokens_shape = jax.ShapeDtypeStruct((images, count, D), BF16)
    blocks = 1 + 2 * NF
    return pl.pallas_call(
        ff_kernel,
        grid_spec=pltpu.PrefetchScalarGridSpec(
            num_scalar_prefetch=1,
            grid=(images,),
            in_specs=[tile_spec(count, D)] * 4
            + [whole_spec((1, D)), whole_spec((1, D)), whole_spec((1, FF)), whole_spec((1, D))]
            + [weight_spec(3 + block) for block in range(blocks)],
            out_specs=[tile_spec(count, D)] * 3
            + [out_whole((blocks, D, D)), out_whole((1, D)), out_whole((1, D)), out_whole((1, FF))],
            scratch_shapes=[
                pltpu.VMEM((blocks, D, D), F32),
                pltpu.VMEM((count, D), F32),
                pltpu.VMEM((count, D), F32),
                pltpu.VMEM((count, D), F32),
            ],
        ),
        out_shape=[tokens_shape] * 3
        + [
            jax.ShapeDtypeStruct((blocks, D, D), BF16),
            jax.ShapeDtypeStruct((1, D), F32),
            jax.ShapeDtypeStruct((1, D), F32),
            jax.ShapeDtypeStruct((1, FF), F32),
        ],
        compiler_params=pltpu.CompilerParams(vmem_limit_bytes=60 * MIB),
        cost_estimate=pl.CostEstimate(
            flops=images * count * D * D * 54, bytes_accessed=images * count * D * 14, transcendentals=0
        ),
        name="feed_forward",
    )(owner, tokens, attended, cotangent, inverse, gain, shift, bias_up, bias_down, *([slots] * blocks))


def back_kernel(first, last, owner, *refs):
    (q_ref, k_ref, v_ref, o_ref, do_ref, e_ref, xh_ref, mean_ref, g_ref, s_ref, wq_ref, wk_ref, wv_ref) = refs[:13]
    refs = refs[13:]
    if not first:
        old_acc_ref, old_gg_ref, old_gs_ref = refs[:3]
        refs = refs[4:]
    dlow_ref, dm_ref, acc_ref, gg_ref, gs_ref = refs[:5]
    refs = refs[5:]
    if last:
        grads_ref = refs[0]
        refs = refs[1:]
    dt_ref, sk_ref, sv_ref, dsk_ref, dsv_ref, skt_ref = refs
    step = pl.program_id(0)
    rows = q_ref.shape[1] // ROW
    scale = 1.0 / math.sqrt(HD)

    @pl.when(step == 0)
    def _():
        acc_ref[...] = jnp.zeros_like(acc_ref) if first else old_acc_ref[...]
        gg_ref[...] = jnp.zeros_like(gg_ref) if first else old_gg_ref[...]
        gs_ref[...] = jnp.zeros_like(gs_ref) if first else old_gs_ref[...]

    mean_x = mean_ref[0].astype(F32)
    mean_a = (mean_x * g_ref[...] + s_ref[...]).astype(BF16)
    sum_k = dot(mean_a, wk_ref[0]).astype(BF16)
    sk_ref[...] = sum_k
    skt_ref[...] = (sum_k * scale).T
    sv_ref[...] = dot(mean_a, wv_ref[0]).astype(BF16)
    dsk_ref[...] = jnp.zeros_like(dsk_ref)
    dsv_ref[...] = jnp.zeros_like(dsv_ref)
    masks = head_masks(BF16)
    minus = [jnp.broadcast_to(-mask, (KEYS, PAIR)) for mask in masks]

    def one_row(row, carry):
        here = pl.ds(pl.multiple_of(row * ROW, ROW), ROW)
        d_out = do_ref[0, here, :]
        d_out_o = d_out * o_ref[0, here, :]
        q_t = (q_ref[0, here, :] * scale).T
        d_out_t = d_out.T
        k_t = jnp.concatenate([(k_ref[0, here, :] * scale).T, skt_ref[...]], 1)
        for pair in range(PAIRS):
            lanes = slice(pair * PAIR, (pair + 1) * PAIR)
            values = jnp.concatenate([v_ref[0, here, lanes], sv_ref[:, lanes]], 0)
            left = jnp.concatenate([d_out[:, lanes], d_out_o[:, lanes]], 1)
            for half in range(2):
                head = 2 * pair + half
                mine = slice(head * HD, (head + 1) * HD)
                right = jnp.concatenate([values * masks[half], minus[half]], 1)
                weight = e_ref[0, row, head]
                d_score = weight * dot_nt(left, right).astype(BF16)
                d_v = dot(d_out_t[mine], weight)
                d_k = dot(q_t[mine], d_score)
                d_q = dot_nt(k_t[mine], d_score)
                dt_ref[mine, :] = d_q.astype(BF16)
                dt_ref[D + head * HD : D + (head + 1) * HD, :] = d_k[:, :ROW].astype(BF16)
                dt_ref[2 * D + head * HD : 2 * D + (head + 1) * HD, :] = d_v[:, :ROW].astype(BF16)
                dsk_ref[mine, :] += d_k[:, PAIR:]
                dsv_ref[mine, :] += d_v[:, PAIR:]
        normal = xh_ref[0, here, :].astype(F32)
        a1 = (normal * g_ref[...] + s_ref[...]).astype(BF16)
        acc_ref[...] += dot(dt_ref[...], a1)
        low = (
            dot(wq_ref[0], dt_ref[0:D, :])
            + dot(wk_ref[0], dt_ref[D : 2 * D, :])
            + dot(wv_ref[0], dt_ref[2 * D : 3 * D, :])
        ).T
        dlow_ref[0, here, :] = low.astype(BF16)
        gs_ref[...] += jnp.sum(low, 0, keepdims=True)
        gg_ref[...] += jnp.sum(low * normal, 0, keepdims=True)
        return carry

    lax.fori_loop(0, rows, one_row, 0)
    d_sum_k = dsk_ref[:, ROW - PAIR :].astype(BF16)
    d_sum_v = dsv_ref[:, ROW - PAIR :].astype(BF16)
    acc_ref[D : 2 * D, :] += dot(d_sum_k, mean_a)
    acc_ref[2 * D : 3 * D, :] += dot(d_sum_v, mean_a)
    d_mean = (dot(wk_ref[0], d_sum_k) + dot(wv_ref[0], d_sum_v)).T
    dm_ref[0] = d_mean.astype(BF16)
    gs_ref[...] += jnp.sum(d_mean, 0, keepdims=True)
    gg_ref[...] += jnp.sum(d_mean * mean_x, 0, keepdims=True)

    if not last:
        return

    @pl.when(step == pl.num_programs(0) - 1)
    def _():
        for block in range(3):
            grads_ref[block] = acc_ref[block * D : (block + 1) * D, :].T.astype(BF16)


def back_call(start, stop, before, owner, operands, gain, shift, slots):
    images, count, _ = operands[0].shape
    rows = count // ROW
    first, last = start == 0, stop == images

    def at(*tail):
        zeros = (0,) * len(tail)
        return pl.BlockSpec((1,) + tail, lambda step, *_: (start + step,) + zeros)

    in_specs = (
        [at(count, D)] * 5
        + [at(rows, HEADS, ROW, KEYS), at(count, D), at(ROWS_IMG, D)]
        + [whole_spec((1, D)), whole_spec((1, D))]
        + [weight_spec(block) for block in range(3)]
    )
    inputs = [owner, *operands, gain, shift, slots, slots, slots]
    aliases = {}
    if not first:
        d_low, *sums = before
        in_specs += [whole_spec((3 * D, D)), whole_spec((1, D)), whole_spec((1, D)), pl.BlockSpec(memory_space=pl.ANY)]
        inputs += [*sums, d_low]
        aliases = {len(inputs) - 1: 0}
    return pl.pallas_call(
        functools.partial(back_kernel, first, last),
        grid_spec=pltpu.PrefetchScalarGridSpec(
            num_scalar_prefetch=1,
            grid=(stop - start,),
            in_specs=in_specs,
            out_specs=[
                at(count, D), tile_spec(ROWS_IMG, D), out_whole((3 * D, D)), out_whole((1, D)), out_whole((1, D)),
            ]
            + [out_whole((3, D, D))] * last,
            scratch_shapes=[
                pltpu.VMEM((3 * D, ROW), BF16),
                pltpu.VMEM((ROWS_IMG, D), BF16),
                pltpu.VMEM((ROWS_IMG, D), BF16),
                pltpu.VMEM((D, PAIR), F32),
                pltpu.VMEM((D, PAIR), F32),
                pltpu.VMEM((D, ROWS_IMG), BF16),
            ],
        ),
        out_shape=[
            jax.ShapeDtypeStruct((images, count, D), BF16),
            jax.ShapeDtypeStruct((stop - start, ROWS_IMG, D), BF16),
            jax.ShapeDtypeStruct((3 * D, D), F32),
            jax.ShapeDtypeStruct((1, D), F32),
            jax.ShapeDtypeStruct((1, D), F32),
        ]
        + [jax.ShapeDtypeStruct((3, D, D), BF16)] * last,
        input_output_aliases=aliases,
        compiler_params=pltpu.CompilerParams(vmem_limit_bytes=56 * MIB),
        cost_estimate=pl.CostEstimate(
            flops=(stop - start) * count * D * D * 20,
            bytes_accessed=(stop - start) * count * D * 24,
            transcendentals=0,
        ),
        name="attend_back",
    )(*inputs)


def last_kernel(x_ref, low_ref, dr_ref, dm_ref, g_ref, out_ref):
    for row in range(dm_ref.shape[1]):
        here = slice(row * ROW, (row + 1) * ROW)
        normal, spread = normalize(x_ref[0, here, :].astype(F32))
        total = low_ref[0, here, :].astype(F32) + dm_ref[0, row : row + 1, :] * (1.0 / ROW)
        d_normal = total * g_ref[...]
        middle = jnp.mean(d_normal, -1, keepdims=True)
        along = jnp.mean(d_normal * normal, -1, keepdims=True)
        out_ref[0, here, :] = dr_ref[0, here, :].astype(F32) + spread * (d_normal - middle - normal * along)


def last_call(tokens, d_low, d_branch, d_mean, gain):
    images, count, _ = tokens.shape
    return pl.pallas_call(
        last_kernel,
        grid=(images,),
        in_specs=[tile_spec(count, D)] * 3 + [tile_spec(count // ROW, D), whole_spec((1, D))],
        out_specs=tile_spec(count, D),
        out_shape=jax.ShapeDtypeStruct((images, count, D), F32),
        compiler_params=pltpu.CompilerParams(vmem_limit_bytes=40 * MIB),
        cost_estimate=pl.CostEstimate(
            flops=images * count * D * 20, bytes_accessed=images * count * D * 10, transcendentals=0
        ),
        name="norm_one_back",
    )(tokens, d_low, d_branch, d_mean, gain)


def adamw_update(weight_now, gradient, first_moment, second_moment, decay_rate, step_rate):
    first_new = 0.9 * first_moment + 0.1 * gradient
    second_new = 0.95 * second_moment + 0.05 * gradient * gradient
    direction = first_new / (1.0 - 0.9**STEP) / (jnp.sqrt(second_new / (1.0 - 0.95**STEP)) + 1e-08)
    return (weight_now - step_rate * (direction + decay_rate * weight_now), first_new, second_new)


def swap(value, axis, bit):
    size = lax.axis_size(axis)
    return lax.ppermute(value, axis, [(index, index ^ bit) for index in range(size)])


def sum_everywhere(value):
    for axis in ("narrow", "wide"):
        bit = 1
        while bit < lax.axis_size(axis):
            value = value + swap(value, axis, bit)
            bit *= 2
    return value


def join(value, axis, inner):
    size = lax.axis_size(axis)
    near = jnp.stack([value] + [swap(value, axis, inner * step) for step in range(1, size // inner)])
    far = jnp.stack([near] + [swap(near, axis, step) for step in range(1, inner)], 1)
    return jnp.take(far.reshape((size,) + value.shape), lax.axis_index(axis) ^ jnp.arange(size), axis=0)


def fetch_blocks(low_master, owners, means):
    wide = lax.axis_size("wide")
    narrow = lax.axis_size("narrow")
    pieces = lax.all_to_all(low_master.reshape(wide, -1, D), "wide", 0, 0, tiled=True)
    mine = jnp.take(pieces, owners, axis=0)
    count = owners.shape[0]
    depth = mine.shape[1]
    joined = join(jnp.concatenate([mine.reshape(-1, D), means.reshape(-1, D)], 0), "wide", near_size())
    halves = join(joined[:, : count * depth], "narrow", 1)
    blocks = halves.reshape(narrow, wide, count, depth, D).transpose(2, 0, 1, 3, 4).reshape(count, D, D)
    mean_all = joined[:, count * depth :].reshape((wide,) + means.shape).swapaxes(0, 1)
    return blocks, mean_all.reshape(means.shape[0], -1, D)


def sum_narrow(grads):
    blocks = grads.shape[0]
    narrow = lax.axis_size("narrow")
    me = lax.axis_index("narrow")
    parts = grads.reshape(blocks, narrow, D // narrow, D)
    total = lax.dynamic_index_in_dim(parts, me, 1, False).astype(F32)
    for step in range(1, narrow):
        total += swap(lax.dynamic_index_in_dim(parts, me ^ step, 1, False), "narrow", step).astype(F32)
    return total.astype(BF16)


def sum_group(pieces, stride):
    size = pieces.shape[0]
    me = lax.axis_index("wide") // stride % size
    total = lax.dynamic_index_in_dim(pieces, me, 0, False).astype(F32)
    for step in range(1, size):
        part = lax.dynamic_index_in_dim(pieces, me ^ step, 0, False)
        total += swap(part, "wide", step * stride).astype(F32)
    return total


def near_size():
    return min(4, lax.axis_size("wide"))


def to_pieces(rows):
    wide = lax.axis_size("wide")
    pieces = rows.reshape(rows.shape[0], wide, -1, D).swapaxes(0, 1)
    return pieces.reshape(wide, -1, D)


def sum_near(pieces):
    inner = near_size()
    parts = pieces.reshape((-1, inner) + pieces.shape[1:]).swapaxes(0, 1)
    return sum_group(parts, 1).astype(BF16)


def sum_far(pieces):
    return sum_group(pieces, near_size())


def to_slots(shares, owner_list, beside):
    wide = lax.axis_size("wide")
    inner = near_size()
    outer = wide // inner
    me = lax.axis_index("wide")
    far, near = me // inner, me % inner
    slotted = jnp.zeros((wide,) + shares.shape[1:], BF16).at[owner_list].set(shares.astype(BF16))
    slotted = slotted.reshape((outer, inner) + shares.shape[1:])
    parts = [lax.dynamic_index_in_dim(slotted, far, 0, False)]
    for step in range(1, outer):
        parts.append(swap(lax.dynamic_index_in_dim(slotted, far ^ step, 0, False), "wide", step * inner))
    parts, beside = lax.optimization_barrier((jnp.stack(parts, 1), beside))
    pieces = [lax.dynamic_index_in_dim(parts, near, 0, False)]
    for step in range(1, inner):
        pieces.append(swap(lax.dynamic_index_in_dim(parts, near ^ step, 0, False), "wide", step))
    pieces = jnp.stack(pieces, 1).reshape((wide,) + shares.shape[1:])
    ordered = jnp.take(pieces, me ^ jnp.arange(wide), axis=0)
    return ordered.reshape(1, -1, D).astype(F32), beside


def per_device(
    tokens, cotangent, owner_list, master, moment_one, moment_two, small_params, small_one, small_two
):
    images, count, _ = tokens.shape
    rows = count // ROW
    wide = lax.axis_size("wide")
    small = small_params.reshape(1, -1)
    gain_one = small[:, 0:D]
    shift_one = small[:, D : 2 * D]
    gain_two = small[:, 2 * D : 3 * D]
    shift_two = small[:, 3 * D : 4 * D]
    bias_up = small[:, 4 * D : 4 * D + FF]
    bias_down = small[:, 4 * D + FF :]
    low_master = master.astype(BF16)
    slots = lax.all_gather(low_master.reshape(-1, D), ("wide", "narrow"), axis=0, tiled=True)
    slots = slots.reshape(-1, D, D)
    a1, normal, means, bias_down_grad = norm_call(tokens, cotangent, gain_one, shift_one)
    blocks, mean_all = fetch_blocks(low_master, owner_list[:3], means.astype(BF16))
    first_row = (lax.axis_index("wide") * rows).astype(jnp.int32).reshape(1)
    queries, keys, values, weights, attended, inverse = attend_call(
        first_row, a1, mean_all, gain_one, shift_one, blocks
    )
    block_out, d_branch, d_out, grads_late, gain_two_grad, shift_two_grad, bias_up_grad = ff_call(
        owner_list, tokens, attended, cotangent, inverse, gain_two, shift_two, bias_up, bias_down, slots
    )
    operands = (queries, keys, values, attended, d_out, weights, normal, mean_all)
    quarter = images // 4
    cuts = (0, quarter, images - quarter, images)
    state = None
    d_means = []
    late = grads_late
    stages = (sum_narrow, lambda sums: sum_near(to_pieces(sums)), sum_far)
    for start, stop, stage in zip(cuts[:-1], cuts[1:], stages):
        moved = stage(late)
        d_low, d_mean, *state = back_call(
            start, stop, state, owner_list, operands, gain_one, shift_one, slots
        )
        late, *state = lax.optimization_barrier((moved, d_low, *state))
        d_means.append(d_mean)
    d_low, _, gain_one_grad, shift_one_grad, grads_early = state
    early = to_pieces(sum_narrow(grads_early))
    depth = early.shape[1] // 3
    last = sum_far(sum_near(jnp.concatenate([early] + [to_pieces(d_mean) for d_mean in d_means], 1)))
    own_mean = last[3 * depth :].reshape(images, rows, D)
    grad_tokens = last_call(tokens, d_low, d_branch, own_mean, gain_one)
    shares = jnp.concatenate([last[: 3 * depth], late], 0).reshape(-1, depth, D)
    own_grad, grad_tokens = to_slots(shares, owner_list, grad_tokens)
    small_grad = sum_everywhere(
        jnp.concatenate(
            [gain_one_grad, shift_one_grad, gain_two_grad, shift_two_grad, bias_up_grad, bias_down_grad], 1
        )
    ).reshape(-1)
    owns_slot = jnp.any(owner_list == lax.axis_index("wide"))
    slot_weight, slot_first, slot_second = adamw_update(
        master, own_grad, moment_one, moment_two, 0.1, RATE
    )
    new_master = jnp.where(owns_slot, slot_weight, master)
    new_one = jnp.where(owns_slot, slot_first, moment_one)
    new_two = jnp.where(owns_slot, slot_second, moment_two)
    small_new, small_one_new, small_two_new = adamw_update(
        small_params, small_grad, small_one, small_two, 0.0, GAIN_RATE
    )
    return (block_out, grad_tokens, new_master, new_one, new_two, small_new, small_one_new, small_two_new)


def solution(mesh):
    split = P("narrow", "wide", None)
    slot = P("wide", "narrow", None)
    return jax.shard_map(
        per_device,
        mesh=mesh,
        in_specs=(split, split, P(), slot, slot, slot, P(), P(), P()),
        out_specs=(split, split, slot, slot, slot, P(), P(), P()),
        check_vma=False,
    )
```

```python
import functools
import functools
import math

import jax
import jax.numpy as jnp
from jax import lax
from jax.experimental import pallas as pl
from jax.experimental.pallas import tpu as pltpu
from jax.sharding import PartitionSpec as P

D = 512
HEADS = 8
HD = 64
PAIR = 2 * HD
PAIRS = HEADS // 2
FF = 2048
NF = FF // D
ROW = 192
ROWS_IMG = 64
KEYS = ROW + ROWS_IMG
STEP = 10
RATE = 0.03
GAIN_RATE = 0.4
EPS = 1e-05
LOG2E = math.log2(math.e)
F32 = jnp.float32
BF16 = jnp.bfloat16
MIB = 1024 * 1024


def dot(left, right):
    return jnp.dot(left, right, preferred_element_type=F32)


def dot_nt(left, right):
    return lax.dot_general(left, right, (((1,), (1,)), ((), ())), preferred_element_type=F32)


def normalize(values):
    centred = values - jnp.mean(values, -1, keepdims=True)
    scale = lax.rsqrt(jnp.mean(centred * centred, -1, keepdims=True) + EPS)
    return centred * scale, scale


def head_masks(dtype):
    lane = lax.broadcasted_iota(jnp.int32, (1, PAIR), 1)
    first = (lane < HD).astype(F32)
    return first.astype(dtype), (1.0 - first).astype(dtype)


def tile_spec(*tail, buffers=None):
    zeros = (0,) * len(tail)
    return pl.BlockSpec((1,) + tail, lambda step, *_: (step,) + zeros)


def whole_spec(shape):
    zeros = (0,) * len(shape)
    return pl.BlockSpec(shape, lambda step, *_: zeros, pipeline_mode=pl.Buffered(1))


def weight_spec(block):
    return pl.BlockSpec(
        (1, D, D), lambda step, owner, *_: (owner[block], 0, 0), pipeline_mode=pl.Buffered(1)
    )


def out_whole(shape):
    zeros = (0,) * len(shape)
    return pl.BlockSpec(shape, lambda step, *_: zeros)


def norm_kernel(x_ref, xh_ref, mean_ref):
    normal, _ = normalize(x_ref[0].astype(F32))
    xh_ref[0] = normal.astype(BF16)
    for row in range(mean_ref.shape[1]):
        part = normal[row * ROW : (row + 1) * ROW]
        mean_ref[0, row : row + 1, :] = jnp.mean(part, 0, keepdims=True)


def norm_call(tokens):
    images, count, _ = tokens.shape
    rows = count // ROW
    return pl.pallas_call(
        norm_kernel,
        grid=(images,),
        in_specs=[tile_spec(count, D)],
        out_specs=[tile_spec(count, D), tile_spec(rows, D)],
        out_shape=[
            jax.ShapeDtypeStruct((images, count, D), BF16),
            jax.ShapeDtypeStruct((images, rows, D), F32),
        ],
        compiler_params=pltpu.CompilerParams(vmem_limit_bytes=60 * MIB),
        cost_estimate=pl.CostEstimate(
            flops=images * count * D * 10, bytes_accessed=images * count * D * 4, transcendentals=0
        ),
        name="norm_one",
    )(tokens)


def group_sizes(wide):
    inner = min(4, wide)
    return inner, wide // inner


def write_pieces(place, out_refs, read):
    narrow = len(out_refs)
    inner, outer, height, _ = out_refs[0].shape
    depth = D // narrow // (inner * outer)

    def one(distance, carry):
        for step, out_ref in enumerate(out_refs):
            start = (place[1] ^ step) * (D // narrow) + (place[0] ^ distance) * depth
            here = pl.ds(pl.multiple_of(start, depth), depth)
            for block in range(height // depth):
                value = read(block, here).astype(BF16)
                out_ref[distance % inner, distance // inner, block * depth : (block + 1) * depth, :] = value
        return carry

    lax.fori_loop(0, inner * outer, one, 0)


def attend_kernel(
    parts, place, xh_ref, mean_ref, g_ref, s_ref, *refs
):
    part_refs, refs = refs[:parts], refs[parts:]
    q_ref, k_ref, v_ref, e_ref, o_ref, li_ref, sk_ref, sv_ref, bias_ref, w_ref = refs
    rows = xh_ref.shape[1] // ROW
    first_row = place[0] * rows

    @pl.when(pl.program_id(0) == 0)
    def _():
        query = lax.broadcasted_iota(jnp.int32, (ROW, KEYS), 0)
        key = lax.broadcasted_iota(jnp.int32, (ROW, KEYS), 1)
        for row in range(rows):
            own = jnp.where(key <= query, 0.0, -1e30)
            earlier = jnp.where(key - ROW < first_row + row, math.log2(ROW), -1e30)
            bias_ref[row] = jnp.where(key < ROW, own, earlier)
        if parts == 1:
            w_ref[...] = part_refs[0][...]
            return
        wide, height, _ = part_refs[0].shape
        depth = D // parts // wide

        def one(distance, carry):
            for step, part_ref in enumerate(part_refs):
                start = (place[1] ^ step) * (D // parts) + (place[0] ^ distance) * depth
                here = pl.ds(pl.multiple_of(start, depth), depth)
                for block in range(3):
                    w_ref[block, here, :] = part_ref[distance, block * depth : (block + 1) * depth, :]
            return carry

        lax.fori_loop(0, wide, one, 0)

    a1 = (xh_ref[0].astype(F32) * g_ref[...] + s_ref[...]).astype(BF16)
    q_ref[0] = dot(a1, w_ref[0]).astype(BF16)
    k_ref[0] = dot(a1, w_ref[1]).astype(BF16)
    v_ref[0] = dot(a1, w_ref[2]).astype(BF16)
    mean_a = (mean_ref[0].astype(F32) * g_ref[...] + s_ref[...]).astype(BF16)
    sum_k = dot(mean_a, w_ref[1]).astype(BF16)
    sum_v = dot(mean_a, w_ref[2]).astype(BF16)
    sk_ref[0] = sum_k
    sv_ref[0] = sum_v
    masks = head_masks(BF16)
    ones = [jnp.broadcast_to(mask, (KEYS, PAIR)) for mask in masks]
    scale = LOG2E / math.sqrt(HD)

    for row in range(rows):
        here = slice(row * ROW, (row + 1) * ROW)
        for pair in range(PAIRS):
            lanes = slice(pair * PAIR, (pair + 1) * PAIR)
            query = q_ref[0, here, lanes]
            keys = jnp.concatenate([k_ref[0, here, lanes], sum_k[:, lanes]], 0)
            values = jnp.concatenate([v_ref[0, here, lanes], sum_v[:, lanes]], 0)
            total = None
            for half in range(2):
                score = dot_nt(query, keys * masks[half]) * scale + bias_ref[row]
                weight = jnp.exp2(score - jnp.max(score, -1, keepdims=True)).astype(BF16)
                e_ref[0, row, 2 * pair + half] = weight
                part = dot(weight, jnp.concatenate([values * masks[half], ones[half]], 1))
                total = part if total is None else total + part
            inverse = 1.0 / total[:, PAIR:]
            o_ref[0, here, lanes] = (total[:, :PAIR] * inverse).astype(BF16)
            li_ref[0, here, lanes] = inverse.astype(BF16)


def attend_call(place, normal, mean_all, gain, shift, parts):
    images, count, _ = normal.shape
    rows = count // ROW
    tokens_shape = jax.ShapeDtypeStruct((images, count, D), BF16)
    return pl.pallas_call(
        functools.partial(attend_kernel, len(parts)),
        grid_spec=pltpu.PrefetchScalarGridSpec(
            num_scalar_prefetch=1,
            grid=(images,),
            in_specs=[
                tile_spec(count, D), tile_spec(ROWS_IMG, D), whole_spec((1, D)), whole_spec((1, D)),
            ]
            + [whole_spec(part.shape) for part in parts],
            out_specs=[tile_spec(count, D)] * 3
            + [tile_spec(rows, HEADS, ROW, KEYS)]
            + [tile_spec(count, D)] * 2
            + [tile_spec(ROWS_IMG, D)] * 2,
            scratch_shapes=[
                pltpu.VMEM((rows, ROW, KEYS), F32),
                pltpu.VMEM((3, D, D), BF16),
            ],
        ),
        out_shape=[tokens_shape] * 3
        + [jax.ShapeDtypeStruct((images, rows, HEADS, ROW, KEYS), BF16)]
        + [tokens_shape] * 2
        + [jax.ShapeDtypeStruct((images, ROWS_IMG, D), BF16)] * 2,
        compiler_params=pltpu.CompilerParams(vmem_limit_bytes=60 * MIB),
        cost_estimate=pl.CostEstimate(
            flops=images * count * D * D * 10, bytes_accessed=images * count * D * 20, transcendentals=0
        ),
        name="attend",
    )(place, normal, mean_all, gain, shift, *parts)


def ff_kernel(
    pieces, owner, place, x_ref, o_ref, cot_ref, li_ref, g_ref, s_ref, bu_ref,
    wo_ref, u0_ref, u1_ref, u2_ref, u3_ref, d0_ref, d1_ref, d2_ref, d3_ref,
    act_ref, h_ref, dr_ref, do_ref, gg_ref, gs_ref, gbu_ref, gbd_ref, *refs
):
    grads_refs, (acc_ref, xh_ref, da_ref) = refs[:-3], refs[-3:]
    step = pl.program_id(0)
    ups = (u0_ref, u1_ref, u2_ref, u3_ref)
    downs = (d0_ref, d1_ref, d2_ref, d3_ref)

    @pl.when(step == 0)
    def _():
        acc_ref[...] = jnp.zeros_like(acc_ref)
        gg_ref[...] = jnp.zeros_like(gg_ref)
        gs_ref[...] = jnp.zeros_like(gs_ref)
        gbu_ref[...] = jnp.zeros_like(gbu_ref)
        gbd_ref[...] = jnp.zeros_like(gbd_ref)

    hidden = x_ref[0].astype(F32) + dot(o_ref[0], wo_ref[0])
    normal, spread = normalize(hidden)
    xh_ref[...] = normal
    h_ref[0] = hidden.astype(BF16)
    a2 = (normal * g_ref[...] + s_ref[...]).astype(BF16)
    a2_t = a2.T
    cot = cot_ref[0]
    cot_t = cot.T
    c_one = math.sqrt(2.0 / math.pi)
    c_two = c_one * 0.044715
    for block in range(NF):
        w_up = ups[block][0]
        w_down = downs[block][0]
        pre = dot(a2, w_up) + bu_ref[:, block * D : (block + 1) * D]
        d_act = dot_nt(cot, w_down)
        square = pre * pre
        half = 0.5 + 0.5 * jnp.tanh(pre * (c_one + c_two * square))
        act = pre * half
        slope = half + act * (1.0 - half) * (2.0 * c_one + (6.0 * c_two) * square)
        act = act.astype(BF16)
        d_pre = d_act * slope
        gbu_ref[:, block * D : (block + 1) * D] += jnp.sum(d_pre, 0, keepdims=True)
        d_pre = d_pre.astype(BF16)
        act_ref[0, :, block * D : (block + 1) * D] = act
        part = dot_nt(d_pre, w_up)
        if block == 0:
            da_ref[...] = part
        else:
            da_ref[...] += part
        acc_ref[1 + block] += dot(a2_t, d_pre)
        acc_ref[1 + NF + block] += dot(cot_t, act)
    d_a2 = da_ref[...]
    normal = xh_ref[...]
    gs_ref[...] += jnp.sum(d_a2, 0, keepdims=True)
    gg_ref[...] += jnp.sum(d_a2 * normal, 0, keepdims=True)
    d_normal = d_a2 * g_ref[...]
    middle = jnp.mean(d_normal, -1, keepdims=True)
    along = jnp.mean(d_normal * normal, -1, keepdims=True)
    cot = cot.astype(F32)
    gbd_ref[...] += jnp.sum(cot, 0, keepdims=True)
    d_hidden = cot + spread * (d_normal - middle - normal * along)
    branch = d_hidden.astype(BF16)
    dr_ref[0] = branch
    acc_ref[0] += dot(o_ref[0].T, branch)
    do_ref[0] = (dot_nt(branch, wo_ref[0]) * li_ref[0].astype(F32)).astype(BF16)

    @pl.when(step == pl.num_programs(0) - 1)
    def _():
        for block in range(1 + NF, 1 + 2 * NF):
            acc_ref[block] = acc_ref[block].T
        if pieces:
            write_pieces(place, grads_refs, lambda block, here: acc_ref[block, here, :])
        else:
            grads_refs[0][...] = acc_ref[...].astype(BF16)


def grad_shapes(groups, blocks):
    if groups is None:
        return [(blocks, D, D)]
    narrow, inner, outer = groups
    return [(inner, outer, blocks * (D // narrow // inner // outer), D)] * narrow


def ff_call(owner, place, groups, tokens, attended, cotangent, inverse, gain, shift, bias_up, slots):
    images, count, _ = tokens.shape
    tokens_shape = jax.ShapeDtypeStruct((images, count, D), BF16)
    blocks = 1 + 2 * NF
    grads = grad_shapes(groups, blocks)
    return pl.pallas_call(
        functools.partial(ff_kernel, groups is not None),
        grid_spec=pltpu.PrefetchScalarGridSpec(
            num_scalar_prefetch=2,
            grid=(images,),
            in_specs=[tile_spec(count, D)] * 4
            + [whole_spec((1, D)), whole_spec((1, D)), whole_spec((1, FF))]
            + [weight_spec(3 + block) for block in range(blocks)],
            out_specs=[tile_spec(count, FF)]
            + [tile_spec(count, D)] * 3
            + [out_whole((1, D)), out_whole((1, D)), out_whole((1, FF)), out_whole((1, D))]
            + [out_whole(shape) for shape in grads],
            scratch_shapes=[
                pltpu.VMEM((blocks, D, D), F32),
                pltpu.VMEM((count, D), F32),
                pltpu.VMEM((count, D), F32),
            ],
        ),
        out_shape=[jax.ShapeDtypeStruct((images, count, FF), BF16)]
        + [tokens_shape] * 3
        + [
            jax.ShapeDtypeStruct((1, D), F32),
            jax.ShapeDtypeStruct((1, D), F32),
            jax.ShapeDtypeStruct((1, FF), F32),
            jax.ShapeDtypeStruct((1, D), F32),
        ]
        + [jax.ShapeDtypeStruct(shape, BF16) for shape in grads],
        compiler_params=pltpu.CompilerParams(vmem_limit_bytes=60 * MIB),
        cost_estimate=pl.CostEstimate(
            flops=images * count * D * D * 46, bytes_accessed=images * count * D * 22, transcendentals=0
        ),
        name="feed_forward",
    )(owner, place, tokens, attended, cotangent, inverse, gain, shift, bias_up, *([slots] * blocks))


def down_kernel(owner, act_ref, h_ref, b_ref, d0_ref, d1_ref, d2_ref, d3_ref, *refs):
    out_ref = refs[-1]
    total = h_ref[0].astype(F32) + b_ref[...]
    for block, down in enumerate((d0_ref, d1_ref, d2_ref, d3_ref)):
        total += dot(act_ref[0, :, block * D : (block + 1) * D], down[0])
    out_ref[0] = total.astype(BF16)


def image_spec(start, *tail):
    zeros = (0,) * len(tail)
    return pl.BlockSpec((1,) + tail, lambda step, *_: (start + step,) + zeros)


def down_call(start, stop, before, owner, act, hidden, bias, slots):
    images, count, _ = hidden.shape
    earlier = [] if before is None else [before]
    return pl.pallas_call(
        down_kernel,
        grid_spec=pltpu.PrefetchScalarGridSpec(
            num_scalar_prefetch=1,
            grid=(stop - start,),
            in_specs=[image_spec(start, count, FF), image_spec(start, count, D), whole_spec((1, D))]
            + [weight_spec(4 + NF + block) for block in range(NF)]
            + [pl.BlockSpec(memory_space=pl.ANY)] * len(earlier),
            out_specs=image_spec(start, count, D),
        ),
        out_shape=jax.ShapeDtypeStruct((images, count, D), BF16),
        input_output_aliases={4 + NF: 0} if earlier else {},
        compiler_params=pltpu.CompilerParams(vmem_limit_bytes=60 * MIB),
        cost_estimate=pl.CostEstimate(
            flops=(stop - start) * count * D * D * 8,
            bytes_accessed=(stop - start) * count * D * 12,
            transcendentals=0,
        ),
        name="down",
    )(owner, act, hidden, bias, *([slots] * NF), *earlier)


def back_kernel(first, last, start, pieces, owner, place, *refs):
    (q_ref, k_ref, v_ref, o_ref, do_ref, e_ref, xh_ref, sk_ref, sv_ref, mean_ref, g_ref, s_ref) = refs[:12]
    wq_ref, wk_ref, wv_ref = refs[12:15]
    refs = refs[15:]
    if not first:
        old_acc_ref, old_gg_ref, old_gs_ref = refs[:3]
        refs = refs[4:]
    dlow_ref, dm_ref, acc_ref, gg_ref, gs_ref = refs[:5]
    grads_refs = refs[5:-3]
    grad_ref, dsk_ref, dsv_ref = refs[-3:]
    step = pl.program_id(0)
    rows = q_ref.shape[1] // ROW
    scale = 1.0 / math.sqrt(HD)

    @pl.when(step == 0)
    def _():
        acc_ref[...] = jnp.zeros_like(acc_ref) if first else old_acc_ref[...]
        gg_ref[...] = jnp.zeros_like(gg_ref) if first else old_gg_ref[...]
        gs_ref[...] = jnp.zeros_like(gs_ref) if first else old_gs_ref[...]

    sum_k = sk_ref[0]
    sum_v = sv_ref[0]
    masks = head_masks(BF16)
    blank = jnp.zeros((HD, KEYS), BF16)
    minus = jnp.full((HD, KEYS), -1.0, BF16)
    d_sum_k = jnp.zeros((ROWS_IMG, D), F32)
    d_sum_v = jnp.zeros((ROWS_IMG, D), F32)
    for row in range(rows):
        here = slice(row * ROW, (row + 1) * ROW)
        d_out = do_ref[0, here, :]
        d_out_o = d_out * o_ref[0, here, :]
        q_t = (q_ref[0, here, :] * scale).T
        d_out_t = d_out.T
        v_t = jnp.concatenate([v_ref[0, here, :], sum_v], 0).T
        d_keys = []
        d_values = []
        for pair in range(PAIRS):
            lanes = slice(pair * PAIR, (pair + 1) * PAIR)
            keys = jnp.concatenate([k_ref[0, here, lanes], sum_k[:, lanes]], 0)
            left = jnp.concatenate([d_out[:, lanes], d_out_o[:, lanes]], 1)
            d_query = None
            for half in range(2):
                head = 2 * pair + half
                mine = slice(head * HD, (head + 1) * HD)
                own = v_t[mine]
                right = [own, blank, minus, blank] if half == 0 else [blank, own, blank, minus]
                weight = e_ref[0, row, head]
                d_score = weight * dot(left, jnp.concatenate(right, 0)).astype(BF16)
                d_values.append(dot(d_out_t[mine], weight).astype(BF16))
                d_keys.append(dot(q_t[mine], d_score).astype(BF16))
                part = dot(d_score, keys * masks[half])
                d_query = part if d_query is None else d_query + part
            grad_ref[here, lanes] = (d_query * scale).astype(BF16)
        d_key = jnp.concatenate(d_keys, 0).T
        d_value = jnp.concatenate(d_values, 0).T
        grad_ref[here, D : 2 * D] = d_key[:ROW]
        grad_ref[here, 2 * D :] = d_value[:ROW]
        d_sum_k += d_key[ROW:].astype(F32)
        d_sum_v += d_value[ROW:].astype(F32)
    dsk_ref[step] = d_sum_k.astype(BF16)
    dsv_ref[step] = d_sum_v.astype(BF16)
    normal = xh_ref[0].astype(F32)
    a_t = (normal * g_ref[...] + s_ref[...]).astype(BF16).T
    low = jnp.zeros_like(normal)
    for block, w_ref in enumerate((wq_ref, wk_ref, wv_ref)):
        columns = slice(block * D, (block + 1) * D)
        acc_ref[:, columns] += dot(a_t, grad_ref[:, columns])
        low += dot_nt(grad_ref[:, columns], w_ref[0])
    dlow_ref[0] = low.astype(BF16)
    gs_ref[...] += jnp.sum(low, 0, keepdims=True)
    gg_ref[...] += jnp.sum(low * normal, 0, keepdims=True)

    @pl.when(step == pl.num_programs(0) - 1)
    def _():
        mean_x = mean_ref[start : start + dm_ref.shape[0]].reshape(-1, D).astype(F32)
        mean_t = (mean_x * g_ref[...] + s_ref[...]).astype(BF16).T
        all_k = dsk_ref[...].reshape(-1, D)
        all_v = dsv_ref[...].reshape(-1, D)
        acc_ref[:, D : 2 * D] += dot(mean_t, all_k)
        acc_ref[:, 2 * D :] += dot(mean_t, all_v)
        d_mean = dot_nt(all_k, wk_ref[0]) + dot_nt(all_v, wv_ref[0])
        dm_ref[...] = d_mean.astype(BF16).reshape(dm_ref.shape)
        gs_ref[...] += jnp.sum(d_mean, 0, keepdims=True)
        gg_ref[...] += jnp.sum(d_mean * mean_x, 0, keepdims=True)
        if last and pieces:
            write_pieces(place, grads_refs, lambda block, here: acc_ref[here, block * D : (block + 1) * D])
        elif last:
            for block in range(3):
                grads_refs[0][block] = acc_ref[:, block * D : (block + 1) * D].astype(BF16)


def back_call(start, stop, before, owner, place, groups, operands, gain, shift, slots):
    images, count, _ = operands[0].shape
    rows = count // ROW
    first, last = start == 0, stop == images

    at = functools.partial(image_spec, start)
    grads = grad_shapes(groups, 3) if last else []
    in_specs = (
        [at(count, D)] * 5
        + [at(rows, HEADS, ROW, KEYS), at(count, D), at(ROWS_IMG, D), at(ROWS_IMG, D)]
        + [whole_spec((images, ROWS_IMG, D))]
        + [whole_spec((1, D)), whole_spec((1, D))]
        + [weight_spec(block) for block in range(3)]
    )
    inputs = [owner, place, *operands, gain, shift, slots, slots, slots]
    aliases = {}
    if not first:
        d_low, *sums = before
        in_specs += [whole_spec((D, 3 * D)), whole_spec((1, D)), whole_spec((1, D)), pl.BlockSpec(memory_space=pl.ANY)]
        inputs += [*sums, d_low]
        aliases = {len(inputs) - 1: 0}
    return pl.pallas_call(
        functools.partial(back_kernel, first, last, start, groups is not None),
        grid_spec=pltpu.PrefetchScalarGridSpec(
            num_scalar_prefetch=2,
            grid=(stop - start,),
            in_specs=in_specs,
            out_specs=[
                at(count, D), out_whole((stop - start, ROWS_IMG, D)), out_whole((D, 3 * D)),
                out_whole((1, D)), out_whole((1, D)),
            ]
            + [out_whole(shape) for shape in grads],
            scratch_shapes=[
                pltpu.VMEM((count, 3 * D), BF16),
                pltpu.VMEM((stop - start, ROWS_IMG, D), BF16),
                pltpu.VMEM((stop - start, ROWS_IMG, D), BF16),
            ],
        ),
        out_shape=[
            jax.ShapeDtypeStruct((images, count, D), BF16),
            jax.ShapeDtypeStruct((stop - start, ROWS_IMG, D), BF16),
            jax.ShapeDtypeStruct((D, 3 * D), F32),
            jax.ShapeDtypeStruct((1, D), F32),
            jax.ShapeDtypeStruct((1, D), F32),
        ]
        + [jax.ShapeDtypeStruct(shape, BF16) for shape in grads],
        input_output_aliases=aliases,
        compiler_params=pltpu.CompilerParams(vmem_limit_bytes=60 * MIB),
        cost_estimate=pl.CostEstimate(
            flops=(stop - start) * count * D * D * 20,
            bytes_accessed=(stop - start) * count * D * 24,
            transcendentals=0,
        ),
        name="attend_back",
    )(*inputs)


def last_kernel(x_ref, low_ref, dr_ref, dm_ref, g_ref, *refs):
    out_ref = refs[-1]
    for row in range(dm_ref.shape[1]):
        here = slice(row * ROW, (row + 1) * ROW)
        normal, spread = normalize(x_ref[0, here, :].astype(F32))
        total = low_ref[0, here, :].astype(F32) + dm_ref[0, row : row + 1, :] * (1.0 / ROW)
        d_normal = total * g_ref[...]
        middle = jnp.mean(d_normal, -1, keepdims=True)
        along = jnp.mean(d_normal * normal, -1, keepdims=True)
        out_ref[0, here, :] = dr_ref[0, here, :].astype(F32) + spread * (d_normal - middle - normal * along)


def last_call(start, stop, before, tokens, d_low, d_branch, d_mean, gain):
    images, count, _ = tokens.shape
    earlier = [] if before is None else [before]
    return pl.pallas_call(
        last_kernel,
        grid=(stop - start,),
        in_specs=[image_spec(start, count, D)] * 3
        + [image_spec(start, count // ROW, D), whole_spec((1, D))]
        + [pl.BlockSpec(memory_space=pl.ANY)] * len(earlier),
        out_specs=image_spec(start, count, D),
        out_shape=jax.ShapeDtypeStruct((images, count, D), F32),
        input_output_aliases={5: 0} if earlier else {},
        compiler_params=pltpu.CompilerParams(vmem_limit_bytes=60 * MIB),
        cost_estimate=pl.CostEstimate(
            flops=(stop - start) * count * D * 20,
            bytes_accessed=(stop - start) * count * D * 10,
            transcendentals=0,
        ),
        name="norm_one_back",
    )(tokens, d_low, d_branch, d_mean, gain, *earlier)


def adamw_update(weight_now, gradient, first_moment, second_moment, decay_rate, step_rate):
    first_new = 0.9 * first_moment + 0.1 * gradient
    second_new = 0.95 * second_moment + 0.05 * gradient * gradient
    direction = first_new / (1.0 - 0.9**STEP) / (jnp.sqrt(second_new / (1.0 - 0.95**STEP)) + 1e-08)
    return (weight_now - step_rate * (direction + decay_rate * weight_now), first_new, second_new)


def swap(value, axis, bit):
    size = lax.axis_size(axis)
    return lax.ppermute(value, axis, [(index, index ^ bit) for index in range(size)])


def sum_everywhere(value):
    for axis in ("narrow", "wide"):
        bit = 1
        while bit < lax.axis_size(axis):
            value = value + swap(value, axis, bit)
            bit *= 2
    return value


def join(value):
    inner, outer = group_sizes(lax.axis_size("wide"))
    far = jnp.stack([value] + [swap(value, "wide", inner * step) for step in range(1, outer)])
    near = jnp.stack([far] + [swap(far, "wide", step) for step in range(1, inner)], 1)
    return near.reshape((inner * outer,) + value.shape)


def reorder(value, axis, dim=0):
    return jnp.take(value, lax.axis_index(axis) ^ jnp.arange(lax.axis_size(axis)), axis=dim)


def fetch_blocks(low_master, owners, means, whole_pieces):
    wide = lax.axis_size("wide")
    narrow = lax.axis_size("narrow")
    pieces = lax.all_to_all(low_master.reshape(wide, -1, D), "wide", 0, 0, tiled=True)
    mine = jnp.take(pieces, owners, axis=0)
    count, depth, _ = mine.shape
    joined = join(jnp.concatenate([mine.reshape(-1, D), means.reshape(-1, D)], 0))
    mean_all = reorder(joined[:, count * depth :], "wide").reshape((wide,) + means.shape).swapaxes(0, 1)
    mean_all = mean_all.reshape(means.shape[0], -1, D)
    if whole_pieces:
        return [joined] + [swap(joined, "narrow", step) for step in range(1, narrow)], mean_all
    rows = joined[:, : count * depth]
    halves = jnp.stack([rows] + [swap(rows, "narrow", step) for step in range(1, narrow)])
    halves = reorder(reorder(halves, "narrow"), "wide", 1).reshape(narrow, wide, count, depth, D)
    return [halves.transpose(2, 0, 1, 3, 4).reshape(count, D, D)], mean_all


def piece_lists(grads, groups):
    if len(grads) > 1:
        return list(grads)
    (blocks,) = grads
    narrow = lax.axis_size("narrow")
    wide = lax.axis_size("wide")
    parts = blocks.reshape(blocks.shape[0], narrow, wide, -1, D).transpose(1, 2, 0, 3, 4)
    parts = reorder(reorder(parts, "narrow"), "wide", 1)
    return [by_group(part.reshape(wide, -1, D)) for part in parts]


def by_group(pieces):
    inner, outer = group_sizes(lax.axis_size("wide"))
    return pieces.reshape((outer, inner) + pieces.shape[1:]).swapaxes(0, 1)


def sum_narrow(lists):
    total = lists[0].astype(F32)
    for step in range(1, len(lists)):
        total += swap(lists[step], "narrow", step).astype(F32)
    return total.astype(BF16)


def sum_group(pieces, stride):
    total = pieces[0].astype(F32)
    for step in range(1, len(pieces)):
        total += swap(pieces[step], "wide", step * stride).astype(F32)
    return total


def sum_near(pieces):
    return sum_group(pieces, 1).astype(BF16)


def sum_far(pieces):
    inner, _ = group_sizes(lax.axis_size("wide"))
    return sum_group(pieces, inner)


def after(value, *others):
    return lax.optimization_barrier((value, *others))[0]


def per_device(
    tokens, cotangent, owner_list, master, moment_one, moment_two, small_params, small_one, small_two
):
    images, count, _ = tokens.shape
    rows = count // ROW
    wide = lax.axis_size("wide")
    small = small_params.reshape(1, -1)
    gain_one = small[:, 0:D]
    shift_one = small[:, D : 2 * D]
    gain_two = small[:, 2 * D : 3 * D]
    shift_two = small[:, 3 * D : 4 * D]
    bias_up = small[:, 4 * D : 4 * D + FF]
    bias_down = small[:, 4 * D + FF :]
    low_master = master.astype(BF16)
    slots = lax.all_gather(low_master.reshape(-1, D), ("wide", "narrow"), axis=0, tiled=True)
    slots = slots.reshape(-1, D, D)
    narrow = lax.axis_size("narrow")
    inner, outer = group_sizes(wide)
    depth = D // narrow // wide
    groups = (narrow, inner, outer) if depth % 16 == 0 and narrow > 1 else None
    me = lax.axis_index("wide")
    place = jnp.stack([me, lax.axis_index("narrow")]).astype(jnp.int32)
    normal, means = norm_call(tokens)
    parts, mean_all = fetch_blocks(low_master, owner_list[:3], means.astype(BF16), groups is not None)
    queries, keys, values, weights, attended, inverse, sum_k, sum_v = attend_call(
        place, normal, mean_all, gain_one, shift_one, parts
    )
    act, hidden, d_branch, d_out, gain_two_grad, shift_two_grad, bias_up_grad, bias_down_grad, *grads_late = ff_call(
        owner_list, place, groups, tokens, attended, cotangent, inverse, gain_two, shift_two, bias_up, slots
    )
    quarter = images // 4
    half = images // 2

    late = piece_lists(grads_late, groups)
    block_out = down_call(0, quarter, None, owner_list, act, hidden, bias_down, slots)
    late = after(sum_narrow(late), block_out)
    operands = (after(queries, late), keys, values, attended, d_out, weights, normal, sum_k, sum_v, mean_all)
    back = functools.partial(
        back_call, owner=owner_list, place=place, groups=groups, operands=operands, gain=gain_one,
        shift=shift_one, slots=slots,
    )
    d_low, mean_first, *sums = back(0, half, None)
    late, d_low, *sums = lax.optimization_barrier((sum_near(late), d_low, *sums))
    late_shares = sum_far(late)
    d_low, mean_second, _, gain_one_grad, shift_one_grad, *grads_early = back(half, images, [d_low] + sums)

    d_mean = jnp.concatenate([mean_first, mean_second], 0).reshape(images, wide, rows, D).swapaxes(0, 1)
    d_mean = by_group(reorder(d_mean.reshape(wide, -1, D), "wide"))
    early = sum_narrow(piece_lists(grads_early, groups))
    block_out = down_call(
        quarter, images - quarter, block_out, owner_list, after(act, early), hidden, bias_down, slots
    )
    early = after(sum_near(jnp.concatenate([early, d_mean], 2)), block_out)
    block_out = down_call(
        images - quarter, images, block_out, owner_list, after(act, early), hidden, bias_down, slots
    )
    shares = after(sum_far(early), block_out)
    own_mean = shares[3 * depth :].reshape(images, rows, D)
    shares = jnp.concatenate([shares[: 3 * depth], late_shares], 0).reshape(-1, depth, D).astype(BF16)

    slotted = jnp.zeros((wide, depth, D), BF16).at[owner_list ^ me].set(shares)
    slotted = slotted.reshape(outer, inner, depth, D)
    moved = jnp.stack([slotted[0]] + [swap(slotted[step], "wide", step * inner) for step in range(1, outer)], 1)
    grad_tokens = last_call(0, half, None, tokens, d_low, d_branch, own_mean, gain_one)
    moved, grad_tokens = lax.optimization_barrier((moved, grad_tokens))
    moved = jnp.stack([moved[0]] + [swap(moved[step], "wide", step) for step in range(1, inner)], 1)
    grad_tokens = last_call(half, images, grad_tokens, tokens, d_low, d_branch, own_mean, gain_one)
    moved, grad_tokens = lax.optimization_barrier((moved, grad_tokens))
    own_grad = reorder(moved.reshape(wide, depth, D), "wide").reshape(1, -1, D).astype(F32)
    small_grad = sum_everywhere(
        jnp.concatenate(
            [gain_one_grad, shift_one_grad, gain_two_grad, shift_two_grad, bias_up_grad, bias_down_grad], 1
        )
    ).reshape(-1)
    owns_slot = jnp.any(owner_list == me)
    slot_weight, slot_first, slot_second = adamw_update(
        master, own_grad, moment_one, moment_two, 0.1, RATE
    )
    new_master = jnp.where(owns_slot, slot_weight, master)
    new_one = jnp.where(owns_slot, slot_first, moment_one)
    new_two = jnp.where(owns_slot, slot_second, moment_two)
    small_new, small_one_new, small_two_new = adamw_update(
        small_params, small_grad, small_one, small_two, 0.0, GAIN_RATE
    )
    return (block_out, grad_tokens, new_master, new_one, new_two, small_new, small_one_new, small_two_new)


def solution(mesh):
    split = P("narrow", "wide", None)
    slot = P("wide", "narrow", None)
    return jax.shard_map(
        per_device,
        mesh=mesh,
        in_specs=(split, split, P(), slot, slot, slot, P(), P(), P()),
        out_specs=(split, split, slot, slot, slot, P(), P(), P()),
        check_vma=False,
    )
```

```python
import functools
import functools
import math

import jax
import jax.numpy as jnp
from jax import lax
from jax.experimental import pallas as pl
from jax.experimental.pallas import tpu as pltpu
from jax.sharding import PartitionSpec as P

D = 512
HEADS = 8
HD = 64
PAIR = 2 * HD
PAIRS = HEADS // 2
FF = 2048
NF = FF // D
ROW = 192
ROWS_IMG = 64
KEYS = ROW + ROWS_IMG
STEP = 10
RATE = 0.03
GAIN_RATE = 0.4
EPS = 1e-05
LOG2E = math.log2(math.e)
F32 = jnp.float32
BF16 = jnp.bfloat16
MIB = 1024 * 1024


def dot(left, right):
    return jnp.dot(left, right, preferred_element_type=F32)


def dot_nt(left, right):
    return lax.dot_general(left, right, (((1,), (1,)), ((), ())), preferred_element_type=F32)


def normalize(values):
    centred = values - jnp.mean(values, -1, keepdims=True)
    scale = lax.rsqrt(jnp.mean(centred * centred, -1, keepdims=True) + EPS)
    return centred * scale, scale


def head_masks(dtype):
    lane = lax.broadcasted_iota(jnp.int32, (1, PAIR), 1)
    first = (lane < HD).astype(F32)
    return first.astype(dtype), (1.0 - first).astype(dtype)


def tile_spec(*tail, buffers=None):
    zeros = (0,) * len(tail)
    return pl.BlockSpec((1,) + tail, lambda step, *_: (step,) + zeros)


def whole_spec(shape):
    zeros = (0,) * len(shape)
    return pl.BlockSpec(shape, lambda step, *_: zeros, pipeline_mode=pl.Buffered(1))


def weight_spec(block):
    return pl.BlockSpec(
        (1, D, D), lambda step, owner, *_: (owner[block], 0, 0), pipeline_mode=pl.Buffered(1)
    )


def out_whole(shape):
    zeros = (0,) * len(shape)
    return pl.BlockSpec(shape, lambda step, *_: zeros)


def norm_kernel(x_ref, xh_ref, scale_ref, mean_ref):
    normal, scale_ref[0] = normalize(x_ref[0].astype(F32))
    xh_ref[0] = normal.astype(BF16)
    for row in range(mean_ref.shape[1]):
        part = normal[row * ROW : (row + 1) * ROW]
        mean_ref[0, row : row + 1, :] = jnp.mean(part, 0, keepdims=True)


def norm_call(tokens):
    images, count, _ = tokens.shape
    rows = count // ROW
    return pl.pallas_call(
        norm_kernel,
        grid=(images,),
        in_specs=[tile_spec(count, D)],
        out_specs=[tile_spec(count, D), tile_spec(count, 1), tile_spec(rows, D)],
        out_shape=[
            jax.ShapeDtypeStruct((images, count, D), BF16),
            jax.ShapeDtypeStruct((images, count, 1), F32),
            jax.ShapeDtypeStruct((images, rows, D), F32),
        ],
        compiler_params=pltpu.CompilerParams(vmem_limit_bytes=60 * MIB),
        cost_estimate=pl.CostEstimate(
            flops=images * count * D * 10, bytes_accessed=images * count * D * 4, transcendentals=0
        ),
        name="norm_one",
    )(tokens)


def group_sizes(wide):
    inner = min(4, wide)
    return inner, wide // inner


def write_pieces(place, out_refs, read):
    narrow = len(out_refs)
    inner, outer, height, _ = out_refs[0].shape
    depth = D // narrow // (inner * outer)

    def one(distance, carry):
        for step, out_ref in enumerate(out_refs):
            start = (place[1] ^ step) * (D // narrow) + (place[0] ^ distance) * depth
            here = pl.ds(pl.multiple_of(start, depth), depth)
            for block in range(height // depth):
                value = read(block, here).astype(BF16)
                out_ref[distance % inner, distance // inner, block * depth : (block + 1) * depth, :] = value
        return carry

    lax.fori_loop(0, inner * outer, one, 0)


def attend_kernel(
    parts, place, xh_ref, mean_ref, params_ref, *refs
):
    g_ref, s_ref = params_ref.at[:, 0:D], params_ref.at[:, D : 2 * D]
    part_refs, refs = refs[:parts], refs[parts:]
    q_ref, k_ref, v_ref, e_ref, o_ref, li_ref, sk_ref, sv_ref, bias_ref, w_ref = refs
    rows = xh_ref.shape[1] // ROW
    first_row = place[0] * rows

    @pl.when(pl.program_id(0) == 0)
    def _():
        query = lax.broadcasted_iota(jnp.int32, (ROW, KEYS), 0)
        key = lax.broadcasted_iota(jnp.int32, (ROW, KEYS), 1)
        summary = jnp.maximum(key - ROW, 0)
        image_row = (place[0] ^ lax.div(summary, rows)) * rows + lax.rem(summary, rows)
        for row in range(rows):
            own = jnp.where(key <= query, 0.0, -1e30)
            earlier = jnp.where(image_row < first_row + row, math.log2(ROW), -1e30)
            bias_ref[row] = jnp.where(key < ROW, own, earlier)
        if parts == 1:
            w_ref[...] = part_refs[0][...]
            return
        wide, height, _ = part_refs[0].shape
        depth = D // parts // wide

        def one(distance, carry):
            for step, part_ref in enumerate(part_refs):
                start = (place[1] ^ step) * (D // parts) + (place[0] ^ distance) * depth
                here = pl.ds(pl.multiple_of(start, depth), depth)
                for block in range(3):
                    w_ref[block, here, :] = part_ref[distance, block * depth : (block + 1) * depth, :]
            return carry

        lax.fori_loop(0, wide, one, 0)

    a1 = (xh_ref[0].astype(F32) * g_ref[...] + s_ref[...]).astype(BF16)
    q_ref[0] = dot(a1, w_ref[0]).astype(BF16)
    k_ref[0] = dot(a1, w_ref[1]).astype(BF16)
    v_ref[0] = dot(a1, w_ref[2]).astype(BF16)
    mean_a = (mean_ref[0].astype(F32) * g_ref[...] + s_ref[...]).astype(BF16)
    sum_k = dot(mean_a, w_ref[1]).astype(BF16)
    sum_v = dot(mean_a, w_ref[2]).astype(BF16)
    sk_ref[0] = sum_k
    sv_ref[0] = sum_v
    masks = head_masks(BF16)
    ones = [jnp.broadcast_to(mask, (KEYS, PAIR)) for mask in masks]
    scale = LOG2E / math.sqrt(HD)

    for row in range(rows):
        here = slice(row * ROW, (row + 1) * ROW)
        for pair in range(PAIRS):
            lanes = slice(pair * PAIR, (pair + 1) * PAIR)
            query = q_ref[0, here, lanes]
            keys = jnp.concatenate([k_ref[0, here, lanes], sum_k[:, lanes]], 0)
            values = jnp.concatenate([v_ref[0, here, lanes], sum_v[:, lanes]], 0)
            total = None
            for half in range(2):
                score = dot_nt(query, keys * masks[half]) * scale + bias_ref[row]
                weight = jnp.exp2(score - jnp.max(score, -1, keepdims=True)).astype(BF16)
                e_ref[0, row, 2 * pair + half] = weight
                part = dot(weight, jnp.concatenate([values * masks[half], ones[half]], 1))
                total = part if total is None else total + part
            inverse = 1.0 / total[:, PAIR:]
            o_ref[0, here, lanes] = (total[:, :PAIR] * inverse).astype(BF16)
            li_ref[0, here, lanes] = inverse.astype(BF16)


def attend_call(place, normal, mean_all, params, parts):
    images, count, _ = normal.shape
    rows = count // ROW
    tokens_shape = jax.ShapeDtypeStruct((images, count, D), BF16)
    return pl.pallas_call(
        functools.partial(attend_kernel, len(parts)),
        grid_spec=pltpu.PrefetchScalarGridSpec(
            num_scalar_prefetch=1,
            grid=(images,),
            in_specs=[
                tile_spec(count, D), tile_spec(ROWS_IMG, D), whole_spec(params.shape),
            ]
            + [whole_spec(part.shape) for part in parts],
            out_specs=[tile_spec(count, D)] * 3
            + [tile_spec(rows, HEADS, ROW, KEYS)]
            + [tile_spec(count, D)] * 2
            + [tile_spec(ROWS_IMG, D)] * 2,
            scratch_shapes=[
                pltpu.VMEM((rows, ROW, KEYS), F32),
                pltpu.VMEM((3, D, D), BF16),
            ],
        ),
        out_shape=[tokens_shape] * 3
        + [jax.ShapeDtypeStruct((images, rows, HEADS, ROW, KEYS), BF16)]
        + [tokens_shape] * 2
        + [jax.ShapeDtypeStruct((images, ROWS_IMG, D), BF16)] * 2,
        compiler_params=pltpu.CompilerParams(vmem_limit_bytes=60 * MIB),
        cost_estimate=pl.CostEstimate(
            flops=images * count * D * D * 10, bytes_accessed=images * count * D * 20, transcendentals=0
        ),
        name="attend",
    )(place, normal, mean_all, params, *parts)


def ff_kernel(
    pieces, finished, owner, place, x_ref, o_ref, cot_ref, li_ref, params_ref,
    wo_ref, u0_ref, u1_ref, u2_ref, u3_ref, d0_ref, d1_ref, d2_ref, d3_ref,
    out_ref, act_ref, h_ref, dr_ref, do_ref, small_ref, *refs
):
    grads_refs, (acc_ref, xh_ref, dp_ref) = refs[:-3], refs[-3:]
    gg_ref, gs_ref = small_ref.at[:, 0:D], small_ref.at[:, D : 2 * D]
    gbu_ref, gbd_ref = small_ref.at[:, 2 * D : 2 * D + FF], small_ref.at[:, 2 * D + FF :]
    g_ref, s_ref = params_ref.at[:, 2 * D : 3 * D], params_ref.at[:, 3 * D : 4 * D]
    bu_ref, bd_ref = params_ref.at[:, 4 * D : 4 * D + FF], params_ref.at[:, 4 * D + FF :]
    step = pl.program_id(0)
    ups = (u0_ref, u1_ref, u2_ref, u3_ref)
    downs = (d0_ref, d1_ref, d2_ref, d3_ref)

    @pl.when(step == 0)
    def _():
        acc_ref[...] = jnp.zeros_like(acc_ref)
        small_ref[...] = jnp.zeros_like(small_ref)

    hidden = x_ref[0].astype(F32) + dot(o_ref[0], wo_ref[0])
    normal, spread = normalize(hidden)
    xh_ref[...] = normal
    h_ref[0] = hidden.astype(BF16)
    a2 = (normal * g_ref[...] + s_ref[...]).astype(BF16)
    a2_t = a2.T
    cot = cot_ref[0]
    cot_t = cot.T
    c_one = math.sqrt(2.0 / math.pi)
    c_two = c_one * 0.044715
    width = D // 2
    ones = jnp.ones((16, a2_t.shape[1]), BF16)
    a2_ones = jnp.concatenate([a2_t, ones], 0)

    def first_products(start):
        block, inside = start // D, slice(start % D, start % D + width)
        pre = dot(a2, ups[block][0, :, inside]) + bu_ref[:, start : start + width]
        return pre, dot_nt(cot, downs[block][0, inside, :])

    following = first_products(0)
    for start in range(0, FF, width):
        block, inside, columns = start // D, slice(start % D, start % D + width), slice(start, start + width)
        pre, d_act = following
        if start + width < FF:
            following = first_products(start + width)
        square = pre * pre
        half = 0.5 + 0.5 * jnp.tanh(pre * (c_one + c_two * square))
        act = pre * half
        slope = half + act * (1.0 - half) * (2.0 * c_one + (6.0 * c_two) * square)
        act = act.astype(BF16)
        d_pre = (d_act * slope).astype(BF16)
        act_ref[0, :, columns] = act
        dp_ref[:, columns] = d_pre
        part = dot(a2_ones, d_pre)
        acc_ref[1 + block, :, inside] += part[:D]
        gbu_ref[:, columns] += part[D : D + 1]
        acc_ref[1 + NF + block, :, inside] += dot(cot_t, act)

    @pl.when(step < finished)
    def _():
        output(act_ref, h_ref, bd_ref, downs, out_ref)

    d_a2 = dot_nt(dp_ref[:, 0:D], ups[0][0])
    for block in range(1, NF):
        d_a2 += dot_nt(dp_ref[:, block * D : (block + 1) * D], ups[block][0])
    normal = xh_ref[...]
    gs_ref[...] += jnp.sum(d_a2, 0, keepdims=True)
    gg_ref[...] += jnp.sum(d_a2 * normal, 0, keepdims=True)
    d_normal = d_a2 * g_ref[...]
    middle = jnp.mean(d_normal, -1, keepdims=True)
    along = jnp.mean(d_normal * normal, -1, keepdims=True)
    cot = cot.astype(F32)
    gbd_ref[...] += jnp.sum(cot, 0, keepdims=True)
    d_hidden = cot + spread * (d_normal - middle - normal * along)
    branch = d_hidden.astype(BF16)
    dr_ref[0] = branch
    acc_ref[0] += dot(o_ref[0].T, branch)
    do_ref[0] = (dot_nt(branch, wo_ref[0]) * li_ref[0].astype(F32)).astype(BF16)

    @pl.when(step == pl.num_programs(0) - 1)
    def _():
        for block in range(1 + NF, 1 + 2 * NF):
            acc_ref[block] = acc_ref[block].T
        if pieces:
            write_pieces(place, grads_refs, lambda block, here: acc_ref[block, here, :])
        else:
            grads_refs[0][...] = acc_ref[...].astype(BF16)


def grad_shapes(groups, blocks):
    if groups is None:
        return [(blocks, D, D)]
    narrow, inner, outer = groups
    return [(inner, outer, blocks * (D // narrow // inner // outer), D)] * narrow


def ff_call(owner, place, groups, finished, tokens, attended, cotangent, inverse, params, slots):
    images, count, _ = tokens.shape
    tokens_shape = jax.ShapeDtypeStruct((images, count, D), BF16)
    blocks = 1 + 2 * NF
    grads = grad_shapes(groups, blocks)
    return pl.pallas_call(
        functools.partial(ff_kernel, groups is not None, finished),
        grid_spec=pltpu.PrefetchScalarGridSpec(
            num_scalar_prefetch=2,
            grid=(images,),
            in_specs=[tile_spec(count, D)] * 4
            + [whole_spec(params.shape)]
            + [weight_spec(3 + block) for block in range(blocks)],
            out_specs=[
                pl.BlockSpec((1, count, D), lambda step, *_: (jnp.minimum(step, finished - 1), 0, 0)),
                pl.BlockSpec((1, count, FF), lambda step, *_: (jnp.maximum(step - finished, 0), 0, 0)),
                pl.BlockSpec((1, count, D), lambda step, *_: (jnp.maximum(step - finished, 0), 0, 0)),
            ]
            + [tile_spec(count, D)] * 2
            + [out_whole((1, 3 * D + FF))]
            + [out_whole(shape) for shape in grads],
            scratch_shapes=[
                pltpu.VMEM((blocks, D, D), F32),
                pltpu.VMEM((count, D), F32),
                pltpu.VMEM((count, FF), BF16),
            ],
        ),
        out_shape=[
            tokens_shape,
            jax.ShapeDtypeStruct((images - finished, count, FF), BF16),
            jax.ShapeDtypeStruct((images - finished, count, D), BF16),
        ]
        + [tokens_shape] * 2
        + [jax.ShapeDtypeStruct((1, 3 * D + FF), F32)]
        + [jax.ShapeDtypeStruct(shape, BF16) for shape in grads],
        compiler_params=pltpu.CompilerParams(vmem_limit_bytes=60 * MIB),
        cost_estimate=pl.CostEstimate(
            flops=images * count * D * D * 46, bytes_accessed=images * count * D * 22, transcendentals=0
        ),
        name="feed_forward",
    )(owner, place, tokens, attended, cotangent, inverse, params, *([slots] * blocks))


def output(act_ref, h_ref, b_ref, downs, out_ref):
    total = h_ref[0].astype(F32) + b_ref[...]
    for block, down in enumerate(downs):
        total += dot(act_ref[0, :, block * D : (block + 1) * D], down[0])
    out_ref[0] = total.astype(BF16)


def down_kernel(owner, act_ref, h_ref, params_ref, d0_ref, d1_ref, d2_ref, d3_ref, before_ref, out_ref):
    output(act_ref, h_ref, params_ref.at[:, 4 * D + FF :], (d0_ref, d1_ref, d2_ref, d3_ref), out_ref)


def image_spec(start, *tail):
    zeros = (0,) * len(tail)
    return pl.BlockSpec((1,) + tail, lambda step, *_: (start + step,) + zeros)


def down_call(before, owner, act, hidden, params, slots):
    images, count, _ = before.shape
    left = hidden.shape[0]
    return pl.pallas_call(
        down_kernel,
        grid_spec=pltpu.PrefetchScalarGridSpec(
            num_scalar_prefetch=1,
            grid=(left,),
            in_specs=[tile_spec(count, FF), tile_spec(count, D), whole_spec(params.shape)]
            + [weight_spec(4 + NF + block) for block in range(NF)]
            + [pl.BlockSpec(memory_space=pl.ANY)],
            out_specs=image_spec(images - left, count, D),
        ),
        out_shape=jax.ShapeDtypeStruct((images, count, D), BF16),
        input_output_aliases={4 + NF: 0},
        compiler_params=pltpu.CompilerParams(vmem_limit_bytes=60 * MIB),
        cost_estimate=pl.CostEstimate(
            flops=left * count * D * D * 8, bytes_accessed=left * count * D * 12, transcendentals=0
        ),
        name="down",
    )(owner, act, hidden, params, *([slots] * NF), before)


def back_kernel(pieces, owner, place, *refs):
    (q_ref, k_ref, v_ref, o_ref, do_ref, e_ref, xh_ref, sk_ref, sv_ref, mean_ref, params_ref) = refs[:11]
    wq_ref, wk_ref, wv_ref = refs[11:14]
    g_ref, s_ref = params_ref.at[:, 0:D], params_ref.at[:, D : 2 * D]
    dlow_ref, dm_ref, small_ref, *grads_refs = refs[14:-4]
    gg_ref, gs_ref = small_ref.at[:, 0:D], small_ref.at[:, D : 2 * D]
    acc_ref, grad_ref, dsk_ref, dsv_ref = refs[-4:]
    step = pl.program_id(0)
    rows = q_ref.shape[1] // ROW
    scale = 1.0 / math.sqrt(HD)

    @pl.when(step == 0)
    def _():
        acc_ref[...] = jnp.zeros_like(acc_ref)
        small_ref[...] = jnp.zeros_like(small_ref)

    sum_k = sk_ref[0]
    sum_v = sv_ref[0]
    masks = head_masks(BF16)
    blank = jnp.zeros((HD, KEYS), BF16)
    minus = jnp.full((HD, KEYS), -1.0, BF16)
    d_sum_k = jnp.zeros((ROWS_IMG, D), F32)
    d_sum_v = jnp.zeros((ROWS_IMG, D), F32)
    for row in range(rows):
        here = slice(row * ROW, (row + 1) * ROW)
        d_out = do_ref[0, here, :]
        d_out_o = d_out * o_ref[0, here, :]
        q_t = (q_ref[0, here, :] * scale).T
        d_out_t = d_out.T
        v_t = jnp.concatenate([v_ref[0, here, :], sum_v], 0).T
        d_keys = []
        d_values = []
        for pair in range(PAIRS):
            lanes = slice(pair * PAIR, (pair + 1) * PAIR)
            keys = jnp.concatenate([k_ref[0, here, lanes], sum_k[:, lanes]], 0)
            left = jnp.concatenate([d_out[:, lanes], d_out_o[:, lanes]], 1)
            d_query = None
            for half in range(2):
                head = 2 * pair + half
                mine = slice(head * HD, (head + 1) * HD)
                own = v_t[mine]
                right = [own, blank, minus, blank] if half == 0 else [blank, own, blank, minus]
                weight = e_ref[0, row, head]
                d_score = weight * dot(left, jnp.concatenate(right, 0)).astype(BF16)
                d_values.append(dot(d_out_t[mine], weight).astype(BF16))
                d_keys.append(dot(q_t[mine], d_score).astype(BF16))
                part = dot(d_score, keys * masks[half])
                d_query = part if d_query is None else d_query + part
            grad_ref[here, lanes] = (d_query * scale).astype(BF16)
        d_key = jnp.concatenate(d_keys, 0).T
        d_value = jnp.concatenate(d_values, 0).T
        grad_ref[here, D : 2 * D] = d_key[:ROW]
        grad_ref[here, 2 * D :] = d_value[:ROW]
        d_sum_k += d_key[ROW:].astype(F32)
        d_sum_v += d_value[ROW:].astype(F32)
    dsk_ref[step] = d_sum_k.astype(BF16)
    dsv_ref[step] = d_sum_v.astype(BF16)
    normal = xh_ref[0].astype(F32)
    a_t = (normal * g_ref[...] + s_ref[...]).astype(BF16).T
    low = jnp.zeros_like(normal)
    for block, w_ref in enumerate((wq_ref, wk_ref, wv_ref)):
        columns = slice(block * D, (block + 1) * D)
        acc_ref[:, columns] += dot(a_t, grad_ref[:, columns])
        low += dot_nt(grad_ref[:, columns], w_ref[0])
    dlow_ref[0] = low.astype(BF16)
    gs_ref[...] += jnp.sum(low, 0, keepdims=True)
    gg_ref[...] += jnp.sum(low * normal, 0, keepdims=True)

    @pl.when(step == pl.num_programs(0) - 1)
    def _():
        mean_x = mean_ref[...].reshape(-1, D).astype(F32)
        mean_t = (mean_x * g_ref[...] + s_ref[...]).astype(BF16).T
        all_k = dsk_ref[...].reshape(-1, D)
        all_v = dsv_ref[...].reshape(-1, D)
        acc_ref[:, D : 2 * D] += dot(mean_t, all_k)
        acc_ref[:, 2 * D :] += dot(mean_t, all_v)
        d_mean = dot_nt(all_k, wk_ref[0]) + dot_nt(all_v, wv_ref[0])
        dm_ref[...] = d_mean.astype(BF16).reshape(dm_ref.shape)
        gs_ref[...] += jnp.sum(d_mean, 0, keepdims=True)
        gg_ref[...] += jnp.sum(d_mean * mean_x, 0, keepdims=True)
        if pieces:
            write_pieces(place, grads_refs, lambda block, here: acc_ref[here, block * D : (block + 1) * D])
        else:
            for block in range(3):
                grads_refs[0][block] = acc_ref[:, block * D : (block + 1) * D].astype(BF16)


def back_call(owner, place, groups, operands, params, slots):
    images, count, _ = operands[0].shape
    rows = count // ROW
    grads = grad_shapes(groups, 3)
    return pl.pallas_call(
        functools.partial(back_kernel, groups is not None),
        grid_spec=pltpu.PrefetchScalarGridSpec(
            num_scalar_prefetch=2,
            grid=(images,),
            in_specs=[tile_spec(count, D)] * 5
            + [tile_spec(rows, HEADS, ROW, KEYS), tile_spec(count, D)]
            + [tile_spec(ROWS_IMG, D)] * 2
            + [whole_spec((images, ROWS_IMG, D)), whole_spec(params.shape)]
            + [weight_spec(block) for block in range(3)],
            out_specs=[tile_spec(count, D), out_whole((images, ROWS_IMG, D)), out_whole((1, 2 * D))]
            + [out_whole(shape) for shape in grads],
            scratch_shapes=[
                pltpu.VMEM((D, 3 * D), F32),
                pltpu.VMEM((count, 3 * D), BF16),
                pltpu.VMEM((images, ROWS_IMG, D), BF16),
                pltpu.VMEM((images, ROWS_IMG, D), BF16),
            ],
        ),
        out_shape=[
            jax.ShapeDtypeStruct((images, count, D), BF16),
            jax.ShapeDtypeStruct((images, ROWS_IMG, D), BF16),
            jax.ShapeDtypeStruct((1, 2 * D), F32),
        ]
        + [jax.ShapeDtypeStruct(shape, BF16) for shape in grads],
        compiler_params=pltpu.CompilerParams(vmem_limit_bytes=60 * MIB),
        cost_estimate=pl.CostEstimate(
            flops=images * count * D * D * 20, bytes_accessed=images * count * D * 24, transcendentals=0
        ),
        name="attend_back",
    )(owner, place, *operands, params, slots, slots, slots)


def last_kernel(xh_ref, scale_ref, low_ref, dr_ref, dm_ref, params_ref, out_ref):
    g_ref = params_ref.at[:, 0:D]
    for row in range(dm_ref.shape[1]):
        here = slice(row * ROW, (row + 1) * ROW)
        normal, spread = xh_ref[0, here, :].astype(F32), scale_ref[0, here, :]
        total = low_ref[0, here, :].astype(F32) + dm_ref[0, row : row + 1, :] * (1.0 / ROW)
        d_normal = total * g_ref[...]
        middle = jnp.mean(d_normal, -1, keepdims=True)
        along = jnp.mean(d_normal * normal, -1, keepdims=True)
        out_ref[0, here, :] = dr_ref[0, here, :].astype(F32) + spread * (d_normal - middle - normal * along)


def last_call(normal, scale, d_low, d_branch, d_mean, params):
    images, count, _ = normal.shape
    return pl.pallas_call(
        last_kernel,
        grid=(images,),
        in_specs=[tile_spec(count, D), tile_spec(count, 1), tile_spec(count, D), tile_spec(count, D)]
        + [tile_spec(count // ROW, D), whole_spec(params.shape)],
        out_specs=tile_spec(count, D),
        out_shape=jax.ShapeDtypeStruct((images, count, D), F32),
        compiler_params=pltpu.CompilerParams(vmem_limit_bytes=60 * MIB),
        cost_estimate=pl.CostEstimate(
            flops=images * count * D * 20, bytes_accessed=images * count * D * 11, transcendentals=0
        ),
        name="norm_one_back",
    )(normal, scale, d_low, d_branch, d_mean, params)


def adamw_update(weight_now, gradient, first_moment, second_moment, decay_rate, step_rate):
    first_new = 0.9 * first_moment + 0.1 * gradient
    second_new = 0.95 * second_moment + 0.05 * gradient * gradient
    direction = first_new / (1.0 - 0.9**STEP) / (jnp.sqrt(second_new / (1.0 - 0.95**STEP)) + 1e-08)
    return (weight_now - step_rate * (direction + decay_rate * weight_now), first_new, second_new)


def swap(value, axis, bit):
    size = lax.axis_size(axis)
    return lax.ppermute(value, axis, [(index, index ^ bit) for index in range(size)])


def sum_steps():
    inner, outer = group_sizes(lax.axis_size("wide"))

    def bits(axis, size, stride):
        return [[(axis, stride << bit)] for bit in range(size.bit_length() - 1)]

    near = bits("wide", inner, 1)
    far = [[("wide", inner * distance) for distance in range(1, outer)]]
    return bits("narrow", lax.axis_size("narrow"), 1) + near[:1] + far + near[1:]


def join(value):
    inner, outer = group_sizes(lax.axis_size("wide"))
    far = jnp.stack([value] + [swap(value, "wide", inner * step) for step in range(1, outer)])
    near = jnp.stack([far] + [swap(far, "wide", step) for step in range(1, inner)], 1)
    return near.reshape((inner * outer,) + value.shape)


def reorder(value, axis, dim=0):
    return jnp.take(value, lax.axis_index(axis) ^ jnp.arange(lax.axis_size(axis)), axis=dim)


def fetch_blocks(low_master, owners, means, whole_pieces):
    wide = lax.axis_size("wide")
    narrow = lax.axis_size("narrow")
    pieces = lax.all_to_all(low_master.reshape(wide, -1, D), "wide", 0, 0, tiled=True)
    mine = jnp.take(pieces, owners, axis=0)
    count, depth, _ = mine.shape
    joined = join(jnp.concatenate([mine.reshape(-1, D), means.reshape(-1, D)], 0))
    mean_all = joined[:, count * depth :].reshape((wide,) + means.shape).swapaxes(0, 1)
    mean_all = mean_all.reshape(means.shape[0], -1, D)
    if whole_pieces:
        return [joined] + [swap(joined, "narrow", step) for step in range(1, narrow)], mean_all
    rows = joined[:, : count * depth]
    halves = jnp.stack([rows] + [swap(rows, "narrow", step) for step in range(1, narrow)])
    halves = reorder(reorder(halves, "narrow"), "wide", 1).reshape(narrow, wide, count, depth, D)
    return [halves.transpose(2, 0, 1, 3, 4).reshape(count, D, D)], mean_all


def piece_lists(grads, groups):
    if len(grads) > 1:
        return list(grads)
    (blocks,) = grads
    narrow = lax.axis_size("narrow")
    wide = lax.axis_size("wide")
    parts = blocks.reshape(blocks.shape[0], narrow, wide, -1, D).transpose(1, 2, 0, 3, 4)
    parts = reorder(reorder(parts, "narrow"), "wide", 1)
    return [by_group(part.reshape(wide, -1, D)) for part in parts]


def by_group(pieces):
    inner, outer = group_sizes(lax.axis_size("wide"))
    return pieces.reshape((outer, inner) + pieces.shape[1:]).swapaxes(0, 1)


def sum_narrow(lists):
    total = lists[0].astype(F32)
    for step in range(1, len(lists)):
        total += swap(lists[step], "narrow", step).astype(F32)
    return total.astype(BF16)


def sum_group(pieces, stride):
    total = pieces[0].astype(F32)
    for step in range(1, len(pieces)):
        total += swap(pieces[step], "wide", step * stride).astype(F32)
    return total


def sum_near(pieces):
    return sum_group(pieces, 1).astype(BF16)


def sum_far(pieces):
    inner, _ = group_sizes(lax.axis_size("wide"))
    return sum_group(pieces, inner)


def after(value, *others):
    return lax.optimization_barrier((value, *others))[0]


def per_device(
    tokens, cotangent, owner_list, master, moment_one, moment_two, small_params, small_one, small_two
):
    images, count, _ = tokens.shape
    rows = count // ROW
    wide = lax.axis_size("wide")
    small = small_params.reshape(1, -1)
    low_master = master.astype(BF16)
    slots = lax.all_gather(low_master.reshape(-1, D), ("wide", "narrow"), axis=0, tiled=True)
    slots = slots.reshape(-1, D, D)
    narrow = lax.axis_size("narrow")
    inner, outer = group_sizes(wide)
    depth = D // narrow // wide
    groups = (narrow, inner, outer) if depth % 16 == 0 and narrow > 1 else None
    me = lax.axis_index("wide")
    names = owner_list[None, :] == jnp.arange(wide, dtype=jnp.int32)[:, None]
    owned = jnp.any(names, 1)
    block_of = jnp.argmax(names, 1)
    place = jnp.stack([me, lax.axis_index("narrow")]).astype(jnp.int32)
    normal, scale, means = norm_call(tokens)
    parts, mean_all = fetch_blocks(low_master, owner_list[:3], means.astype(BF16), groups is not None)
    queries, keys, values, weights, attended, inverse, sum_k, sum_v = attend_call(
        place, normal, mean_all, small, parts
    )
    half = images // 2
    block_out, act, hidden, d_branch, d_out, late_small, *grads_late = ff_call(
        owner_list, place, groups, images - half, tokens, attended, cotangent, inverse, small, slots
    )

    tie = lax.optimization_barrier
    late, queries = tie((sum_narrow(piece_lists(grads_late, groups)), queries))
    operands = (queries, keys, values, attended, d_out, weights, normal, sum_k, sum_v, mean_all)
    d_low, d_mean, early_small, *grads_early = back_call(
        owner_list, place, groups, operands, small, slots
    )
    late, early_small, *grads_early = tie((sum_near(late), early_small, *grads_early))
    small_sums = jnp.concatenate([early_small, late_small], 1)
    steps = sum_steps()

    def small_step():
        total = small_sums
        for axis, distance in steps.pop(0) if steps else ():
            total += swap(small_sums, axis, distance)
        return total

    d_mean = d_mean.reshape(images, wide, rows, D).swapaxes(0, 1).reshape(wide, -1, D)
    d_mean = by_group(d_mean)
    early, small_sums, act, late = tie((sum_narrow(piece_lists(grads_early, groups)), small_step(), act, late))
    late = sum_far(late)
    block_out = down_call(block_out, owner_list, act, hidden, small, slots)
    early = sum_near(jnp.concatenate([early, d_mean], 2))
    early, late, small_sums, block_out = tie((early, late, small_step(), block_out))
    shares, small_sums = tie((sum_far(early), small_step()))
    own_mean = shares[3 * depth :].reshape(images, rows, D)
    shares = jnp.concatenate([shares[: 3 * depth], late], 0).reshape(-1, depth, D).astype(BF16)

    moved = jnp.where(owned[:, None, None], jnp.take(shares, block_of, axis=0), jnp.zeros((), BF16))
    moved = lax.all_to_all(moved, "wide", 0, 0, tiled=True)
    small_sums = small_step()
    grad_tokens = last_call(normal, scale, d_low, d_branch, own_mean, small)
    moved, small_sums, grad_tokens = tie((moved, small_sums, grad_tokens))
    own_grad = moved.reshape(1, -1, D).astype(F32)
    while steps:
        small_sums = small_step()
    small_grad = small_sums.reshape(-1)
    owns_slot = jnp.any(owner_list == me)
    slot_weight, slot_first, slot_second = adamw_update(
        master, own_grad, moment_one, moment_two, 0.1, RATE
    )
    new_master = jnp.where(owns_slot, slot_weight, master)
    new_one = jnp.where(owns_slot, slot_first, moment_one)
    new_two = jnp.where(owns_slot, slot_second, moment_two)
    small_new, small_one_new, small_two_new = adamw_update(
        small_params, small_grad, small_one, small_two, 0.0, GAIN_RATE
    )
    return (block_out, grad_tokens, new_master, new_one, new_two, small_new, small_one_new, small_two_new)


def solution(mesh):
    split = P("narrow", "wide", None)
    slot = P("wide", "narrow", None)
    return jax.shard_map(
        per_device,
        mesh=mesh,
        in_specs=(split, split, P(), slot, slot, slot, P(), P(), P()),
        out_specs=(split, split, slot, slot, slot, P(), P(), P()),
        check_vma=False,
    )
```

```python
import functools
import functools
import itertools
import math

import jax
import jax.numpy as jnp
from jax import lax
from jax.experimental import pallas as pl
from jax.experimental.pallas import tpu as pltpu
from jax.sharding import PartitionSpec as P

D = 512
HEADS = 8
HD = 64
PAIR = 2 * HD
PAIRS = HEADS // 2
FF = 2048
NF = FF // D
ROW = 192
ROWS_IMG = 64
KEYS = ROW + ROWS_IMG
STEP = 10
RATE = 0.03
GAIN_RATE = 0.4
EPS = 1e-05
LOG2E = math.log2(math.e)
F32 = jnp.float32
BF16 = jnp.bfloat16
MIB = 1024 * 1024


def dot(left, right):
    return jnp.dot(left, right, preferred_element_type=F32)


def dot_nt(left, right):
    return lax.dot_general(left, right, (((1,), (1,)), ((), ())), preferred_element_type=F32)


def normalize(values):
    centred = values - jnp.mean(values, -1, keepdims=True)
    scale = lax.rsqrt(jnp.mean(centred * centred, -1, keepdims=True) + EPS)
    return centred * scale, scale


def head_masks(dtype):
    lane = lax.broadcasted_iota(jnp.int32, (1, PAIR), 1)
    first = (lane < HD).astype(F32)
    return first.astype(dtype), (1.0 - first).astype(dtype)


def tile_spec(*tail, buffers=None):
    zeros = (0,) * len(tail)
    return pl.BlockSpec((1,) + tail, lambda step, *_: (step,) + zeros)


def two_spec(*tail):
    zeros = (0,) * len(tail)
    return pl.BlockSpec((2,) + tail, lambda step, *_: (step,) + zeros)


def whole_spec(shape):
    zeros = (0,) * len(shape)
    return pl.BlockSpec(shape, lambda step, *_: zeros, pipeline_mode=pl.Buffered(1))


def weight_spec(block):
    return pl.BlockSpec(
        (1, D, D), lambda step, owner, *_: (owner[block], 0, 0), pipeline_mode=pl.Buffered(1)
    )


def out_whole(shape):
    zeros = (0,) * len(shape)
    return pl.BlockSpec(shape, lambda step, *_: zeros)


def with_ones(rows):
    return jnp.concatenate([rows, jnp.ones((16, rows.shape[1]), rows.dtype)], 0)


def norm_kernel(x_ref, xh_ref, scale_ref, mean_ref):
    normal, scale_ref[0] = normalize(x_ref[0].astype(F32))
    xh_ref[0] = normal.astype(BF16)
    for row in range(mean_ref.shape[1]):
        part = normal[row * ROW : (row + 1) * ROW]
        mean_ref[0, row : row + 1, :] = jnp.mean(part, 0, keepdims=True).astype(BF16)


def norm_call(tokens):
    images, count, _ = tokens.shape
    rows = count // ROW
    return pl.pallas_call(
        norm_kernel,
        grid=(images,),
        in_specs=[tile_spec(count, D)],
        out_specs=[tile_spec(count, D), tile_spec(count, 1), tile_spec(rows, D)],
        out_shape=[
            jax.ShapeDtypeStruct((images, count, D), BF16),
            jax.ShapeDtypeStruct((images, count, 1), F32),
            jax.ShapeDtypeStruct((images, rows, D), BF16),
        ],
        compiler_params=pltpu.CompilerParams(vmem_limit_bytes=60 * MIB),
        cost_estimate=pl.CostEstimate(
            flops=images * count * D * 10, bytes_accessed=images * count * D * 4, transcendentals=0
        ),
        name="norm_one",
    )(tokens)


def group_sizes(wide):
    inner = min(4, wide)
    return inner, wide // inner


def write_pieces(place, out_refs, read):
    narrow = len(out_refs)
    inner, outer, height, _ = out_refs[0].shape
    depth = D // narrow // (inner * outer)

    def one(distance, carry):
        for step, out_ref in enumerate(out_refs):
            start = (place[1] ^ step) * (D // narrow) + (place[0] ^ distance) * depth
            here = pl.ds(pl.multiple_of(start, depth), depth)
            for block in range(height // depth):
                value = read(block, here).astype(BF16)
                out_ref[distance % inner, distance // inner, block * depth : (block + 1) * depth, :] = value
        return carry

    lax.fori_loop(0, inner * outer, one, 0)


def attend_kernel(
    parts, place, xh_ref, mean_ref, params_ref, *refs
):
    g_ref, s_ref = params_ref.at[:, 0:D], params_ref.at[:, D : 2 * D]
    part_refs, refs = refs[:parts], refs[parts:]
    q_ref, k_ref, v_ref, e_ref, o_ref, li_ref, sk_ref, sv_ref, bias_ref, w_ref = refs
    rows = xh_ref.shape[1] // ROW
    first_row = place[0] * rows

    @pl.when(pl.program_id(0) == 0)
    def _():
        query = lax.broadcasted_iota(jnp.int32, (ROW, KEYS), 0)
        key = lax.broadcasted_iota(jnp.int32, (ROW, KEYS), 1)
        summary = jnp.maximum(key - ROW, 0)
        image_row = (place[0] ^ lax.div(summary, rows)) * rows + lax.rem(summary, rows)
        for row in range(rows):
            own = jnp.where(key <= query, 0.0, -1e30)
            earlier = jnp.where(image_row < first_row + row, math.log2(ROW), -1e30)
            bias_ref[row] = jnp.where(key < ROW, own, earlier)
        if parts == 1:
            w_ref[...] = part_refs[0][...]
            return
        wide, height, _ = part_refs[0].shape
        depth = D // parts // wide

        def one(distance, carry):
            for step, part_ref in enumerate(part_refs):
                start = (place[1] ^ step) * (D // parts) + (place[0] ^ distance) * depth
                here = pl.ds(pl.multiple_of(start, depth), depth)
                for block in range(3):
                    w_ref[block, here, :] = part_ref[distance, block * depth : (block + 1) * depth, :]
            return carry

        lax.fori_loop(0, wide, one, 0)

    a1 = (xh_ref[0].astype(F32) * g_ref[...] + s_ref[...]).astype(BF16)
    q_ref[0] = dot(a1, w_ref[0]).astype(BF16)
    k_ref[0] = dot(a1, w_ref[1]).astype(BF16)
    v_ref[0] = dot(a1, w_ref[2]).astype(BF16)
    mean_a = (mean_ref[0].astype(F32) * g_ref[...] + s_ref[...]).astype(BF16)
    sum_k = dot(mean_a, w_ref[1]).astype(BF16)
    sum_v = dot(mean_a, w_ref[2]).astype(BF16)
    sk_ref[0] = sum_k
    sv_ref[0] = sum_v
    masks = head_masks(BF16)
    ones = [jnp.broadcast_to(mask, (KEYS, PAIR)) for mask in masks]
    scale = LOG2E / math.sqrt(HD)

    for row in range(rows):
        here = slice(row * ROW, (row + 1) * ROW)
        for pair in range(PAIRS):
            lanes = slice(pair * PAIR, (pair + 1) * PAIR)
            query = q_ref[0, here, lanes]
            keys = jnp.concatenate([k_ref[0, here, lanes], sum_k[:, lanes]], 0)
            values = jnp.concatenate([v_ref[0, here, lanes], sum_v[:, lanes]], 0)
            total = None
            for half in range(2):
                score = dot_nt(query, keys * masks[half]) * scale + bias_ref[row]
                weight = jnp.exp2(score - jnp.max(score, -1, keepdims=True)).astype(BF16)
                e_ref[0, row, 2 * pair + half] = weight
                part = dot(weight, jnp.concatenate([values * masks[half], ones[half]], 1))
                total = part if total is None else total + part
            inverse = 1.0 / total[:, PAIR:]
            o_ref[0, here, lanes] = (total[:, :PAIR] * inverse).astype(BF16)
            li_ref[0, here, lanes] = inverse.astype(BF16)


def attend_call(place, normal, mean_all, params, parts):
    images, count, _ = normal.shape
    rows = count // ROW
    tokens_shape = jax.ShapeDtypeStruct((images, count, D), BF16)
    return pl.pallas_call(
        functools.partial(attend_kernel, len(parts)),
        grid_spec=pltpu.PrefetchScalarGridSpec(
            num_scalar_prefetch=1,
            grid=(images,),
            in_specs=[
                tile_spec(count, D), tile_spec(ROWS_IMG, D), whole_spec(params.shape),
            ]
            + [whole_spec(part.shape) for part in parts],
            out_specs=[tile_spec(count, D)] * 3
            + [tile_spec(rows, HEADS, ROW, KEYS)]
            + [tile_spec(count, D)] * 2
            + [tile_spec(ROWS_IMG, D)] * 2,
            scratch_shapes=[
                pltpu.VMEM((rows, ROW, KEYS), F32),
                pltpu.VMEM((3, D, D), BF16),
            ],
        ),
        out_shape=[tokens_shape] * 3
        + [jax.ShapeDtypeStruct((images, rows, HEADS, ROW, KEYS), BF16)]
        + [tokens_shape] * 2
        + [jax.ShapeDtypeStruct((images, ROWS_IMG, D), BF16)] * 2,
        compiler_params=pltpu.CompilerParams(vmem_limit_bytes=60 * MIB),
        cost_estimate=pl.CostEstimate(
            flops=images * count * D * D * 10, bytes_accessed=images * count * D * 20, transcendentals=0
        ),
        name="attend",
    )(place, normal, mean_all, params, *parts)


def ff_kernel(
    pieces, owner, place, x_ref, o_ref, cot_ref, li_ref, params_ref,
    wo_ref, u0_ref, u1_ref, u2_ref, u3_ref, d0_ref, d1_ref, d2_ref, d3_ref,
    out_ref, dr_ref, do_ref, small_ref, *refs
):
    grads_refs, (acc_ref, h_ref, xh_ref, act_ref, dp_ref) = refs[:-5], refs[-5:]
    gg_ref, gs_ref = small_ref.at[:, 0:D], small_ref.at[:, D : 2 * D]
    gbu_ref, gbd_ref = small_ref.at[:, 2 * D : 2 * D + FF], small_ref.at[:, 2 * D + FF :]
    g_ref, s_ref = params_ref.at[:, 2 * D : 3 * D], params_ref.at[:, 3 * D : 4 * D]
    bu_ref, bd_ref = params_ref.at[:, 4 * D : 4 * D + FF], params_ref.at[:, 4 * D + FF :]
    step = pl.program_id(0)
    ups = (u0_ref, u1_ref, u2_ref, u3_ref)
    downs = (d0_ref, d1_ref, d2_ref, d3_ref)

    @pl.when(step == 0)
    def _():
        acc_ref[...] = jnp.zeros_like(acc_ref)
        small_ref[...] = jnp.zeros_like(small_ref)

    hidden = x_ref[0].astype(F32) + dot(o_ref[0], wo_ref[0])
    normal, spread = normalize(hidden)
    xh_ref[...] = normal
    h_ref[...] = hidden + bd_ref[...]
    a2 = (normal * g_ref[...] + s_ref[...]).astype(BF16)
    a2_t = a2.T
    cot = cot_ref[0]
    cot_t = cot.T
    c_one = math.sqrt(2.0 / math.pi)
    c_two = c_one * 0.044715
    width = D // 2
    a2_ones = with_ones(a2_t)

    def first_products(start):
        block, inside = start // D, slice(start % D, start % D + width)
        pre = dot(a2, ups[block][0, :, inside]) + bu_ref[:, start : start + width]
        return pre, dot_nt(cot, downs[block][0, inside, :])

    following = first_products(0)
    for start in range(0, FF, width):
        block, inside, columns = start // D, slice(start % D, start % D + width), slice(start, start + width)
        pre, d_act = following
        if start + width < FF:
            following = first_products(start + width)
        square = pre * pre
        half = 0.5 + 0.5 * jnp.tanh(pre * (c_one + c_two * square))
        act = pre * half
        slope = half + act * (1.0 - half) * (2.0 * c_one + (6.0 * c_two) * square)
        act = act.astype(BF16)
        d_pre = (d_act * slope).astype(BF16)
        act_ref[:, columns] = act
        dp_ref[:, columns] = d_pre
        part = dot(a2_ones, d_pre)
        acc_ref[1 + block, :, inside] += part[:D]
        gbu_ref[:, columns] += part[D : D + 1]
        acc_ref[1 + NF + block, :, inside] += dot(cot_t, act)
    d_a2 = dot_nt(dp_ref[:, 0:D], ups[0][0])
    for block in range(1, NF):
        d_a2 += dot_nt(dp_ref[:, block * D : (block + 1) * D], ups[block][0])
    normal = xh_ref[...]
    gs_ref[...] += jnp.sum(d_a2, 0, keepdims=True)
    gg_ref[...] += jnp.sum(d_a2 * normal, 0, keepdims=True)
    d_normal = d_a2 * g_ref[...]
    middle = jnp.mean(d_normal, -1, keepdims=True)
    along = jnp.mean(d_normal * normal, -1, keepdims=True)
    cot = cot.astype(F32)
    gbd_ref[...] += jnp.sum(cot, 0, keepdims=True)
    d_hidden = cot + spread * (d_normal - middle - normal * along)
    branch = d_hidden.astype(BF16)
    dr_ref[0] = branch
    total = h_ref[...]
    for block, down in enumerate(downs):
        total += dot(act_ref[:, block * D : (block + 1) * D], down[0])
    out_ref[0] = total.astype(BF16)
    acc_ref[0] += dot(o_ref[0].T, branch)
    do_ref[0] = (dot_nt(branch, wo_ref[0]) * li_ref[0].astype(F32)).astype(BF16)

    @pl.when(step == pl.num_programs(0) - 1)
    def _():
        for block in range(1 + NF, 1 + 2 * NF):
            acc_ref[block] = acc_ref[block].T
        if pieces:
            write_pieces(place, grads_refs, lambda block, here: acc_ref[block, here, :])
        else:
            grads_refs[0][...] = acc_ref[...].astype(BF16)


def grad_shapes(groups, blocks):
    if groups is None:
        return [(blocks, D, D)]
    narrow, inner, outer = groups
    return [(inner, outer, blocks * (D // narrow // inner // outer), D)] * narrow


def ff_call(owner, place, groups, tokens, attended, cotangent, inverse, params, slots):
    images, count, _ = tokens.shape
    tokens_shape = jax.ShapeDtypeStruct((images, count, D), BF16)
    blocks = 1 + 2 * NF
    grads = grad_shapes(groups, blocks)
    return pl.pallas_call(
        functools.partial(ff_kernel, groups is not None),
        grid_spec=pltpu.PrefetchScalarGridSpec(
            num_scalar_prefetch=2,
            grid=(images,),
            in_specs=[tile_spec(count, D)] * 4
            + [whole_spec(params.shape)]
            + [weight_spec(3 + block) for block in range(blocks)],
            out_specs=[tile_spec(count, D)] * 3
            + [out_whole((1, 3 * D + FF))]
            + [out_whole(shape) for shape in grads],
            scratch_shapes=[
                pltpu.VMEM((blocks, D, D), F32),
                pltpu.VMEM((count, D), F32),
                pltpu.VMEM((count, D), F32),
                pltpu.VMEM((count, FF), BF16),
                pltpu.VMEM((count, FF), BF16),
            ],
        ),
        out_shape=[tokens_shape] * 3
        + [jax.ShapeDtypeStruct((1, 3 * D + FF), F32)]
        + [jax.ShapeDtypeStruct(shape, BF16) for shape in grads],
        compiler_params=pltpu.CompilerParams(vmem_limit_bytes=60 * MIB),
        cost_estimate=pl.CostEstimate(
            flops=images * count * D * D * 54, bytes_accessed=images * count * D * 14, transcendentals=0
        ),
        name="feed_forward",
    )(owner, place, tokens, attended, cotangent, inverse, params, *([slots] * blocks))


def back_kernel(pieces, owner, place, *refs):
    (q_ref, k_ref, v_ref, o_ref, do_ref, e_ref, xh_ref, sk_ref, sv_ref, mean_ref, params_ref) = refs[:11]
    weights = refs[11:14]
    grad_ref, dm_ref, small_ref, *grads_refs = refs[14:-3]
    acc_ref, dsk_ref, dsv_ref = refs[-3:]
    step = pl.program_id(0)
    rows = q_ref.shape[1] // ROW
    scale = 1.0 / math.sqrt(HD)

    @pl.when(step == 0)
    def _():
        acc_ref[...] = jnp.zeros_like(acc_ref)

    sum_k = sk_ref[0]
    sum_v = sv_ref[0]
    masks = head_masks(BF16)
    blank = jnp.zeros((HD, KEYS), BF16)
    minus = jnp.full((HD, KEYS), -1.0, BF16)
    d_sum_k = jnp.zeros((ROWS_IMG, D), F32)
    d_sum_v = jnp.zeros((ROWS_IMG, D), F32)
    for row in range(rows):
        here = slice(row * ROW, (row + 1) * ROW)
        d_out = do_ref[0, here, :]
        d_out_o = d_out * o_ref[0, here, :]
        q_t = (q_ref[0, here, :] * scale).T
        d_out_t = d_out.T
        v_t = jnp.concatenate([v_ref[0, here, :], sum_v], 0).T
        d_keys = []
        d_values = []
        for pair in range(PAIRS):
            lanes = slice(pair * PAIR, (pair + 1) * PAIR)
            keys = jnp.concatenate([k_ref[0, here, lanes], sum_k[:, lanes]], 0)
            left = jnp.concatenate([d_out[:, lanes], d_out_o[:, lanes]], 1)
            d_query = None
            for half in range(2):
                head = 2 * pair + half
                mine = slice(head * HD, (head + 1) * HD)
                own = v_t[mine]
                right = [own, blank, minus, blank] if half == 0 else [blank, own, blank, minus]
                weight = e_ref[0, row, head]
                d_score = weight * dot(left, jnp.concatenate(right, 0)).astype(BF16)
                d_values.append(dot(d_out_t[mine], weight).astype(BF16))
                d_keys.append(dot(q_t[mine], d_score).astype(BF16))
                part = dot(d_score, keys * masks[half])
                d_query = part if d_query is None else d_query + part
            grad_ref[0, here, lanes] = (d_query * scale).astype(BF16)
        d_key = jnp.concatenate(d_keys, 0).T
        d_value = jnp.concatenate(d_values, 0).T
        grad_ref[0, here, D : 2 * D] = d_key[:ROW]
        grad_ref[0, here, 2 * D :] = d_value[:ROW]
        d_sum_k += d_key[ROW:].astype(F32)
        d_sum_v += d_value[ROW:].astype(F32)
    dsk_ref[step] = d_sum_k.astype(BF16)
    dsv_ref[step] = d_sum_v.astype(BF16)
    acc_ref[...] += dot(with_ones(xh_ref[0].T), grad_ref[0])

    @pl.when(step == pl.num_programs(0) - 1)
    def _():
        mean_t = with_ones(mean_ref[...].reshape(-1, D).T)
        all_k = dsk_ref[...].reshape(-1, D)
        all_v = dsv_ref[...].reshape(-1, D)
        acc_ref[:, D : 2 * D] += dot(mean_t, all_k)
        acc_ref[:, 2 * D :] += dot(mean_t, all_v)
        d_mean = dot_nt(all_k, weights[1][0]) + dot_nt(all_v, weights[2][0])
        dm_ref[...] = d_mean.astype(BF16).reshape(dm_ref.shape)
        gain_grad = jnp.zeros((D, 1), F32)
        shift_grad = jnp.zeros((1, D), F32)
        gain = jnp.broadcast_to(params_ref[:, 0:D], (8, D)).T[:, 0:1]
        shift = jnp.broadcast_to(params_ref[:, D : 2 * D], (8, D)).T[:, 0:1]
        for block, w_ref in enumerate(weights):
            columns = slice(block * D, (block + 1) * D)
            product = acc_ref[0:D, columns]
            sums = acc_ref[D : D + 1, columns]
            gain_grad += jnp.sum(product * w_ref[0].astype(F32), -1, keepdims=True)
            high = sums.astype(BF16)
            parts = jnp.concatenate([high, (sums - high.astype(F32)).astype(BF16)], 0)
            parts = jnp.concatenate([parts, jnp.zeros((14, D), BF16)], 0)
            shift_grad += jnp.sum(dot_nt(parts, w_ref[0]), 0, keepdims=True)
            acc_ref[0:D, columns] = product * gain + shift * sums
        small_ref[:, 0:D] = jnp.broadcast_to(gain_grad, (D, 128)).T[0:1]
        small_ref[:, D:] = shift_grad
        if pieces:
            write_pieces(place, grads_refs, lambda block, here: acc_ref[here, block * D : (block + 1) * D])
        else:
            for block in range(3):
                grads_refs[0][block] = acc_ref[0:D, block * D : (block + 1) * D].astype(BF16)


def back_call(owner, place, groups, operands, params, slots):
    images, count, _ = operands[0].shape
    rows = count // ROW
    grads = grad_shapes(groups, 3)
    return pl.pallas_call(
        functools.partial(back_kernel, groups is not None),
        grid_spec=pltpu.PrefetchScalarGridSpec(
            num_scalar_prefetch=2,
            grid=(images,),
            in_specs=[tile_spec(count, D)] * 5
            + [tile_spec(rows, HEADS, ROW, KEYS), tile_spec(count, D)]
            + [tile_spec(ROWS_IMG, D)] * 2
            + [whole_spec((images, ROWS_IMG, D)), whole_spec(params.shape)]
            + [weight_spec(block) for block in range(3)],
            out_specs=[tile_spec(count, 3 * D), out_whole((images, ROWS_IMG, D)), out_whole((1, 2 * D))]
            + [out_whole(shape) for shape in grads],
            scratch_shapes=[
                pltpu.VMEM((D + 16, 3 * D), F32),
                pltpu.VMEM((images, ROWS_IMG, D), BF16),
                pltpu.VMEM((images, ROWS_IMG, D), BF16),
            ],
        ),
        out_shape=[
            jax.ShapeDtypeStruct((images, count, 3 * D), BF16),
            jax.ShapeDtypeStruct((images, ROWS_IMG, D), BF16),
            jax.ShapeDtypeStruct((1, 2 * D), F32),
        ]
        + [jax.ShapeDtypeStruct(shape, BF16) for shape in grads],
        compiler_params=pltpu.CompilerParams(vmem_limit_bytes=60 * MIB),
        cost_estimate=pl.CostEstimate(
            flops=images * count * D * D * 20, bytes_accessed=images * count * D * 24, transcendentals=0
        ),
        name="attend_back",
    )(owner, place, *operands, params, slots, slots, slots)


def low_kernel(owner, grad_ref, wq_ref, wk_ref, wv_ref, low_ref):
    joined = jnp.concatenate([wq_ref[0], wk_ref[0], wv_ref[0]], 1)
    low_ref[...] = dot_nt(grad_ref[...].reshape(-1, 3 * D), joined).astype(BF16).reshape(low_ref.shape)


def low_call(owner, grads, slots):
    images, count, _ = grads.shape
    return pl.pallas_call(
        low_kernel,
        grid_spec=pltpu.PrefetchScalarGridSpec(
            num_scalar_prefetch=1,
            grid=(images // 2,),
            in_specs=[two_spec(count, 3 * D)] + [weight_spec(block) for block in range(3)],
            out_specs=two_spec(count, D),
        ),
        out_shape=jax.ShapeDtypeStruct((images, count, D), BF16),
        compiler_params=pltpu.CompilerParams(vmem_limit_bytes=60 * MIB),
        cost_estimate=pl.CostEstimate(
            flops=images * count * D * D * 6, bytes_accessed=images * count * D * 8, transcendentals=0
        ),
        name="project_back",
    )(owner, grads, slots, slots, slots)


def last_kernel(xh_ref, scale_ref, low_ref, dr_ref, dm_ref, params_ref, out_ref):
    g_ref = params_ref.at[:, 0:D]
    for image, row in itertools.product(range(2), range(dm_ref.shape[1])):
        here = slice(row * ROW, (row + 1) * ROW)
        normal, spread = xh_ref[image, here, :].astype(F32), scale_ref[image, here, :]
        total = low_ref[image, here, :].astype(F32) + dm_ref[image, row : row + 1, :] * (1.0 / ROW)
        d_normal = total * g_ref[...]
        middle = jnp.mean(d_normal, -1, keepdims=True)
        along = jnp.mean(d_normal * normal, -1, keepdims=True)
        out_ref[image, here, :] = dr_ref[image, here, :].astype(F32) + spread * (d_normal - middle - normal * along)


def last_call(normal, scale, d_low, d_branch, d_mean, params):
    images, count, _ = normal.shape
    return pl.pallas_call(
        last_kernel,
        grid=(images // 2,),
        in_specs=[two_spec(count, D), two_spec(count, 1), two_spec(count, D), two_spec(count, D)]
        + [two_spec(count // ROW, D), whole_spec(params.shape)],
        out_specs=two_spec(count, D),
        out_shape=jax.ShapeDtypeStruct((images, count, D), F32),
        compiler_params=pltpu.CompilerParams(vmem_limit_bytes=60 * MIB),
        cost_estimate=pl.CostEstimate(
            flops=images * count * D * 20, bytes_accessed=images * count * D * 11, transcendentals=0
        ),
        name="norm_one_back",
    )(normal, scale, d_low, d_branch, d_mean, params)


def adamw_update(weight_now, gradient, first_moment, second_moment, decay_rate, step_rate):
    first_new = 0.9 * first_moment + 0.1 * gradient
    second_new = 0.95 * second_moment + 0.05 * gradient * gradient
    direction = first_new / (1.0 - 0.9**STEP) / (jnp.sqrt(second_new / (1.0 - 0.95**STEP)) + 1e-08)
    return (weight_now - step_rate * (direction + decay_rate * weight_now), first_new, second_new)


def swap(value, axis, bit):
    size = lax.axis_size(axis)
    return lax.ppermute(value, axis, [(index, index ^ bit) for index in range(size)])


def to_rows(values):
    high = lax.reduce_precision(values, 8, 7)
    rows = jnp.concatenate([high, values - high], 1).reshape(-1, D).astype(BF16)
    return jnp.pad(rows, ((0, -rows.shape[0] % 16), (0, 0)))


def from_rows(rows, size):
    count = size // D
    return (rows[:count] + rows[count : 2 * count]).reshape(1, size)


def join(value):
    inner, outer = group_sizes(lax.axis_size("wide"))
    far = jnp.stack([value] + [swap(value, "wide", inner * step) for step in range(1, outer)])
    near = jnp.stack([far] + [swap(far, "wide", step) for step in range(1, inner)], 1)
    return near.reshape((inner * outer,) + value.shape)


def reorder(value, axis, dim=0):
    return jnp.take(value, lax.axis_index(axis) ^ jnp.arange(lax.axis_size(axis)), axis=dim)


def fetch_blocks(low_master, owners, means, whole_pieces):
    wide = lax.axis_size("wide")
    narrow = lax.axis_size("narrow")
    pieces = lax.all_to_all(low_master.reshape(wide, -1, D), "wide", 0, 0, tiled=True)
    mine = jnp.take(pieces, owners, axis=0)
    count, depth, _ = mine.shape
    joined = join(jnp.concatenate([mine.reshape(-1, D), means.reshape(-1, D)], 0))
    mean_all = joined[:, count * depth :].reshape((wide,) + means.shape).swapaxes(0, 1)
    mean_all = mean_all.reshape(means.shape[0], -1, D)
    if whole_pieces:
        return [joined] + [swap(joined, "narrow", step) for step in range(1, narrow)], mean_all
    rows = joined[:, : count * depth]
    halves = jnp.stack([rows] + [swap(rows, "narrow", step) for step in range(1, narrow)])
    halves = reorder(reorder(halves, "narrow"), "wide", 1).reshape(narrow, wide, count, depth, D)
    return [halves.transpose(2, 0, 1, 3, 4).reshape(count, D, D)], mean_all


def piece_lists(grads, groups):
    if len(grads) > 1:
        return list(grads)
    (blocks,) = grads
    narrow = lax.axis_size("narrow")
    wide = lax.axis_size("wide")
    parts = blocks.reshape(blocks.shape[0], narrow, wide, -1, D).transpose(1, 2, 0, 3, 4)
    parts = reorder(reorder(parts, "narrow"), "wide", 1)
    return [by_group(part.reshape(wide, -1, D)) for part in parts]


def by_group(pieces):
    inner, outer = group_sizes(lax.axis_size("wide"))
    return pieces.reshape((outer, inner) + pieces.shape[1:]).swapaxes(0, 1)


def sum_narrow(lists):
    total = lists[0].astype(F32)
    for step in range(1, len(lists)):
        total += swap(lists[step], "narrow", step).astype(F32)
    return total.astype(BF16)


def sum_group(pieces, stride):
    total = pieces[0].astype(F32)
    for step in range(1, len(pieces)):
        total += swap(pieces[step], "wide", step * stride).astype(F32)
    return total


def sum_near(pieces):
    return sum_group(pieces, 1).astype(BF16)


def sum_far(pieces):
    inner, _ = group_sizes(lax.axis_size("wide"))
    return sum_group(pieces, inner)


def after(value, *others):
    return lax.optimization_barrier((value, *others))[0]


def per_device(
    tokens, cotangent, owner_list, master, moment_one, moment_two, small_params, small_one, small_two
):
    images, count, _ = tokens.shape
    rows = count // ROW
    wide = lax.axis_size("wide")
    small = small_params.reshape(1, -1)
    low_master = master.astype(BF16)
    slots = lax.all_gather(low_master.reshape(-1, D), ("wide", "narrow"), axis=0, tiled=True)
    slots = slots.reshape(-1, D, D)
    narrow = lax.axis_size("narrow")
    inner, outer = group_sizes(wide)
    depth = D // narrow // wide
    groups = (narrow, inner, outer) if depth % 16 == 0 and narrow > 1 else None
    me = lax.axis_index("wide")
    names = owner_list[None, :] == jnp.arange(wide, dtype=jnp.int32)[:, None]
    owned = jnp.any(names, 1)
    block_of = jnp.argmax(names, 1)
    place = jnp.stack([me, lax.axis_index("narrow")]).astype(jnp.int32)
    place, small, owned, block_of, tokens = lax.optimization_barrier((place, small, owned, block_of, tokens))
    normal, scale, means = norm_call(tokens)
    parts, mean_all = fetch_blocks(low_master, owner_list[:3], means, groups is not None)
    queries, keys, values, weights, attended, inverse, sum_k, sum_v = attend_call(
        place, normal, mean_all, small, parts
    )
    block_out, d_branch, d_out, late_small, *grads_late = ff_call(
        owner_list, place, groups, tokens, attended, cotangent, inverse, small, slots
    )

    tie = lax.optimization_barrier
    late, queries = tie((sum_narrow(piece_lists(grads_late, groups)), queries))
    operands = (queries, keys, values, attended, d_out, weights, normal, sum_k, sum_v, mean_all)
    d_joined, d_mean, early_small, *grads_early = back_call(
        owner_list, place, groups, operands, small, slots
    )
    late, early_small, *grads_early = tie((sum_near(late), early_small, *grads_early))
    small_sums = jnp.concatenate([early_small, late_small], 1)
    size = small_sums.shape[1]
    bit = 1
    while bit < narrow:
        small_sums = small_sums + swap(small_sums, "narrow", bit)
        bit *= 2
    d_mean = by_group(d_mean.reshape(images, wide, rows, D).swapaxes(0, 1).reshape(wide, -1, D))
    early = sum_narrow(piece_lists(grads_early, groups))
    early, small_sums, d_joined, late = tie((early, small_sums, d_joined, late))
    late = sum_far(late)
    d_low = low_call(owner_list, d_joined, slots)

    cuts = (3 * depth, 3 * depth + images * rows)
    small_rows = to_rows(small_sums)
    near = jnp.concatenate([early, d_mean], 2).reshape(inner, outer * cuts[1], D)
    near = sum_group([jnp.concatenate([near[step], small_rows], 0) for step in range(inner)], 1)
    near, late, d_low = tie((near, late, d_low))
    small_rows = to_rows(from_rows(near[outer * cuts[1] :], size))
    far = near[: outer * cuts[1]].astype(BF16).reshape(outer, cuts[1], D)
    far = sum_group([jnp.concatenate([far[step], small_rows], 0) for step in range(outer)], inner)
    own_mean = far[cuts[0] : cuts[1]].reshape(images, rows, D)
    small_grad = from_rows(far[cuts[1] :], size).reshape(-1)
    shares = jnp.concatenate([far[: cuts[0]], late], 0).reshape(-1, depth, D).astype(BF16)

    moved = jnp.where(owned[:, None, None], jnp.take(shares, block_of, axis=0), jnp.zeros((), BF16))
    moved = lax.all_to_all(moved, "wide", 0, 0, tiled=True)
    grad_tokens = last_call(normal, scale, d_low, d_branch, own_mean, small)
    moved, grad_tokens = tie((moved, grad_tokens))
    own_grad = moved.reshape(1, -1, D).astype(F32)
    owns_slot = owned[me]
    slot_weight, slot_first, slot_second = adamw_update(
        master, own_grad, moment_one, moment_two, 0.1, RATE
    )
    new_master = jnp.where(owns_slot, slot_weight, master)
    new_one = jnp.where(owns_slot, slot_first, moment_one)
    new_two = jnp.where(owns_slot, slot_second, moment_two)
    small_new, small_one_new, small_two_new = adamw_update(
        small_params, small_grad, small_one, small_two, 0.0, GAIN_RATE
    )
    return (block_out, grad_tokens, new_master, new_one, new_two, small_new, small_one_new, small_two_new)


def solution(mesh):
    split = P("narrow", "wide", None)
    slot = P("wide", "narrow", None)
    return jax.shard_map(
        per_device,
        mesh=mesh,
        in_specs=(split, split, P(), slot, slot, slot, P(), P(), P()),
        out_specs=(split, split, slot, slot, slot, P(), P(), P()),
        check_vma=False,
    )
```

```python
import functools
import functools
import itertools
import math

import jax
import jax.numpy as jnp
from jax import lax
from jax.experimental import pallas as pl
from jax.experimental.pallas import tpu as pltpu
from jax.sharding import PartitionSpec as P

D = 512
HEADS = 8
HD = 64
PAIR = 2 * HD
PAIRS = HEADS // 2
FF = 2048
NF = FF // D
ROW = 192
ROWS_IMG = 64
KEYS = ROW + ROWS_IMG
STEP = 10
RATE = 0.03
GAIN_RATE = 0.4
EPS = 1e-05
LOG2E = math.log2(math.e)
F32 = jnp.float32
BF16 = jnp.bfloat16
MIB = 1024 * 1024


def dot(left, right):
    return jnp.dot(left, right, preferred_element_type=F32)


def dot_nt(left, right):
    return lax.dot_general(left, right, (((1,), (1,)), ((), ())), preferred_element_type=F32)


def normalize(values):
    centred = values - jnp.mean(values, -1, keepdims=True)
    scale = lax.rsqrt(jnp.mean(centred * centred, -1, keepdims=True) + EPS)
    return centred * scale, scale


def head_masks(dtype):
    lane = lax.broadcasted_iota(jnp.int32, (1, PAIR), 1)
    first = (lane < HD).astype(F32)
    return first.astype(dtype), (1.0 - first).astype(dtype)


def tile_spec(*tail, buffers=None):
    zeros = (0,) * len(tail)
    return pl.BlockSpec((1,) + tail, lambda step, *_: (step,) + zeros)


def two_spec(*tail):
    zeros = (0,) * len(tail)
    return pl.BlockSpec((2,) + tail, lambda step, *_: (step,) + zeros)


def whole_spec(shape):
    zeros = (0,) * len(shape)
    return pl.BlockSpec(shape, lambda step, *_: zeros, pipeline_mode=pl.Buffered(1))


def weight_spec(block):
    return pl.BlockSpec(
        (1, D, D), lambda step, owner, *_: (owner[block], 0, 0), pipeline_mode=pl.Buffered(1)
    )


def out_whole(shape):
    zeros = (0,) * len(shape)
    return pl.BlockSpec(shape, lambda step, *_: zeros)


def with_ones(rows):
    return jnp.concatenate([rows, jnp.ones((16, rows.shape[1]), rows.dtype)], 0)


def norm_kernel(x_ref, xh_ref, scale_ref, mean_ref):
    normal, scale_ref[0] = normalize(x_ref[0].astype(F32))
    xh_ref[0] = normal.astype(BF16)
    for row in range(mean_ref.shape[1]):
        part = normal[row * ROW : (row + 1) * ROW]
        mean_ref[0, row : row + 1, :] = jnp.mean(part, 0, keepdims=True).astype(BF16)


def norm_call(tokens):
    images, count, _ = tokens.shape
    rows = count // ROW
    return pl.pallas_call(
        norm_kernel,
        grid=(images,),
        in_specs=[tile_spec(count, D)],
        out_specs=[tile_spec(count, D), tile_spec(count, 1), tile_spec(rows, D)],
        out_shape=[
            jax.ShapeDtypeStruct((images, count, D), BF16),
            jax.ShapeDtypeStruct((images, count, 1), F32),
            jax.ShapeDtypeStruct((images, rows, D), BF16),
        ],
        compiler_params=pltpu.CompilerParams(vmem_limit_bytes=60 * MIB),
        cost_estimate=pl.CostEstimate(
            flops=images * count * D * 10, bytes_accessed=images * count * D * 4, transcendentals=0
        ),
        name="norm_one",
    )(tokens)


def group_sizes(wide):
    inner = min(4, wide)
    return inner, wide // inner


def write_pieces(place, out_refs, read):
    narrow = len(out_refs)
    *lead, height, _ = out_refs[0].shape
    wide = math.prod(lead)
    depth = D // narrow // wide

    def one(number, carry):
        for step, out_ref in enumerate(out_refs):
            device = number if len(lead) == 1 else place[0] ^ number
            start = (place[1] ^ step) * (D // narrow) + device * depth
            here = pl.ds(pl.multiple_of(start, depth), depth)
            index = (number,) if len(lead) == 1 else (number % lead[0], number // lead[0])
            for block in range(height // depth):
                value = read(block, here).astype(BF16)
                out_ref[index + (slice(block * depth, (block + 1) * depth), slice(None))] = value
        return carry

    lax.fori_loop(0, wide, one, 0)


def attend_kernel(
    parts, place, xh_ref, mean_ref, params_ref, *refs
):
    g_ref, s_ref = params_ref.at[:, 0:D], params_ref.at[:, D : 2 * D]
    part_refs, refs = refs[:parts], refs[parts:]
    q_ref, k_ref, v_ref, e_ref, o_ref, li_ref, sk_ref, sv_ref, bias_ref, w_ref = refs
    rows = xh_ref.shape[1] // ROW
    first_row = place[0] * rows

    @pl.when(pl.program_id(0) == 0)
    def _():
        query = lax.broadcasted_iota(jnp.int32, (ROW, KEYS), 0)
        key = lax.broadcasted_iota(jnp.int32, (ROW, KEYS), 1)
        summary = jnp.maximum(key - ROW, 0)
        image_row = (place[0] ^ lax.div(summary, rows)) * rows + lax.rem(summary, rows)
        for row in range(rows):
            own = jnp.where(key <= query, 0.0, -1e30)
            earlier = jnp.where(image_row < first_row + row, math.log2(ROW), -1e30)
            bias_ref[row] = jnp.where(key < ROW, own, earlier)
        if parts == 1:
            w_ref[...] = part_refs[0][...]
            return
        wide, height, _ = part_refs[0].shape
        depth = D // parts // wide

        def one(distance, carry):
            for step, part_ref in enumerate(part_refs):
                start = (place[1] ^ step) * (D // parts) + (place[0] ^ distance) * depth
                here = pl.ds(pl.multiple_of(start, depth), depth)
                for block in range(3):
                    w_ref[block, here, :] = part_ref[distance, block * depth : (block + 1) * depth, :]
            return carry

        lax.fori_loop(0, wide, one, 0)

    a1 = (xh_ref[0].astype(F32) * g_ref[...] + s_ref[...]).astype(BF16)
    q_ref[0] = dot(a1, w_ref[0]).astype(BF16)
    k_ref[0] = dot(a1, w_ref[1]).astype(BF16)
    v_ref[0] = dot(a1, w_ref[2]).astype(BF16)
    mean_a = (mean_ref[0].astype(F32) * g_ref[...] + s_ref[...]).astype(BF16)
    sum_k = dot(mean_a, w_ref[1]).astype(BF16)
    sum_v = dot(mean_a, w_ref[2]).astype(BF16)
    sk_ref[0] = sum_k
    sv_ref[0] = sum_v
    masks = head_masks(BF16)
    ones = [jnp.broadcast_to(mask, (KEYS, PAIR)) for mask in masks]
    scale = LOG2E / math.sqrt(HD)

    for row in range(rows):
        here = slice(row * ROW, (row + 1) * ROW)
        for pair in range(PAIRS):
            lanes = slice(pair * PAIR, (pair + 1) * PAIR)
            query = q_ref[0, here, lanes]
            keys = jnp.concatenate([k_ref[0, here, lanes], sum_k[:, lanes]], 0)
            values = jnp.concatenate([v_ref[0, here, lanes], sum_v[:, lanes]], 0)
            total = None
            for half in range(2):
                score = dot_nt(query, keys * masks[half]) * scale + bias_ref[row]
                weight = jnp.exp2(score - jnp.max(score, -1, keepdims=True)).astype(BF16)
                e_ref[0, row, 2 * pair + half] = weight
                part = dot(weight, jnp.concatenate([values * masks[half], ones[half]], 1))
                total = part if total is None else total + part
            inverse = 1.0 / total[:, PAIR:]
            o_ref[0, here, lanes] = (total[:, :PAIR] * inverse).astype(BF16)
            li_ref[0, here, lanes] = inverse.astype(BF16)


def attend_call(place, normal, mean_all, params, parts):
    images, count, _ = normal.shape
    rows = count // ROW
    tokens_shape = jax.ShapeDtypeStruct((images, count, D), BF16)
    return pl.pallas_call(
        functools.partial(attend_kernel, len(parts)),
        grid_spec=pltpu.PrefetchScalarGridSpec(
            num_scalar_prefetch=1,
            grid=(images,),
            in_specs=[
                tile_spec(count, D), tile_spec(ROWS_IMG, D), whole_spec(params.shape),
            ]
            + [whole_spec(part.shape) for part in parts],
            out_specs=[tile_spec(count, D)] * 3
            + [tile_spec(rows, HEADS, ROW, KEYS)]
            + [tile_spec(count, D)] * 2
            + [tile_spec(ROWS_IMG, D)] * 2,
            scratch_shapes=[
                pltpu.VMEM((rows, ROW, KEYS), F32),
                pltpu.VMEM((3, D, D), BF16),
            ],
        ),
        out_shape=[tokens_shape] * 3
        + [jax.ShapeDtypeStruct((images, rows, HEADS, ROW, KEYS), BF16)]
        + [tokens_shape] * 2
        + [jax.ShapeDtypeStruct((images, ROWS_IMG, D), BF16)] * 2,
        compiler_params=pltpu.CompilerParams(vmem_limit_bytes=60 * MIB),
        cost_estimate=pl.CostEstimate(
            flops=images * count * D * D * 10, bytes_accessed=images * count * D * 20, transcendentals=0
        ),
        name="attend",
    )(place, normal, mean_all, params, *parts)


def ff_kernel(
    pieces, owner, place, x_ref, o_ref, cot_ref, li_ref, params_ref,
    wo_ref, u0_ref, u1_ref, u2_ref, u3_ref, d0_ref, d1_ref, d2_ref, d3_ref,
    out_ref, dr_ref, do_ref, small_ref, *refs
):
    grads_refs, (acc_ref, h_ref, xh_ref, act_ref, dp_ref) = refs[:-5], refs[-5:]
    gg_ref, gs_ref = small_ref.at[:, 0:D], small_ref.at[:, D : 2 * D]
    gbu_ref, gbd_ref = small_ref.at[:, 2 * D : 2 * D + FF], small_ref.at[:, 2 * D + FF :]
    g_ref, s_ref = params_ref.at[:, 2 * D : 3 * D], params_ref.at[:, 3 * D : 4 * D]
    bu_ref, bd_ref = params_ref.at[:, 4 * D : 4 * D + FF], params_ref.at[:, 4 * D + FF :]
    step = pl.program_id(0)
    ups = (u0_ref, u1_ref, u2_ref, u3_ref)
    downs = (d0_ref, d1_ref, d2_ref, d3_ref)

    @pl.when(step == 0)
    def _():
        acc_ref[...] = jnp.zeros_like(acc_ref)
        small_ref[...] = jnp.zeros_like(small_ref)

    hidden = x_ref[0].astype(F32) + dot(o_ref[0], wo_ref[0])
    normal, spread = normalize(hidden)
    xh_ref[...] = normal
    h_ref[...] = hidden + bd_ref[...]
    a2 = (normal * g_ref[...] + s_ref[...]).astype(BF16)
    a2_t = a2.T
    cot = cot_ref[0]
    cot_t = cot.T
    c_one = math.sqrt(2.0 / math.pi)
    c_two = c_one * 0.044715
    width = D // 2
    a2_ones = with_ones(a2_t)

    def first_products(start):
        block, inside = start // D, slice(start % D, start % D + width)
        pre = dot(a2, ups[block][0, :, inside]) + bu_ref[:, start : start + width]
        return pre, dot_nt(cot, downs[block][0, inside, :])

    following = first_products(0)
    for start in range(0, FF, width):
        block, inside, columns = start // D, slice(start % D, start % D + width), slice(start, start + width)
        pre, d_act = following
        if start + width < FF:
            following = first_products(start + width)
        square = pre * pre
        half = 0.5 + 0.5 * jnp.tanh(pre * (c_one + c_two * square))
        act = pre * half
        slope = half + act * (1.0 - half) * (2.0 * c_one + (6.0 * c_two) * square)
        act = act.astype(BF16)
        d_pre = (d_act * slope).astype(BF16)
        act_ref[:, columns] = act
        dp_ref[:, columns] = d_pre
        part = dot(a2_ones, d_pre)
        acc_ref[1 + block, :, inside] += part[:D]
        gbu_ref[:, columns] += part[D : D + 1]
        acc_ref[1 + NF + block, :, inside] += dot(cot_t, act)
    d_a2 = dot_nt(dp_ref[:, 0:D], ups[0][0])
    for block in range(1, NF):
        d_a2 += dot_nt(dp_ref[:, block * D : (block + 1) * D], ups[block][0])
    normal = xh_ref[...]
    gs_ref[...] += jnp.sum(d_a2, 0, keepdims=True)
    gg_ref[...] += jnp.sum(d_a2 * normal, 0, keepdims=True)
    d_normal = d_a2 * g_ref[...]
    middle = jnp.mean(d_normal, -1, keepdims=True)
    along = jnp.mean(d_normal * normal, -1, keepdims=True)
    cot = cot.astype(F32)
    gbd_ref[...] += jnp.sum(cot, 0, keepdims=True)
    d_hidden = cot + spread * (d_normal - middle - normal * along)
    branch = d_hidden.astype(BF16)
    dr_ref[0] = branch
    total = h_ref[...]
    for block, down in enumerate(downs):
        total += dot(act_ref[:, block * D : (block + 1) * D], down[0])
    out_ref[0] = total.astype(BF16)
    acc_ref[0] += dot(o_ref[0].T, branch)
    do_ref[0] = (dot_nt(branch, wo_ref[0]) * li_ref[0].astype(F32)).astype(BF16)

    @pl.when(step == pl.num_programs(0) - 1)
    def _():
        for block in range(1 + NF, 1 + 2 * NF):
            acc_ref[block] = acc_ref[block].T
        if pieces:
            write_pieces(place, grads_refs, lambda block, here: acc_ref[block, here, :])
        else:
            grads_refs[0][...] = acc_ref[...].astype(BF16)


def grad_shapes(groups, blocks, lead):
    if groups is None:
        return [(blocks, D, D)]
    narrow, wide = groups
    return [lead + (blocks * (D // narrow // wide), D)] * narrow


def ff_call(owner, place, groups, tokens, attended, cotangent, inverse, params, slots):
    images, count, _ = tokens.shape
    tokens_shape = jax.ShapeDtypeStruct((images, count, D), BF16)
    blocks = 1 + 2 * NF
    grads = grad_shapes(groups, blocks, groups and groups[1:])
    return pl.pallas_call(
        functools.partial(ff_kernel, groups is not None),
        grid_spec=pltpu.PrefetchScalarGridSpec(
            num_scalar_prefetch=2,
            grid=(images,),
            in_specs=[tile_spec(count, D)] * 4
            + [whole_spec(params.shape)]
            + [weight_spec(3 + block) for block in range(blocks)],
            out_specs=[tile_spec(count, D)] * 3
            + [out_whole((1, 3 * D + FF))]
            + [out_whole(shape) for shape in grads],
            scratch_shapes=[
                pltpu.VMEM((blocks, D, D), F32),
                pltpu.VMEM((count, D), F32),
                pltpu.VMEM((count, D), F32),
                pltpu.VMEM((count, FF), BF16),
                pltpu.VMEM((count, FF), BF16),
            ],
        ),
        out_shape=[tokens_shape] * 3
        + [jax.ShapeDtypeStruct((1, 3 * D + FF), F32)]
        + [jax.ShapeDtypeStruct(shape, BF16) for shape in grads],
        compiler_params=pltpu.CompilerParams(vmem_limit_bytes=60 * MIB),
        cost_estimate=pl.CostEstimate(
            flops=images * count * D * D * 54, bytes_accessed=images * count * D * 14, transcendentals=0
        ),
        name="feed_forward",
    )(owner, place, tokens, attended, cotangent, inverse, params, *([slots] * blocks))


def back_kernel(pieces, owner, place, *refs):
    (q_ref, k_ref, v_ref, o_ref, do_ref, e_ref, xh_ref, sk_ref, sv_ref, mean_ref, params_ref) = refs[:11]
    weights = refs[11:14]
    grad_ref, dm_ref, small_ref, *grads_refs = refs[14:-3]
    acc_ref, dsk_ref, dsv_ref = refs[-3:]
    step = pl.program_id(0)
    rows = q_ref.shape[1] // ROW
    scale = 1.0 / math.sqrt(HD)

    @pl.when(step == 0)
    def _():
        acc_ref[...] = jnp.zeros_like(acc_ref)

    sum_k = sk_ref[0]
    sum_v = sv_ref[0]
    masks = head_masks(BF16)
    blank = jnp.zeros((HD, KEYS), BF16)
    minus = jnp.full((HD, KEYS), -1.0, BF16)
    d_sum_k = jnp.zeros((ROWS_IMG, D), F32)
    d_sum_v = jnp.zeros((ROWS_IMG, D), F32)
    for row in range(rows):
        here = slice(row * ROW, (row + 1) * ROW)
        d_out = do_ref[0, here, :]
        d_out_o = d_out * o_ref[0, here, :]
        q_t = (q_ref[0, here, :] * scale).T
        d_out_t = d_out.T
        v_t = jnp.concatenate([v_ref[0, here, :], sum_v], 0).T
        d_keys = []
        d_values = []
        for pair in range(PAIRS):
            lanes = slice(pair * PAIR, (pair + 1) * PAIR)
            keys = jnp.concatenate([k_ref[0, here, lanes], sum_k[:, lanes]], 0)
            left = jnp.concatenate([d_out[:, lanes], d_out_o[:, lanes]], 1)
            d_query = None
            for half in range(2):
                head = 2 * pair + half
                mine = slice(head * HD, (head + 1) * HD)
                own = v_t[mine]
                right = [own, blank, minus, blank] if half == 0 else [blank, own, blank, minus]
                weight = e_ref[0, row, head]
                d_score = weight * dot(left, jnp.concatenate(right, 0)).astype(BF16)
                d_values.append(dot(d_out_t[mine], weight).astype(BF16))
                d_keys.append(dot(q_t[mine], d_score).astype(BF16))
                part = dot(d_score, keys * masks[half])
                d_query = part if d_query is None else d_query + part
            grad_ref[0, here, lanes] = (d_query * scale).astype(BF16)
        d_key = jnp.concatenate(d_keys, 0).T
        d_value = jnp.concatenate(d_values, 0).T
        grad_ref[0, here, D : 2 * D] = d_key[:ROW]
        grad_ref[0, here, 2 * D :] = d_value[:ROW]
        d_sum_k += d_key[ROW:].astype(F32)
        d_sum_v += d_value[ROW:].astype(F32)
    dsk_ref[step] = d_sum_k.astype(BF16)
    dsv_ref[step] = d_sum_v.astype(BF16)
    acc_ref[...] += dot(with_ones(xh_ref[0].T), grad_ref[0])

    @pl.when(step == pl.num_programs(0) - 1)
    def _():
        mean_t = with_ones(mean_ref[...].reshape(-1, D).T)
        all_k = dsk_ref[...].reshape(-1, D)
        all_v = dsv_ref[...].reshape(-1, D)
        acc_ref[:, D : 2 * D] += dot(mean_t, all_k)
        acc_ref[:, 2 * D :] += dot(mean_t, all_v)
        d_mean = dot_nt(all_k, weights[1][0]) + dot_nt(all_v, weights[2][0])
        dm_ref[...] = d_mean.astype(BF16).reshape(dm_ref.shape)
        gain_grad = jnp.zeros((D, 1), F32)
        shift_grad = jnp.zeros((1, D), F32)
        gain = jnp.broadcast_to(params_ref[:, 0:D], (8, D)).T[:, 0:1]
        shift = jnp.broadcast_to(params_ref[:, D : 2 * D], (8, D)).T[:, 0:1]
        for block, w_ref in enumerate(weights):
            columns = slice(block * D, (block + 1) * D)
            product = acc_ref[0:D, columns]
            sums = acc_ref[D : D + 1, columns]
            gain_grad += jnp.sum(product * w_ref[0].astype(F32), -1, keepdims=True)
            high = sums.astype(BF16)
            parts = jnp.concatenate([high, (sums - high.astype(F32)).astype(BF16)], 0)
            parts = jnp.concatenate([parts, jnp.zeros((14, D), BF16)], 0)
            shift_grad += jnp.sum(dot_nt(parts, w_ref[0]), 0, keepdims=True)
            acc_ref[0:D, columns] = product * gain + shift * sums
        small_ref[:, 0:D] = jnp.broadcast_to(gain_grad, (D, 128)).T[0:1]
        small_ref[:, D:] = shift_grad
        if pieces:
            write_pieces(place, grads_refs, lambda block, here: acc_ref[here, block * D : (block + 1) * D])
        else:
            for block in range(3):
                grads_refs[0][block] = acc_ref[0:D, block * D : (block + 1) * D].astype(BF16)


def back_call(owner, place, groups, operands, params, slots):
    images, count, _ = operands[0].shape
    rows = count // ROW
    grads = grad_shapes(groups, 3, groups and group_sizes(groups[1]))
    return pl.pallas_call(
        functools.partial(back_kernel, groups is not None),
        grid_spec=pltpu.PrefetchScalarGridSpec(
            num_scalar_prefetch=2,
            grid=(images,),
            in_specs=[tile_spec(count, D)] * 5
            + [tile_spec(rows, HEADS, ROW, KEYS), tile_spec(count, D)]
            + [tile_spec(ROWS_IMG, D)] * 2
            + [whole_spec((images, ROWS_IMG, D)), whole_spec(params.shape)]
            + [weight_spec(block) for block in range(3)],
            out_specs=[tile_spec(count, 3 * D), out_whole((images, ROWS_IMG, D)), out_whole((1, 2 * D))]
            + [out_whole(shape) for shape in grads],
            scratch_shapes=[
                pltpu.VMEM((D + 16, 3 * D), F32),
                pltpu.VMEM((images, ROWS_IMG, D), BF16),
                pltpu.VMEM((images, ROWS_IMG, D), BF16),
            ],
        ),
        out_shape=[
            jax.ShapeDtypeStruct((images, count, 3 * D), BF16),
            jax.ShapeDtypeStruct((images, ROWS_IMG, D), BF16),
            jax.ShapeDtypeStruct((1, 2 * D), F32),
        ]
        + [jax.ShapeDtypeStruct(shape, BF16) for shape in grads],
        compiler_params=pltpu.CompilerParams(vmem_limit_bytes=60 * MIB),
        cost_estimate=pl.CostEstimate(
            flops=images * count * D * D * 20, bytes_accessed=images * count * D * 24, transcendentals=0
        ),
        name="attend_back",
    )(owner, place, *operands, params, slots, slots, slots)


def low_kernel(owner, grad_ref, wq_ref, wk_ref, wv_ref, low_ref):
    joined = jnp.concatenate([wq_ref[0], wk_ref[0], wv_ref[0]], 1)
    low_ref[...] = dot_nt(grad_ref[...].reshape(-1, 3 * D), joined).astype(BF16).reshape(low_ref.shape)


def low_call(owner, grads, slots):
    images, count, _ = grads.shape
    return pl.pallas_call(
        low_kernel,
        grid_spec=pltpu.PrefetchScalarGridSpec(
            num_scalar_prefetch=1,
            grid=(images // 2,),
            in_specs=[two_spec(count, 3 * D)] + [weight_spec(block) for block in range(3)],
            out_specs=two_spec(count, D),
        ),
        out_shape=jax.ShapeDtypeStruct((images, count, D), BF16),
        compiler_params=pltpu.CompilerParams(vmem_limit_bytes=60 * MIB),
        cost_estimate=pl.CostEstimate(
            flops=images * count * D * D * 6, bytes_accessed=images * count * D * 8, transcendentals=0
        ),
        name="project_back",
    )(owner, grads, slots, slots, slots)


def last_kernel(xh_ref, scale_ref, low_ref, dr_ref, dm_ref, params_ref, out_ref):
    g_ref = params_ref.at[:, 0:D]
    for image, row in itertools.product(range(2), range(dm_ref.shape[1])):
        here = slice(row * ROW, (row + 1) * ROW)
        normal, spread = xh_ref[image, here, :].astype(F32), scale_ref[image, here, :]
        total = low_ref[image, here, :].astype(F32) + dm_ref[image, row : row + 1, :] * (1.0 / ROW)
        d_normal = total * g_ref[...]
        middle = jnp.mean(d_normal, -1, keepdims=True)
        along = jnp.mean(d_normal * normal, -1, keepdims=True)
        out_ref[image, here, :] = dr_ref[image, here, :].astype(F32) + spread * (d_normal - middle - normal * along)


def last_call(normal, scale, d_low, d_branch, d_mean, params):
    images, count, _ = normal.shape
    return pl.pallas_call(
        last_kernel,
        grid=(images // 2,),
        in_specs=[two_spec(count, D), two_spec(count, 1), two_spec(count, D), two_spec(count, D)]
        + [two_spec(count // ROW, D), whole_spec(params.shape)],
        out_specs=two_spec(count, D),
        out_shape=jax.ShapeDtypeStruct((images, count, D), F32),
        compiler_params=pltpu.CompilerParams(vmem_limit_bytes=60 * MIB),
        cost_estimate=pl.CostEstimate(
            flops=images * count * D * 20, bytes_accessed=images * count * D * 11, transcendentals=0
        ),
        name="norm_one_back",
    )(normal, scale, d_low, d_branch, d_mean, params)


def adamw_update(weight_now, gradient, first_moment, second_moment, decay_rate, step_rate):
    first_new = 0.9 * first_moment + 0.1 * gradient
    second_new = 0.95 * second_moment + 0.05 * gradient * gradient
    direction = first_new / (1.0 - 0.9**STEP) / (jnp.sqrt(second_new / (1.0 - 0.95**STEP)) + 1e-08)
    return (weight_now - step_rate * (direction + decay_rate * weight_now), first_new, second_new)


def swap(value, axis, bit):
    size = lax.axis_size(axis)
    return lax.ppermute(value, axis, [(index, index ^ bit) for index in range(size)])


def to_rows(values):
    high = lax.reduce_precision(values, 8, 7)
    rows = jnp.concatenate([high, values - high], 1).reshape(-1, D).astype(BF16)
    return jnp.pad(rows, ((0, -rows.shape[0] % 16), (0, 0)))


def from_rows(rows, size):
    count = size // D
    return (rows[:count] + rows[count : 2 * count]).reshape(1, size)


def join(value):
    inner, outer = group_sizes(lax.axis_size("wide"))
    far = jnp.stack([value] + [swap(value, "wide", inner * step) for step in range(1, outer)])
    near = jnp.stack([far] + [swap(far, "wide", step) for step in range(1, inner)], 1)
    return near.reshape((inner * outer,) + value.shape)


def reorder(value, axis, dim=0):
    return jnp.take(value, lax.axis_index(axis) ^ jnp.arange(lax.axis_size(axis)), axis=dim)


def fetch_blocks(low_master, owners, means, whole_pieces):
    wide = lax.axis_size("wide")
    narrow = lax.axis_size("narrow")
    pieces = lax.all_to_all(low_master.reshape(wide, -1, D), "wide", 0, 0, tiled=True)
    mine = jnp.take(pieces, owners, axis=0)
    count, depth, _ = mine.shape
    joined = join(jnp.concatenate([mine.reshape(-1, D), means.reshape(-1, D)], 0))
    mean_all = joined[:, count * depth :].reshape((wide,) + means.shape).swapaxes(0, 1)
    mean_all = mean_all.reshape(means.shape[0], -1, D)
    if whole_pieces:
        return [joined] + [swap(joined, "narrow", step) for step in range(1, narrow)], mean_all
    rows = joined[:, : count * depth]
    halves = jnp.stack([rows] + [swap(rows, "narrow", step) for step in range(1, narrow)])
    halves = reorder(reorder(halves, "narrow"), "wide", 1).reshape(narrow, wide, count, depth, D)
    return [halves.transpose(2, 0, 1, 3, 4).reshape(count, D, D)], mean_all


def piece_lists(grads):
    if len(grads) > 1:
        return list(grads)
    (blocks,) = grads
    narrow = lax.axis_size("narrow")
    wide = lax.axis_size("wide")
    parts = blocks.reshape(blocks.shape[0], narrow, wide, -1, D).transpose(1, 2, 0, 3, 4)
    return list(reorder(parts, "narrow").reshape(narrow, wide, -1, D))


def by_group(pieces):
    inner, outer = group_sizes(lax.axis_size("wide"))
    return pieces.reshape((outer, inner) + pieces.shape[1:]).swapaxes(0, 1)


def sum_narrow(lists):
    total = lists[0].astype(F32)
    for step in range(1, len(lists)):
        total += swap(lists[step], "narrow", step).astype(F32)
    return total.astype(BF16)


def sum_group(pieces, stride):
    total = pieces[0].astype(F32)
    for step in range(1, len(pieces)):
        total += swap(pieces[step], "wide", step * stride).astype(F32)
    return total


def per_device(
    tokens, cotangent, owner_list, master, moment_one, moment_two, small_params, small_one, small_two
):
    images, count, _ = tokens.shape
    rows = count // ROW
    wide = lax.axis_size("wide")
    small = small_params.reshape(1, -1)
    low_master = master.astype(BF16)
    slots = lax.all_gather(low_master.reshape(-1, D), ("wide", "narrow"), axis=0, tiled=True)
    slots = slots.reshape(-1, D, D)
    narrow = lax.axis_size("narrow")
    inner, outer = group_sizes(wide)
    depth = D // narrow // wide
    groups = (narrow, wide) if depth % 16 == 0 and narrow > 1 else None
    me = lax.axis_index("wide")
    names = owner_list[None, :] == jnp.arange(wide, dtype=jnp.int32)[:, None]
    owned = jnp.any(names, 1)
    block_of = jnp.argmax(names, 1)
    place = jnp.stack([me, lax.axis_index("narrow")]).astype(jnp.int32)
    place, small, owned, block_of, tokens = lax.optimization_barrier((place, small, owned, block_of, tokens))
    normal, scale, means = norm_call(tokens)
    parts, mean_all = fetch_blocks(low_master, owner_list[:3], means, groups is not None)
    queries, keys, values, weights, attended, inverse, sum_k, sum_v = attend_call(
        place, normal, mean_all, small, parts
    )
    block_out, d_branch, d_out, late_small, *grads_late = ff_call(
        owner_list, place, groups, tokens, attended, cotangent, inverse, small, slots
    )

    tie = lax.optimization_barrier
    late, queries = tie((sum_narrow(piece_lists(grads_late)), queries))
    late = lax.all_to_all(late, "wide", 0, 0, tiled=True)
    operands = (queries, keys, values, attended, d_out, weights, normal, sum_k, sum_v, mean_all)
    d_joined, d_mean, early_small, *grads_early = back_call(
        owner_list, place, groups, operands, small, slots
    )
    late, early_small, *grads_early = tie((late, early_small, *grads_early))
    late = jnp.sum(late.astype(F32), 0)
    small_sums = jnp.concatenate([early_small, late_small], 1)
    size = small_sums.shape[1]
    bit = 1
    while bit < narrow:
        small_sums = small_sums + swap(small_sums, "narrow", bit)
        bit *= 2
    d_mean = by_group(d_mean.reshape(images, wide, rows, D).swapaxes(0, 1).reshape(wide, -1, D))
    early = sum_narrow(piece_lists(grads_early))
    if groups is None:
        early = by_group(reorder(early, "wide"))
    early, small_sums, d_joined = tie((early, small_sums, d_joined))
    d_low = low_call(owner_list, d_joined, slots)

    cuts = (3 * depth, 3 * depth + images * rows)
    small_rows = to_rows(small_sums)
    near = jnp.concatenate([early, d_mean], 2).reshape(inner, outer * cuts[1], D)
    near = sum_group([jnp.concatenate([near[step], small_rows], 0) for step in range(inner)], 1)
    near, late, d_low = tie((near, late, d_low))
    small_rows = to_rows(from_rows(near[outer * cuts[1] :], size))
    far = near[: outer * cuts[1]].astype(BF16).reshape(outer, cuts[1], D)
    far = sum_group([jnp.concatenate([far[step], small_rows], 0) for step in range(outer)], inner)
    own_mean = far[cuts[0] : cuts[1]].reshape(images, rows, D)
    small_grad = from_rows(far[cuts[1] :], size).reshape(-1)
    shares = jnp.concatenate([far[: cuts[0]], late], 0).reshape(-1, depth, D).astype(BF16)

    moved = jnp.where(owned[:, None, None], jnp.take(shares, block_of, axis=0), jnp.zeros((), BF16))
    moved = lax.all_to_all(moved, "wide", 0, 0, tiled=True)
    grad_tokens = last_call(normal, scale, d_low, d_branch, own_mean, small)
    moved, grad_tokens = tie((moved, grad_tokens))
    own_grad = moved.reshape(1, -1, D).astype(F32)
    owns_slot = owned[me]
    slot_weight, slot_first, slot_second = adamw_update(
        master, own_grad, moment_one, moment_two, 0.1, RATE
    )
    new_master = jnp.where(owns_slot, slot_weight, master)
    new_one = jnp.where(owns_slot, slot_first, moment_one)
    new_two = jnp.where(owns_slot, slot_second, moment_two)
    small_new, small_one_new, small_two_new = adamw_update(
        small_params, small_grad, small_one, small_two, 0.0, GAIN_RATE
    )
    return (block_out, grad_tokens, new_master, new_one, new_two, small_new, small_one_new, small_two_new)


def solution(mesh):
    split = P("narrow", "wide", None)
    slot = P("wide", "narrow", None)
    return jax.shard_map(
        per_device,
        mesh=mesh,
        in_specs=(split, split, P(), slot, slot, slot, P(), P(), P()),
        out_specs=(split, split, slot, slot, slot, P(), P(), P()),
        check_vma=False,
    )
```

```python
import functools
import functools
import itertools
import math

import jax
import jax.numpy as jnp
from jax import lax
from jax.experimental import pallas as pl
from jax.experimental.pallas import tpu as pltpu
from jax.sharding import PartitionSpec as P

D = 512
HEADS = 8
HD = 64
PAIR = 2 * HD
PAIRS = HEADS // 2
FF = 2048
NF = FF // D
ROW = 192
ROWS_IMG = 64
KEYS = ROW + ROWS_IMG
STEP = 10
RATE = 0.03
GAIN_RATE = 0.4
EPS = 1e-05
LOG2E = math.log2(math.e)
F32 = jnp.float32
BF16 = jnp.bfloat16
MIB = 1024 * 1024


def dot(left, right):
    return jnp.dot(left, right, preferred_element_type=F32)


def dot_nt(left, right):
    return lax.dot_general(left, right, (((1,), (1,)), ((), ())), preferred_element_type=F32)


def normalize(values):
    centred = values - jnp.mean(values, -1, keepdims=True)
    scale = lax.rsqrt(jnp.mean(centred * centred, -1, keepdims=True) + EPS)
    return centred * scale, scale


def head_masks(dtype):
    lane = lax.broadcasted_iota(jnp.int32, (1, PAIR), 1)
    first = (lane < HD).astype(F32)
    return first.astype(dtype), (1.0 - first).astype(dtype)


def tile_spec(*tail, buffers=None):
    zeros = (0,) * len(tail)
    return pl.BlockSpec((1,) + tail, lambda step, *_: (step,) + zeros)


def two_spec(*tail):
    zeros = (0,) * len(tail)
    return pl.BlockSpec((2,) + tail, lambda step, *_: (step,) + zeros)


def whole_spec(shape):
    zeros = (0,) * len(shape)
    return pl.BlockSpec(shape, lambda step, *_: zeros, pipeline_mode=pl.Buffered(1))


def weight_spec(block):
    return pl.BlockSpec(
        (1, D, D), lambda step, owner, *_: (owner[block], 0, 0), pipeline_mode=pl.Buffered(1)
    )


def out_whole(shape):
    zeros = (0,) * len(shape)
    return pl.BlockSpec(shape, lambda step, *_: zeros)


def with_ones(rows):
    return jnp.concatenate([rows, jnp.ones((16, rows.shape[1]), rows.dtype)], 0)


def norm_kernel(x_ref, xh_ref, scale_ref, mean_ref):
    normal, scale_ref[0] = normalize(x_ref[0].astype(F32))
    xh_ref[0] = normal.astype(BF16)
    for row in range(mean_ref.shape[1]):
        part = normal[row * ROW : (row + 1) * ROW]
        mean_ref[0, row : row + 1, :] = jnp.mean(part, 0, keepdims=True).astype(BF16)


def norm_call(tokens):
    images, count, _ = tokens.shape
    rows = count // ROW
    return pl.pallas_call(
        norm_kernel,
        grid=(images,),
        in_specs=[tile_spec(count, D)],
        out_specs=[tile_spec(count, D), tile_spec(count, 1), tile_spec(rows, D)],
        out_shape=[
            jax.ShapeDtypeStruct((images, count, D), BF16),
            jax.ShapeDtypeStruct((images, count, 1), F32),
            jax.ShapeDtypeStruct((images, rows, D), BF16),
        ],
        compiler_params=pltpu.CompilerParams(vmem_limit_bytes=60 * MIB),
        cost_estimate=pl.CostEstimate(
            flops=images * count * D * 10, bytes_accessed=images * count * D * 4, transcendentals=0
        ),
        name="norm_one",
    )(tokens)


def group_sizes(wide):
    inner = min(4, wide)
    return inner, wide // inner


def write_pieces(place, out_refs, read):
    narrow = len(out_refs)
    *lead, height, _ = out_refs[0].shape
    wide = math.prod(lead)
    depth = D // narrow // wide

    def one(number, carry):
        for step, out_ref in enumerate(out_refs):
            device = number if len(lead) == 1 else place[0] ^ number
            start = (place[1] ^ step) * (D // narrow) + device * depth
            here = pl.ds(pl.multiple_of(start, depth), depth)
            index = (number,) if len(lead) == 1 else (number % lead[0], number // lead[0])
            for block in range(height // depth):
                value = read(block, here).astype(BF16)
                out_ref[index + (slice(block * depth, (block + 1) * depth), slice(None))] = value
        return carry

    lax.fori_loop(0, wide, one, 0)


def attend_kernel(
    parts, place, xh_ref, mean_ref, params_ref, *refs
):
    g_ref, s_ref = params_ref.at[:, 0:D], params_ref.at[:, D : 2 * D]
    part_refs, refs = refs[:parts], refs[parts:]
    q_ref, k_ref, v_ref, e_ref, o_ref, li_ref, sk_ref, sv_ref, bias_ref, w_ref = refs
    rows = xh_ref.shape[1] // ROW
    first_row = place[0] * rows

    @pl.when(pl.program_id(0) == 0)
    def _():
        query = lax.broadcasted_iota(jnp.int32, (ROW, KEYS), 0)
        key = lax.broadcasted_iota(jnp.int32, (ROW, KEYS), 1)
        summary = jnp.maximum(key - ROW, 0)
        image_row = (place[0] ^ lax.div(summary, rows)) * rows + lax.rem(summary, rows)
        for row in range(rows):
            own = jnp.where(key <= query, 0.0, -1e30)
            earlier = jnp.where(image_row < first_row + row, math.log2(ROW), -1e30)
            bias_ref[row] = jnp.where(key < ROW, own, earlier)
        if parts == 1:
            w_ref[...] = part_refs[0][...]
            return
        wide, height, _ = part_refs[0].shape
        depth = D // parts // wide

        def one(distance, carry):
            for step, part_ref in enumerate(part_refs):
                start = (place[1] ^ step) * (D // parts) + (place[0] ^ distance) * depth
                here = pl.ds(pl.multiple_of(start, depth), depth)
                for block in range(3):
                    w_ref[block, here, :] = part_ref[distance, block * depth : (block + 1) * depth, :]
            return carry

        lax.fori_loop(0, wide, one, 0)

    a1 = (xh_ref[0].astype(F32) * g_ref[...] + s_ref[...]).astype(BF16)
    q_ref[0] = dot(a1, w_ref[0]).astype(BF16)
    k_ref[0] = dot(a1, w_ref[1]).astype(BF16)
    v_ref[0] = dot(a1, w_ref[2]).astype(BF16)
    mean_a = (mean_ref[0].astype(F32) * g_ref[...] + s_ref[...]).astype(BF16)
    sum_k = dot(mean_a, w_ref[1]).astype(BF16)
    sum_v = dot(mean_a, w_ref[2]).astype(BF16)
    sk_ref[0] = sum_k
    sv_ref[0] = sum_v
    masks = head_masks(BF16)
    ones = [jnp.broadcast_to(mask, (KEYS, PAIR)) for mask in masks]
    scale = LOG2E / math.sqrt(HD)

    for row in range(rows):
        here = slice(row * ROW, (row + 1) * ROW)
        for pair in range(PAIRS):
            lanes = slice(pair * PAIR, (pair + 1) * PAIR)
            query = q_ref[0, here, lanes]
            keys = jnp.concatenate([k_ref[0, here, lanes], sum_k[:, lanes]], 0)
            values = jnp.concatenate([v_ref[0, here, lanes], sum_v[:, lanes]], 0)
            total = None
            for half in range(2):
                score = dot_nt(query, keys * masks[half]) * scale + bias_ref[row]
                weight = jnp.exp2(score - jnp.max(score, -1, keepdims=True)).astype(BF16)
                e_ref[0, row, 2 * pair + half] = weight
                part = dot(weight, jnp.concatenate([values * masks[half], ones[half]], 1))
                total = part if total is None else total + part
            inverse = 1.0 / total[:, PAIR:]
            o_ref[0, here, lanes] = (total[:, :PAIR] * inverse).astype(BF16)
            li_ref[0, here, lanes] = inverse.astype(BF16)


def attend_call(place, normal, mean_all, params, parts):
    images, count, _ = normal.shape
    rows = count // ROW
    tokens_shape = jax.ShapeDtypeStruct((images, count, D), BF16)
    return pl.pallas_call(
        functools.partial(attend_kernel, len(parts)),
        grid_spec=pltpu.PrefetchScalarGridSpec(
            num_scalar_prefetch=1,
            grid=(images,),
            in_specs=[
                tile_spec(count, D), tile_spec(ROWS_IMG, D), whole_spec(params.shape),
            ]
            + [whole_spec(part.shape) for part in parts],
            out_specs=[tile_spec(count, D)] * 3
            + [tile_spec(rows, HEADS, ROW, KEYS)]
            + [tile_spec(count, D)] * 2
            + [tile_spec(ROWS_IMG, D)] * 2,
            scratch_shapes=[
                pltpu.VMEM((rows, ROW, KEYS), F32),
                pltpu.VMEM((3, D, D), BF16),
            ],
        ),
        out_shape=[tokens_shape] * 3
        + [jax.ShapeDtypeStruct((images, rows, HEADS, ROW, KEYS), BF16)]
        + [tokens_shape] * 2
        + [jax.ShapeDtypeStruct((images, ROWS_IMG, D), BF16)] * 2,
        compiler_params=pltpu.CompilerParams(vmem_limit_bytes=60 * MIB),
        cost_estimate=pl.CostEstimate(
            flops=images * count * D * D * 10, bytes_accessed=images * count * D * 20, transcendentals=0
        ),
        name="attend",
    )(place, normal, mean_all, params, *parts)


def ff_kernel(
    pieces, owner, place, x_ref, o_ref, cot_ref, li_ref, params_ref,
    wo_ref, u0_ref, u1_ref, u2_ref, u3_ref, d0_ref, d1_ref, d2_ref, d3_ref,
    out_ref, dr_ref, do_ref, small_ref, *refs
):
    grads_refs, (acc_ref, h_ref, xh_ref, act_ref, dp_ref) = refs[:-5], refs[-5:]
    gg_ref, gs_ref = small_ref.at[:, 0:D], small_ref.at[:, D : 2 * D]
    gbu_ref, gbd_ref = small_ref.at[:, 2 * D : 2 * D + FF], small_ref.at[:, 2 * D + FF :]
    g_ref, s_ref = params_ref.at[:, 2 * D : 3 * D], params_ref.at[:, 3 * D : 4 * D]
    bu_ref, bd_ref = params_ref.at[:, 4 * D : 4 * D + FF], params_ref.at[:, 4 * D + FF :]
    step = pl.program_id(0)
    ups = (u0_ref, u1_ref, u2_ref, u3_ref)
    downs = (d0_ref, d1_ref, d2_ref, d3_ref)

    @pl.when(step == 0)
    def _():
        acc_ref[...] = jnp.zeros_like(acc_ref)
        small_ref[...] = jnp.zeros_like(small_ref)

    hidden = x_ref[0].astype(F32) + dot(o_ref[0], wo_ref[0])
    normal, spread = normalize(hidden)
    xh_ref[...] = normal
    h_ref[...] = hidden + bd_ref[...]
    a2 = (normal * g_ref[...] + s_ref[...]).astype(BF16)
    a2_t = a2.T
    cot = cot_ref[0]
    cot_t = cot.T
    c_one = math.sqrt(2.0 / math.pi)
    c_two = c_one * 0.044715
    width = D // 2
    a2_ones = with_ones(a2_t)

    def first_products(start):
        block, inside = start // D, slice(start % D, start % D + width)
        pre = dot(a2, ups[block][0, :, inside]) + bu_ref[:, start : start + width]
        return pre, dot_nt(cot, downs[block][0, inside, :])

    following = first_products(0)
    for start in range(0, FF, width):
        block, inside, columns = start // D, slice(start % D, start % D + width), slice(start, start + width)
        pre, d_act = following
        if start + width < FF:
            following = first_products(start + width)
        square = pre * pre
        half = 0.5 + 0.5 * jnp.tanh(pre * (c_one + c_two * square))
        act = (pre * half).astype(BF16)
        rest = (1.0 - half).astype(BF16)
        half = half.astype(BF16)
        slope = half + act * rest * (2.0 * c_one + (6.0 * c_two) * square.astype(BF16))
        d_pre = d_act.astype(BF16) * slope
        act_ref[:, columns] = act
        dp_ref[:, columns] = d_pre
        part = dot(a2_ones, d_pre)
        acc_ref[1 + block, :, inside] += part[:D]
        gbu_ref[:, columns] += part[D : D + 1]
        acc_ref[1 + NF + block, :, inside] += dot(cot_t, act)
    d_a2 = dot_nt(dp_ref[:, 0:D], ups[0][0])
    for block in range(1, NF):
        d_a2 += dot_nt(dp_ref[:, block * D : (block + 1) * D], ups[block][0])
    normal = xh_ref[...]
    gs_ref[...] += jnp.sum(d_a2, 0, keepdims=True)
    gg_ref[...] += jnp.sum(d_a2 * normal, 0, keepdims=True)
    d_normal = d_a2 * g_ref[...]
    middle = jnp.mean(d_normal, -1, keepdims=True)
    along = jnp.mean(d_normal * normal, -1, keepdims=True)
    cot = cot.astype(F32)
    gbd_ref[...] += jnp.sum(cot, 0, keepdims=True)
    d_hidden = cot + spread * (d_normal - middle - normal * along)
    branch = d_hidden.astype(BF16)
    dr_ref[0] = branch
    total = h_ref[...]
    for block, down in enumerate(downs):
        total += dot(act_ref[:, block * D : (block + 1) * D], down[0])
    out_ref[0] = total.astype(BF16)
    acc_ref[0] += dot(o_ref[0].T, branch)
    do_ref[0] = (dot_nt(branch, wo_ref[0]) * li_ref[0].astype(F32)).astype(BF16)

    @pl.when(step == pl.num_programs(0) - 1)
    def _():
        for block in range(1 + NF, 1 + 2 * NF):
            acc_ref[block] = acc_ref[block].T
        if pieces:
            write_pieces(place, grads_refs, lambda block, here: acc_ref[block, here, :])
        else:
            grads_refs[0][...] = acc_ref[...].astype(BF16)


def grad_shapes(groups, blocks, lead):
    if groups is None:
        return [(blocks, D, D)]
    narrow, wide = groups
    return [lead + (blocks * (D // narrow // wide), D)] * narrow


def ff_call(owner, place, groups, tokens, attended, cotangent, inverse, params, slots):
    images, count, _ = tokens.shape
    tokens_shape = jax.ShapeDtypeStruct((images, count, D), BF16)
    blocks = 1 + 2 * NF
    grads = grad_shapes(groups, blocks, groups and groups[1:])
    return pl.pallas_call(
        functools.partial(ff_kernel, groups is not None),
        grid_spec=pltpu.PrefetchScalarGridSpec(
            num_scalar_prefetch=2,
            grid=(images,),
            in_specs=[tile_spec(count, D)] * 4
            + [whole_spec(params.shape)]
            + [weight_spec(3 + block) for block in range(blocks)],
            out_specs=[tile_spec(count, D)] * 3
            + [out_whole((1, 3 * D + FF))]
            + [out_whole(shape) for shape in grads],
            scratch_shapes=[
                pltpu.VMEM((blocks, D, D), F32),
                pltpu.VMEM((count, D), F32),
                pltpu.VMEM((count, D), F32),
                pltpu.VMEM((count, FF), BF16),
                pltpu.VMEM((count, FF), BF16),
            ],
        ),
        out_shape=[tokens_shape] * 3
        + [jax.ShapeDtypeStruct((1, 3 * D + FF), F32)]
        + [jax.ShapeDtypeStruct(shape, BF16) for shape in grads],
        compiler_params=pltpu.CompilerParams(vmem_limit_bytes=60 * MIB),
        cost_estimate=pl.CostEstimate(
            flops=images * count * D * D * 54, bytes_accessed=images * count * D * 14, transcendentals=0
        ),
        name="feed_forward",
    )(owner, place, tokens, attended, cotangent, inverse, params, *([slots] * blocks))


def back_kernel(pieces, owner, place, *refs):
    (q_ref, k_ref, v_ref, o_ref, do_ref, e_ref, xh_ref, sk_ref, sv_ref, mean_ref, params_ref) = refs[:11]
    weights = refs[11:14]
    grad_ref, dm_ref, small_ref, *grads_refs = refs[14:-3]
    acc_ref, dsk_ref, dsv_ref = refs[-3:]
    step = pl.program_id(0)
    rows = q_ref.shape[1] // ROW
    scale = 1.0 / math.sqrt(HD)

    @pl.when(step == 0)
    def _():
        acc_ref[...] = jnp.zeros_like(acc_ref)

    sum_k = sk_ref[0]
    sum_v = sv_ref[0]
    masks = head_masks(BF16)
    blank = jnp.zeros((HD, KEYS), BF16)
    minus = jnp.full((HD, KEYS), -1.0, BF16)
    d_sum_k = jnp.zeros((ROWS_IMG, D), F32)
    d_sum_v = jnp.zeros((ROWS_IMG, D), F32)
    for row in range(rows):
        here = slice(row * ROW, (row + 1) * ROW)
        d_out = do_ref[0, here, :]
        d_out_o = d_out * o_ref[0, here, :]
        q_t = (q_ref[0, here, :] * scale).T
        d_out_t = d_out.T
        v_t = jnp.concatenate([v_ref[0, here, :], sum_v], 0).T
        d_keys = []
        d_values = []
        for pair in range(PAIRS):
            lanes = slice(pair * PAIR, (pair + 1) * PAIR)
            keys = jnp.concatenate([k_ref[0, here, lanes], sum_k[:, lanes]], 0)
            left = jnp.concatenate([d_out[:, lanes], d_out_o[:, lanes]], 1)
            d_query = None
            for half in range(2):
                head = 2 * pair + half
                mine = slice(head * HD, (head + 1) * HD)
                own = v_t[mine]
                right = [own, blank, minus, blank] if half == 0 else [blank, own, blank, minus]
                weight = e_ref[0, row, head]
                d_score = weight * dot(left, jnp.concatenate(right, 0)).astype(BF16)
                d_values.append(dot(d_out_t[mine], weight).astype(BF16))
                d_keys.append(dot(q_t[mine], d_score).astype(BF16))
                part = dot(d_score, keys * masks[half])
                d_query = part if d_query is None else d_query + part
            grad_ref[0, here, lanes] = (d_query * scale).astype(BF16)
        d_key = jnp.concatenate(d_keys, 0).T
        d_value = jnp.concatenate(d_values, 0).T
        grad_ref[0, here, D : 2 * D] = d_key[:ROW]
        grad_ref[0, here, 2 * D :] = d_value[:ROW]
        d_sum_k += d_key[ROW:].astype(F32)
        d_sum_v += d_value[ROW:].astype(F32)
    dsk_ref[step] = d_sum_k.astype(BF16)
    dsv_ref[step] = d_sum_v.astype(BF16)
    acc_ref[...] += dot(with_ones(xh_ref[0].T), grad_ref[0])

    @pl.when(step == pl.num_programs(0) - 1)
    def _():
        mean_t = with_ones(mean_ref[...].reshape(-1, D).T)
        all_k = dsk_ref[...].reshape(-1, D)
        all_v = dsv_ref[...].reshape(-1, D)
        acc_ref[:, D : 2 * D] += dot(mean_t, all_k)
        acc_ref[:, 2 * D :] += dot(mean_t, all_v)
        d_mean = dot_nt(all_k, weights[1][0]) + dot_nt(all_v, weights[2][0])
        dm_ref[...] = d_mean.astype(BF16).reshape(dm_ref.shape)
        gain_grad = jnp.zeros((D, 1), F32)
        shift_grad = jnp.zeros((1, D), F32)
        gain = jnp.broadcast_to(params_ref[:, 0:D], (8, D)).T[:, 0:1]
        shift = jnp.broadcast_to(params_ref[:, D : 2 * D], (8, D)).T[:, 0:1]
        for block, w_ref in enumerate(weights):
            columns = slice(block * D, (block + 1) * D)
            product = acc_ref[0:D, columns]
            sums = acc_ref[D : D + 1, columns]
            gain_grad += jnp.sum(product * w_ref[0].astype(F32), -1, keepdims=True)
            high = sums.astype(BF16)
            parts = jnp.concatenate([high, (sums - high.astype(F32)).astype(BF16)], 0)
            parts = jnp.concatenate([parts, jnp.zeros((14, D), BF16)], 0)
            shift_grad += jnp.sum(dot_nt(parts, w_ref[0]), 0, keepdims=True)
            acc_ref[0:D, columns] = product * gain + shift * sums
        small_ref[:, 0:D] = jnp.broadcast_to(gain_grad, (D, 128)).T[0:1]
        small_ref[:, D:] = shift_grad
        if pieces:
            write_pieces(place, grads_refs, lambda block, here: acc_ref[here, block * D : (block + 1) * D])
        else:
            for block in range(3):
                grads_refs[0][block] = acc_ref[0:D, block * D : (block + 1) * D].astype(BF16)


def back_call(owner, place, groups, operands, params, slots):
    images, count, _ = operands[0].shape
    rows = count // ROW
    grads = grad_shapes(groups, 3, groups and group_sizes(groups[1]))
    return pl.pallas_call(
        functools.partial(back_kernel, groups is not None),
        grid_spec=pltpu.PrefetchScalarGridSpec(
            num_scalar_prefetch=2,
            grid=(images,),
            in_specs=[tile_spec(count, D)] * 5
            + [tile_spec(rows, HEADS, ROW, KEYS), tile_spec(count, D)]
            + [tile_spec(ROWS_IMG, D)] * 2
            + [whole_spec((images, ROWS_IMG, D)), whole_spec(params.shape)]
            + [weight_spec(block) for block in range(3)],
            out_specs=[tile_spec(count, 3 * D), out_whole((images, ROWS_IMG, D)), out_whole((1, 2 * D))]
            + [out_whole(shape) for shape in grads],
            scratch_shapes=[
                pltpu.VMEM((D + 16, 3 * D), F32),
                pltpu.VMEM((images, ROWS_IMG, D), BF16),
                pltpu.VMEM((images, ROWS_IMG, D), BF16),
            ],
        ),
        out_shape=[
            jax.ShapeDtypeStruct((images, count, 3 * D), BF16),
            jax.ShapeDtypeStruct((images, ROWS_IMG, D), BF16),
            jax.ShapeDtypeStruct((1, 2 * D), F32),
        ]
        + [jax.ShapeDtypeStruct(shape, BF16) for shape in grads],
        compiler_params=pltpu.CompilerParams(vmem_limit_bytes=60 * MIB),
        cost_estimate=pl.CostEstimate(
            flops=images * count * D * D * 20, bytes_accessed=images * count * D * 24, transcendentals=0
        ),
        name="attend_back",
    )(owner, place, *operands, params, slots, slots, slots)


def low_kernel(owner, grad_ref, wq_ref, wk_ref, wv_ref, low_ref):
    joined = jnp.concatenate([wq_ref[0], wk_ref[0], wv_ref[0]], 1)
    low_ref[...] = dot_nt(grad_ref[...].reshape(-1, 3 * D), joined).astype(BF16).reshape(low_ref.shape)


def low_call(owner, grads, slots):
    images, count, _ = grads.shape
    return pl.pallas_call(
        low_kernel,
        grid_spec=pltpu.PrefetchScalarGridSpec(
            num_scalar_prefetch=1,
            grid=(images // 2,),
            in_specs=[two_spec(count, 3 * D)] + [weight_spec(block) for block in range(3)],
            out_specs=two_spec(count, D),
        ),
        out_shape=jax.ShapeDtypeStruct((images, count, D), BF16),
        compiler_params=pltpu.CompilerParams(vmem_limit_bytes=60 * MIB),
        cost_estimate=pl.CostEstimate(
            flops=images * count * D * D * 6, bytes_accessed=images * count * D * 8, transcendentals=0
        ),
        name="project_back",
    )(owner, grads, slots, slots, slots)


def last_kernel(xh_ref, scale_ref, low_ref, dr_ref, dm_ref, params_ref, out_ref):
    g_ref = params_ref.at[:, 0:D]
    for image, row in itertools.product(range(2), range(dm_ref.shape[1])):
        here = slice(row * ROW, (row + 1) * ROW)
        normal, spread = xh_ref[image, here, :].astype(F32), scale_ref[image, here, :]
        total = low_ref[image, here, :].astype(F32) + dm_ref[image, row : row + 1, :] * (1.0 / ROW)
        d_normal = total * g_ref[...]
        middle = jnp.mean(d_normal, -1, keepdims=True)
        along = jnp.mean(d_normal * normal, -1, keepdims=True)
        out_ref[image, here, :] = dr_ref[image, here, :].astype(F32) + spread * (d_normal - middle - normal * along)


def last_call(normal, scale, d_low, d_branch, d_mean, params):
    images, count, _ = normal.shape
    return pl.pallas_call(
        last_kernel,
        grid=(images // 2,),
        in_specs=[two_spec(count, D), two_spec(count, 1), two_spec(count, D), two_spec(count, D)]
        + [two_spec(count // ROW, D), whole_spec(params.shape)],
        out_specs=two_spec(count, D),
        out_shape=jax.ShapeDtypeStruct((images, count, D), F32),
        compiler_params=pltpu.CompilerParams(vmem_limit_bytes=60 * MIB),
        cost_estimate=pl.CostEstimate(
            flops=images * count * D * 20, bytes_accessed=images * count * D * 11, transcendentals=0
        ),
        name="norm_one_back",
    )(normal, scale, d_low, d_branch, d_mean, params)


def adamw_update(weight_now, gradient, first_moment, second_moment, decay_rate, step_rate):
    first_new = 0.9 * first_moment + 0.1 * gradient
    second_new = 0.95 * second_moment + 0.05 * gradient * gradient
    direction = first_new / (1.0 - 0.9**STEP) / (jnp.sqrt(second_new / (1.0 - 0.95**STEP)) + 1e-08)
    return (weight_now - step_rate * (direction + decay_rate * weight_now), first_new, second_new)


def swap(value, axis, bit):
    size = lax.axis_size(axis)
    return lax.ppermute(value, axis, [(index, index ^ bit) for index in range(size)])


def to_rows(values):
    high = lax.reduce_precision(values, 8, 7)
    rows = jnp.concatenate([high, values - high], 1).reshape(-1, D).astype(BF16)
    return jnp.pad(rows, ((0, -rows.shape[0] % 16), (0, 0)))


def from_rows(rows, size):
    count = size // D
    return (rows[:count] + rows[count : 2 * count]).reshape(1, size)


def join(value):
    inner, outer = group_sizes(lax.axis_size("wide"))
    far = jnp.stack([value] + [swap(value, "wide", inner * step) for step in range(1, outer)])
    near = jnp.stack([far] + [swap(far, "wide", step) for step in range(1, inner)], 1)
    return near.reshape((inner * outer,) + value.shape)


def reorder(value, axis, dim=0):
    return jnp.take(value, lax.axis_index(axis) ^ jnp.arange(lax.axis_size(axis)), axis=dim)


def fetch_blocks(low_master, owners, means, whole_pieces):
    wide = lax.axis_size("wide")
    narrow = lax.axis_size("narrow")
    pieces = lax.all_to_all(low_master.reshape(wide, -1, D), "wide", 0, 0, tiled=True)
    mine = jnp.take(pieces, owners, axis=0)
    count, depth, _ = mine.shape
    joined = join(jnp.concatenate([mine.reshape(-1, D), means.reshape(-1, D)], 0))
    mean_all = joined[:, count * depth :].reshape((wide,) + means.shape).swapaxes(0, 1)
    mean_all = mean_all.reshape(means.shape[0], -1, D)
    if whole_pieces:
        return [joined] + [swap(joined, "narrow", step) for step in range(1, narrow)], mean_all
    rows = joined[:, : count * depth]
    halves = jnp.stack([rows] + [swap(rows, "narrow", step) for step in range(1, narrow)])
    halves = reorder(reorder(halves, "narrow"), "wide", 1).reshape(narrow, wide, count, depth, D)
    return [halves.transpose(2, 0, 1, 3, 4).reshape(count, D, D)], mean_all


def piece_lists(grads):
    if len(grads) > 1:
        return list(grads)
    (blocks,) = grads
    narrow = lax.axis_size("narrow")
    wide = lax.axis_size("wide")
    parts = blocks.reshape(blocks.shape[0], narrow, wide, -1, D).transpose(1, 2, 0, 3, 4)
    return list(reorder(parts, "narrow").reshape(narrow, wide, -1, D))


def by_group(pieces):
    inner, outer = group_sizes(lax.axis_size("wide"))
    return pieces.reshape((outer, inner) + pieces.shape[1:]).swapaxes(0, 1)


def sum_narrow(lists):
    total = lists[0].astype(F32)
    for step in range(1, len(lists)):
        total += swap(lists[step], "narrow", step).astype(F32)
    return total.astype(BF16)


def sum_group(pieces, stride):
    total = pieces[0].astype(F32)
    for step in range(1, len(pieces)):
        total += swap(pieces[step], "wide", step * stride).astype(F32)
    return total


def per_device(
    tokens, cotangent, owner_list, master, moment_one, moment_two, small_params, small_one, small_two
):
    images, count, _ = tokens.shape
    rows = count // ROW
    wide = lax.axis_size("wide")
    small = small_params.reshape(1, -1)
    low_master = master.astype(BF16)
    slots = lax.all_gather(low_master.reshape(-1, D), ("wide", "narrow"), axis=0, tiled=True)
    slots = slots.reshape(-1, D, D)
    narrow = lax.axis_size("narrow")
    inner, outer = group_sizes(wide)
    depth = D // narrow // wide
    groups = (narrow, wide) if depth % 16 == 0 and narrow > 1 else None
    me = lax.axis_index("wide")
    names = owner_list[None, :] == jnp.arange(wide, dtype=jnp.int32)[:, None]
    owned = jnp.any(names, 1)
    block_of = jnp.argmax(names, 1)
    place = jnp.stack([me, lax.axis_index("narrow")]).astype(jnp.int32)
    place, small, owned, block_of, tokens = lax.optimization_barrier((place, small, owned, block_of, tokens))
    normal, scale, means = norm_call(tokens)
    parts, mean_all = fetch_blocks(low_master, owner_list[:3], means, groups is not None)
    queries, keys, values, weights, attended, inverse, sum_k, sum_v = attend_call(
        place, normal, mean_all, small, parts
    )
    block_out, d_branch, d_out, late_small, *grads_late = ff_call(
        owner_list, place, groups, tokens, attended, cotangent, inverse, small, slots
    )

    tie = lax.optimization_barrier
    late, queries = tie((sum_narrow(piece_lists(grads_late)), queries))
    late = lax.all_to_all(late, "wide", 0, 0, tiled=True)
    operands = (queries, keys, values, attended, d_out, weights, normal, sum_k, sum_v, mean_all)
    d_joined, d_mean, early_small, *grads_early = back_call(
        owner_list, place, groups, operands, small, slots
    )
    late, early_small, *grads_early = tie((late, early_small, *grads_early))
    late = jnp.sum(late.astype(F32), 0)
    small_sums = jnp.concatenate([early_small, late_small], 1)
    size = small_sums.shape[1]
    bit = 1
    while bit < narrow:
        small_sums = small_sums + swap(small_sums, "narrow", bit)
        bit *= 2
    d_mean = by_group(d_mean.reshape(images, wide, rows, D).swapaxes(0, 1).reshape(wide, -1, D))
    early = sum_narrow(piece_lists(grads_early))
    if groups is None:
        early = by_group(reorder(early, "wide"))
    early, small_sums, d_joined = tie((early, small_sums, d_joined))
    d_low = low_call(owner_list, d_joined, slots)

    cuts = (3 * depth, 3 * depth + images * rows)
    small_rows = to_rows(small_sums)
    near = jnp.concatenate([early, d_mean], 2).reshape(inner, outer * cuts[1], D)
    near = sum_group([jnp.concatenate([near[step], small_rows], 0) for step in range(inner)], 1)
    near, late, d_low = tie((near, late, d_low))
    small_rows = to_rows(from_rows(near[outer * cuts[1] :], size))
    far = near[: outer * cuts[1]].astype(BF16).reshape(outer, cuts[1], D)
    far = sum_group([jnp.concatenate([far[step], small_rows], 0) for step in range(outer)], inner)
    own_mean = far[cuts[0] : cuts[1]].reshape(images, rows, D)
    small_grad = from_rows(far[cuts[1] :], size).reshape(-1)
    shares = jnp.concatenate([far[: cuts[0]], late], 0).reshape(-1, depth, D).astype(BF16)

    moved = jnp.where(owned[:, None, None], jnp.take(shares, block_of, axis=0), jnp.zeros((), BF16))
    moved = lax.all_to_all(moved, "wide", 0, 0, tiled=True)
    grad_tokens = last_call(normal, scale, d_low, d_branch, own_mean, small)
    moved, grad_tokens = tie((moved, grad_tokens))
    own_grad = moved.reshape(1, -1, D).astype(F32)
    owns_slot = owned[me]
    slot_weight, slot_first, slot_second = adamw_update(
        master, own_grad, moment_one, moment_two, 0.1, RATE
    )
    new_master = jnp.where(owns_slot, slot_weight, master)
    new_one = jnp.where(owns_slot, slot_first, moment_one)
    new_two = jnp.where(owns_slot, slot_second, moment_two)
    small_new, small_one_new, small_two_new = adamw_update(
        small_params, small_grad, small_one, small_two, 0.0, GAIN_RATE
    )
    return (block_out, grad_tokens, new_master, new_one, new_two, small_new, small_one_new, small_two_new)


def solution(mesh):
    split = P("narrow", "wide", None)
    slot = P("wide", "narrow", None)
    return jax.shard_map(
        per_device,
        mesh=mesh,
        in_specs=(split, split, P(), slot, slot, slot, P(), P(), P()),
        out_specs=(split, split, slot, slot, slot, P(), P(), P()),
        check_vma=False,
    )
```

```python
import functools
import functools
import itertools
import math

import jax
import jax.numpy as jnp
from jax import lax
from jax.experimental import pallas as pl
from jax.experimental.pallas import tpu as pltpu
from jax.sharding import PartitionSpec as P

D = 512
HEADS = 8
HD = 64
PAIR = 2 * HD
PAIRS = HEADS // 2
FF = 2048
NF = FF // D
ROW = 192
ROWS_IMG = 64
KEYS = ROW + ROWS_IMG
STEP = 10
RATE = 0.03
GAIN_RATE = 0.4
EPS = 1e-05
LOG2E = math.log2(math.e)
F32 = jnp.float32
BF16 = jnp.bfloat16
MIB = 1024 * 1024


def dot(left, right):
    return jnp.dot(left, right, preferred_element_type=F32)


def dot_nt(left, right):
    return lax.dot_general(left, right, (((1,), (1,)), ((), ())), preferred_element_type=F32)


def normalize(values):
    centred = values - jnp.mean(values, -1, keepdims=True)
    scale = lax.rsqrt(jnp.mean(centred * centred, -1, keepdims=True) + EPS)
    return centred * scale, scale


def head_masks(dtype):
    lane = lax.broadcasted_iota(jnp.int32, (1, PAIR), 1)
    first = (lane < HD).astype(F32)
    return first.astype(dtype), (1.0 - first).astype(dtype)


def tile_spec(*tail, buffers=None):
    zeros = (0,) * len(tail)
    return pl.BlockSpec((1,) + tail, lambda step, *_: (step,) + zeros)


def two_spec(*tail):
    zeros = (0,) * len(tail)
    return pl.BlockSpec((2,) + tail, lambda step, *_: (step,) + zeros)


def whole_spec(shape):
    zeros = (0,) * len(shape)
    return pl.BlockSpec(shape, lambda step, *_: zeros, pipeline_mode=pl.Buffered(1))


def weight_spec(block):
    return pl.BlockSpec(
        (1, D, D), lambda step, owner, *_: (owner[block], 0, 0), pipeline_mode=pl.Buffered(1)
    )


def out_whole(shape):
    zeros = (0,) * len(shape)
    return pl.BlockSpec(shape, lambda step, *_: zeros)


def with_ones(rows):
    return jnp.concatenate([rows, jnp.ones((16, rows.shape[1]), rows.dtype)], 0)


def norm_kernel(x_ref, xh_ref, scale_ref, mean_ref):
    normal, scale_ref[0] = normalize(x_ref[0].astype(F32))
    xh_ref[0] = normal.astype(BF16)
    for row in range(mean_ref.shape[1]):
        part = normal[row * ROW : (row + 1) * ROW]
        mean_ref[0, row : row + 1, :] = jnp.mean(part, 0, keepdims=True).astype(BF16)


def norm_call(tokens):
    images, count, _ = tokens.shape
    rows = count // ROW
    return pl.pallas_call(
        norm_kernel,
        grid=(images,),
        in_specs=[tile_spec(count, D)],
        out_specs=[tile_spec(count, D), tile_spec(count, 1), tile_spec(rows, D)],
        out_shape=[
            jax.ShapeDtypeStruct((images, count, D), BF16),
            jax.ShapeDtypeStruct((images, count, 1), F32),
            jax.ShapeDtypeStruct((images, rows, D), BF16),
        ],
        compiler_params=pltpu.CompilerParams(vmem_limit_bytes=60 * MIB),
        cost_estimate=pl.CostEstimate(
            flops=images * count * D * 10, bytes_accessed=images * count * D * 4, transcendentals=0
        ),
        name="norm_one",
    )(tokens)


def group_sizes(wide):
    inner = min(4, wide)
    return inner, wide // inner


def write_pieces(place, out_refs, read):
    narrow = len(out_refs)
    *lead, height, _ = out_refs[0].shape
    wide = math.prod(lead)
    depth = D // narrow // wide

    def one(number, carry):
        for step, out_ref in enumerate(out_refs):
            device = number if len(lead) == 1 else place[0] ^ number
            start = (place[1] ^ step) * (D // narrow) + device * depth
            here = pl.ds(pl.multiple_of(start, depth), depth)
            index = (number,) if len(lead) == 1 else (number % lead[0], number // lead[0])
            for block in range(height // depth):
                value = read(block, here).astype(BF16)
                out_ref[index + (slice(block * depth, (block + 1) * depth), slice(None))] = value
        return carry

    lax.fori_loop(0, wide, one, 0)


def attend_kernel(
    parts, place, xh_ref, mean_ref, params_ref, *refs
):
    g_ref, s_ref = params_ref.at[:, 0:D], params_ref.at[:, D : 2 * D]
    part_refs, refs = refs[:parts], refs[parts:]
    q_ref, k_ref, v_ref, e_ref, o_ref, li_ref, sk_ref, sv_ref, bias_ref, w_ref = refs
    rows = xh_ref.shape[1] // ROW
    first_row = place[0] * rows

    @pl.when(pl.program_id(0) == 0)
    def _():
        query = lax.broadcasted_iota(jnp.int32, (ROW, KEYS), 0)
        key = lax.broadcasted_iota(jnp.int32, (ROW, KEYS), 1)
        summary = jnp.maximum(key - ROW, 0)
        image_row = (place[0] ^ lax.div(summary, rows)) * rows + lax.rem(summary, rows)
        for row in range(rows):
            own = jnp.where(key <= query, 0.0, -1e30)
            earlier = jnp.where(image_row < first_row + row, math.log2(ROW), -1e30)
            bias_ref[row] = jnp.where(key < ROW, own, earlier)
        if parts == 1:
            w_ref[...] = part_refs[0][...]
            return
        wide, height, _ = part_refs[0].shape
        depth = D // parts // wide

        def one(distance, carry):
            for step, part_ref in enumerate(part_refs):
                start = (place[1] ^ step) * (D // parts) + (place[0] ^ distance) * depth
                here = pl.ds(pl.multiple_of(start, depth), depth)
                for block in range(3):
                    w_ref[block, here, :] = part_ref[distance, block * depth : (block + 1) * depth, :]
            return carry

        lax.fori_loop(0, wide, one, 0)

    a1 = (xh_ref[0].astype(F32) * g_ref[...] + s_ref[...]).astype(BF16)
    q_ref[0] = dot(a1, w_ref[0]).astype(BF16)
    k_ref[0] = dot(a1, w_ref[1]).astype(BF16)
    v_ref[0] = dot(a1, w_ref[2]).astype(BF16)
    mean_a = (mean_ref[0].astype(F32) * g_ref[...] + s_ref[...]).astype(BF16)
    sum_k = dot(mean_a, w_ref[1]).astype(BF16)
    sum_v = dot(mean_a, w_ref[2]).astype(BF16)
    sk_ref[0] = sum_k
    sv_ref[0] = sum_v
    masks = head_masks(BF16)
    ones = [jnp.broadcast_to(mask, (KEYS, PAIR)) for mask in masks]
    scale = LOG2E / math.sqrt(HD)

    for row in range(rows):
        here = slice(row * ROW, (row + 1) * ROW)
        for pair in range(PAIRS):
            lanes = slice(pair * PAIR, (pair + 1) * PAIR)
            query = q_ref[0, here, lanes]
            keys = jnp.concatenate([k_ref[0, here, lanes], sum_k[:, lanes]], 0)
            values = jnp.concatenate([v_ref[0, here, lanes], sum_v[:, lanes]], 0)
            total = None
            for half in range(2):
                score = dot_nt(query, keys * masks[half]) * scale + bias_ref[row]
                weight = jnp.exp2(score - jnp.max(score, -1, keepdims=True)).astype(BF16)
                e_ref[0, row, 2 * pair + half] = weight
                part = dot(weight, jnp.concatenate([values * masks[half], ones[half]], 1))
                total = part if total is None else total + part
            inverse = 1.0 / total[:, PAIR:]
            o_ref[0, here, lanes] = (total[:, :PAIR] * inverse).astype(BF16)
            li_ref[0, here, lanes] = inverse.astype(BF16)


def attend_call(place, normal, mean_all, params, parts):
    images, count, _ = normal.shape
    rows = count // ROW
    tokens_shape = jax.ShapeDtypeStruct((images, count, D), BF16)
    return pl.pallas_call(
        functools.partial(attend_kernel, len(parts)),
        grid_spec=pltpu.PrefetchScalarGridSpec(
            num_scalar_prefetch=1,
            grid=(images,),
            in_specs=[
                tile_spec(count, D), tile_spec(ROWS_IMG, D), whole_spec(params.shape),
            ]
            + [whole_spec(part.shape) for part in parts],
            out_specs=[tile_spec(count, D)] * 3
            + [tile_spec(rows, HEADS, ROW, KEYS)]
            + [tile_spec(count, D)] * 2
            + [tile_spec(ROWS_IMG, D)] * 2,
            scratch_shapes=[
                pltpu.VMEM((rows, ROW, KEYS), F32),
                pltpu.VMEM((3, D, D), BF16),
            ],
        ),
        out_shape=[tokens_shape] * 3
        + [jax.ShapeDtypeStruct((images, rows, HEADS, ROW, KEYS), BF16)]
        + [tokens_shape] * 2
        + [jax.ShapeDtypeStruct((images, ROWS_IMG, D), BF16)] * 2,
        compiler_params=pltpu.CompilerParams(vmem_limit_bytes=60 * MIB),
        cost_estimate=pl.CostEstimate(
            flops=images * count * D * D * 10, bytes_accessed=images * count * D * 20, transcendentals=0
        ),
        name="attend",
    )(place, normal, mean_all, params, *parts)


def ff_kernel(
    pieces, owner, place, x_ref, o_ref, cot_ref, li_ref, params_ref,
    wo_ref, u0_ref, u1_ref, u2_ref, u3_ref, d0_ref, d1_ref, d2_ref, d3_ref,
    out_ref, dr_ref, do_ref, small_ref, *refs
):
    grads_refs, (acc_ref, h_ref, xh_ref, act_ref, dp_ref) = refs[:-5], refs[-5:]
    gg_ref, gs_ref = small_ref.at[:, 0:D], small_ref.at[:, D : 2 * D]
    gbu_ref, gbd_ref = small_ref.at[:, 2 * D : 2 * D + FF], small_ref.at[:, 2 * D + FF :]
    g_ref, s_ref = params_ref.at[:, 2 * D : 3 * D], params_ref.at[:, 3 * D : 4 * D]
    bu_ref, bd_ref = params_ref.at[:, 4 * D : 4 * D + FF], params_ref.at[:, 4 * D + FF :]
    step = pl.program_id(0)
    ups = (u0_ref, u1_ref, u2_ref, u3_ref)
    downs = (d0_ref, d1_ref, d2_ref, d3_ref)

    @pl.when(step == 0)
    def _():
        acc_ref[...] = jnp.zeros_like(acc_ref)
        small_ref[...] = jnp.zeros_like(small_ref)

    hidden = x_ref[0].astype(F32) + dot(o_ref[0], wo_ref[0])
    normal, spread = normalize(hidden)
    xh_ref[...] = normal
    h_ref[...] = hidden + bd_ref[...]
    a2 = (normal * g_ref[...] + s_ref[...]).astype(BF16)
    a2_t = a2.T
    cot = cot_ref[0]
    cot_t = cot.T
    c_one = math.sqrt(2.0 / math.pi)
    c_two = c_one * 0.044715
    width = D // 2
    a2_ones = with_ones(a2_t)

    def first_products(start):
        block, inside = start // D, slice(start % D, start % D + width)
        pre = dot(a2, ups[block][0, :, inside]) + bu_ref[:, start : start + width]
        return pre, dot_nt(cot, downs[block][0, inside, :])

    following = first_products(0)
    for start in range(0, FF, width):
        block, inside, columns = start // D, slice(start % D, start % D + width), slice(start, start + width)
        pre, d_act = following
        if start + width < FF:
            following = first_products(start + width)
        square = pre * pre
        half = 0.5 + 0.5 * jnp.tanh(pre * (c_one + c_two * square))
        act = (pre * half).astype(BF16)
        rest = (1.0 - half).astype(BF16)
        half = half.astype(BF16)
        slope = half + act * rest * (2.0 * c_one + (6.0 * c_two) * square.astype(BF16))
        d_pre = d_act.astype(BF16) * slope
        act_ref[:, columns] = act
        dp_ref[:, columns] = d_pre
        part = dot(a2_ones, d_pre)
        acc_ref[1 + block, :, inside] += part[:D]
        gbu_ref[:, columns] += part[D : D + 1]
        acc_ref[1 + NF + block, :, inside] += dot(cot_t, act)
    d_a2 = dot_nt(dp_ref[:, 0:D], ups[0][0])
    for block in range(1, NF):
        d_a2 += dot_nt(dp_ref[:, block * D : (block + 1) * D], ups[block][0])
    normal = xh_ref[...]
    gs_ref[...] += jnp.sum(d_a2, 0, keepdims=True)
    gg_ref[...] += jnp.sum(d_a2 * normal, 0, keepdims=True)
    d_normal = d_a2 * g_ref[...]
    middle = jnp.mean(d_normal, -1, keepdims=True)
    along = jnp.mean(d_normal * normal, -1, keepdims=True)
    cot = cot.astype(F32)
    gbd_ref[...] += jnp.sum(cot, 0, keepdims=True)
    d_hidden = cot + spread * (d_normal - middle - normal * along)
    branch = d_hidden.astype(BF16)
    dr_ref[0] = branch
    total = h_ref[...]
    for block, down in enumerate(downs):
        total += dot(act_ref[:, block * D : (block + 1) * D], down[0])
    out_ref[0] = total.astype(BF16)
    acc_ref[0] += dot(o_ref[0].T, branch)
    do_ref[0] = (dot_nt(branch, wo_ref[0]) * li_ref[0].astype(F32)).astype(BF16)

    @pl.when(step == pl.num_programs(0) - 1)
    def _():
        for block in range(1 + NF, 1 + 2 * NF):
            acc_ref[block] = acc_ref[block].T
        if pieces:
            write_pieces(place, grads_refs, lambda block, here: acc_ref[block, here, :])
        else:
            grads_refs[0][...] = acc_ref[...].astype(BF16)


def grad_shapes(groups, blocks, lead):
    if groups is None:
        return [(blocks, D, D)]
    narrow, wide = groups
    return [lead + (blocks * (D // narrow // wide), D)] * narrow


def ff_call(owner, place, groups, tokens, attended, cotangent, inverse, params, slots):
    images, count, _ = tokens.shape
    tokens_shape = jax.ShapeDtypeStruct((images, count, D), BF16)
    blocks = 1 + 2 * NF
    grads = grad_shapes(groups, blocks, groups and groups[1:])
    return pl.pallas_call(
        functools.partial(ff_kernel, groups is not None),
        grid_spec=pltpu.PrefetchScalarGridSpec(
            num_scalar_prefetch=2,
            grid=(images,),
            in_specs=[tile_spec(count, D)] * 4
            + [whole_spec(params.shape)]
            + [weight_spec(3 + block) for block in range(blocks)],
            out_specs=[tile_spec(count, D)] * 3
            + [out_whole((1, 3 * D + FF))]
            + [out_whole(shape) for shape in grads],
            scratch_shapes=[
                pltpu.VMEM((blocks, D, D), F32),
                pltpu.VMEM((count, D), F32),
                pltpu.VMEM((count, D), F32),
                pltpu.VMEM((count, FF), BF16),
                pltpu.VMEM((count, FF), BF16),
            ],
        ),
        out_shape=[tokens_shape] * 3
        + [jax.ShapeDtypeStruct((1, 3 * D + FF), F32)]
        + [jax.ShapeDtypeStruct(shape, BF16) for shape in grads],
        compiler_params=pltpu.CompilerParams(vmem_limit_bytes=60 * MIB),
        cost_estimate=pl.CostEstimate(
            flops=images * count * D * D * 54, bytes_accessed=images * count * D * 14, transcendentals=0
        ),
        name="feed_forward",
    )(owner, place, tokens, attended, cotangent, inverse, params, *([slots] * blocks))


def back_kernel(pieces, owner, place, *refs):
    (q_ref, k_ref, v_ref, o_ref, do_ref, e_ref, xh_ref, sk_ref, sv_ref, mean_ref, params_ref) = refs[:11]
    weights = refs[11:14]
    grad_ref, dm_ref, small_ref, *grads_refs = refs[14:-3]
    acc_ref, dsk_ref, dsv_ref = refs[-3:]
    step = pl.program_id(0)
    rows = q_ref.shape[1] // ROW
    scale = 1.0 / math.sqrt(HD)

    @pl.when(step == 0)
    def _():
        acc_ref[...] = jnp.zeros_like(acc_ref)

    sum_k = sk_ref[0]
    sum_v = sv_ref[0]
    masks = head_masks(BF16)
    blank = jnp.zeros((HD, KEYS), BF16)
    minus = jnp.full((HD, KEYS), -1.0, BF16)
    d_sum_k = jnp.zeros((ROWS_IMG, D), F32)
    d_sum_v = jnp.zeros((ROWS_IMG, D), F32)
    for row in range(rows):
        here = slice(row * ROW, (row + 1) * ROW)
        d_out = do_ref[0, here, :]
        d_out_o = d_out * o_ref[0, here, :]
        q_t = (q_ref[0, here, :] * scale).T
        d_out_t = d_out.T
        v_t = jnp.concatenate([v_ref[0, here, :], sum_v], 0).T
        d_keys = []
        d_values = []
        for pair in range(PAIRS):
            lanes = slice(pair * PAIR, (pair + 1) * PAIR)
            keys = jnp.concatenate([k_ref[0, here, lanes], sum_k[:, lanes]], 0)
            left = jnp.concatenate([d_out[:, lanes], d_out_o[:, lanes]], 1)
            d_query = None
            for half in range(2):
                head = 2 * pair + half
                mine = slice(head * HD, (head + 1) * HD)
                own = v_t[mine]
                right = [own, blank, minus, blank] if half == 0 else [blank, own, blank, minus]
                weight = e_ref[0, row, head]
                d_score = weight * dot(left, jnp.concatenate(right, 0)).astype(BF16)
                d_values.append(dot(d_out_t[mine], weight).astype(BF16))
                d_keys.append(dot(q_t[mine], d_score).astype(BF16))
                part = dot(d_score, keys * masks[half])
                d_query = part if d_query is None else d_query + part
            grad_ref[0, here, lanes] = (d_query * scale).astype(BF16)
        d_key = jnp.concatenate(d_keys, 0).T
        d_value = jnp.concatenate(d_values, 0).T
        grad_ref[0, here, D : 2 * D] = d_key[:ROW]
        grad_ref[0, here, 2 * D :] = d_value[:ROW]
        d_sum_k += d_key[ROW:].astype(F32)
        d_sum_v += d_value[ROW:].astype(F32)
    dsk_ref[step] = d_sum_k.astype(BF16)
    dsv_ref[step] = d_sum_v.astype(BF16)
    acc_ref[...] += dot(with_ones(xh_ref[0].T), grad_ref[0])

    @pl.when(step == pl.num_programs(0) - 1)
    def _():
        mean_t = with_ones(mean_ref[...].reshape(-1, D).T)
        all_k = dsk_ref[...].reshape(-1, D)
        all_v = dsv_ref[...].reshape(-1, D)
        acc_ref[:, D : 2 * D] += dot(mean_t, all_k)
        acc_ref[:, 2 * D :] += dot(mean_t, all_v)
        d_mean = dot_nt(all_k, weights[1][0]) + dot_nt(all_v, weights[2][0])
        inner, outer, height, _ = dm_ref.shape
        for distance in range(inner * outer):
            first = range(distance * rows, d_mean.shape[0], ROWS_IMG)
            piece = jnp.concatenate([d_mean[row : row + rows] for row in first], 0)
            dm_ref[distance % inner, distance // inner] = piece.astype(BF16)
        gain_grad = jnp.zeros((D, 1), F32)
        shift_grad = jnp.zeros((1, D), F32)
        gain = jnp.broadcast_to(params_ref[:, 0:D], (8, D)).T[:, 0:1]
        shift = jnp.broadcast_to(params_ref[:, D : 2 * D], (8, D)).T[:, 0:1]
        for block, w_ref in enumerate(weights):
            columns = slice(block * D, (block + 1) * D)
            product = acc_ref[0:D, columns]
            sums = acc_ref[D : D + 1, columns]
            gain_grad += jnp.sum(product * w_ref[0].astype(F32), -1, keepdims=True)
            high = sums.astype(BF16)
            parts = jnp.concatenate([high, (sums - high.astype(F32)).astype(BF16)], 0)
            parts = jnp.concatenate([parts, jnp.zeros((14, D), BF16)], 0)
            shift_grad += jnp.sum(dot_nt(parts, w_ref[0]), 0, keepdims=True)
            acc_ref[0:D, columns] = product * gain + shift * sums
        small_ref[:, 0:D] = jnp.broadcast_to(gain_grad, (D, 128)).T[0:1]
        small_ref[:, D:] = shift_grad
        if pieces:
            write_pieces(place, grads_refs, lambda block, here: acc_ref[here, block * D : (block + 1) * D])
        else:
            for block in range(3):
                grads_refs[0][block] = acc_ref[0:D, block * D : (block + 1) * D].astype(BF16)


def back_call(owner, place, groups, operands, params, slots):
    images, count, _ = operands[0].shape
    rows = count // ROW
    grads = grad_shapes(groups, 3, groups and group_sizes(groups[1]))
    mean_shape = group_sizes(ROWS_IMG // rows) + (images * rows, D)
    return pl.pallas_call(
        functools.partial(back_kernel, groups is not None),
        grid_spec=pltpu.PrefetchScalarGridSpec(
            num_scalar_prefetch=2,
            grid=(images,),
            in_specs=[tile_spec(count, D)] * 5
            + [tile_spec(rows, HEADS, ROW, KEYS), tile_spec(count, D)]
            + [tile_spec(ROWS_IMG, D)] * 2
            + [whole_spec((images, ROWS_IMG, D)), whole_spec(params.shape)]
            + [weight_spec(block) for block in range(3)],
            out_specs=[tile_spec(count, 3 * D), out_whole(mean_shape), out_whole((1, 2 * D))]
            + [out_whole(shape) for shape in grads],
            scratch_shapes=[
                pltpu.VMEM((D + 16, 3 * D), F32),
                pltpu.VMEM((images, ROWS_IMG, D), BF16),
                pltpu.VMEM((images, ROWS_IMG, D), BF16),
            ],
        ),
        out_shape=[
            jax.ShapeDtypeStruct((images, count, 3 * D), BF16),
            jax.ShapeDtypeStruct(mean_shape, BF16),
            jax.ShapeDtypeStruct((1, 2 * D), F32),
        ]
        + [jax.ShapeDtypeStruct(shape, BF16) for shape in grads],
        compiler_params=pltpu.CompilerParams(vmem_limit_bytes=60 * MIB),
        cost_estimate=pl.CostEstimate(
            flops=images * count * D * D * 20, bytes_accessed=images * count * D * 24, transcendentals=0
        ),
        name="attend_back",
    )(owner, place, *operands, params, slots, slots, slots)


def low_kernel(owner, grad_ref, wq_ref, wk_ref, wv_ref, low_ref):
    joined = jnp.concatenate([wq_ref[0], wk_ref[0], wv_ref[0]], 1)
    low_ref[...] = dot_nt(grad_ref[...].reshape(-1, 3 * D), joined).astype(BF16).reshape(low_ref.shape)


def low_call(owner, grads, slots):
    images, count, _ = grads.shape
    return pl.pallas_call(
        low_kernel,
        grid_spec=pltpu.PrefetchScalarGridSpec(
            num_scalar_prefetch=1,
            grid=(images // 2,),
            in_specs=[two_spec(count, 3 * D)] + [weight_spec(block) for block in range(3)],
            out_specs=two_spec(count, D),
        ),
        out_shape=jax.ShapeDtypeStruct((images, count, D), BF16),
        compiler_params=pltpu.CompilerParams(vmem_limit_bytes=60 * MIB),
        cost_estimate=pl.CostEstimate(
            flops=images * count * D * D * 6, bytes_accessed=images * count * D * 8, transcendentals=0
        ),
        name="project_back",
    )(owner, grads, slots, slots, slots)


def last_kernel(start, rows, xh_ref, scale_ref, low_ref, dr_ref, sums_ref, params_ref, out_ref):
    g_ref = params_ref.at[:, 0:D]
    for image, row in itertools.product(range(2), range(rows)):
        mean_row = start + (2 * pl.program_id(0) + image) * rows + row
        here = slice(row * ROW, (row + 1) * ROW)
        normal, spread = xh_ref[image, here, :].astype(F32), scale_ref[image, here, :]
        total = low_ref[image, here, :].astype(F32) + sums_ref[pl.ds(mean_row, 1), :] * (1.0 / ROW)
        d_normal = total * g_ref[...]
        middle = jnp.mean(d_normal, -1, keepdims=True)
        along = jnp.mean(d_normal * normal, -1, keepdims=True)
        out_ref[image, here, :] = dr_ref[image, here, :].astype(F32) + spread * (d_normal - middle - normal * along)


def last_call(normal, scale, d_low, d_branch, sums, start, params):
    images, count, _ = normal.shape
    return pl.pallas_call(
        functools.partial(last_kernel, start, count // ROW),
        grid=(images // 2,),
        in_specs=[two_spec(count, D), two_spec(count, 1), two_spec(count, D), two_spec(count, D)]
        + [whole_spec(sums.shape), whole_spec(params.shape)],
        out_specs=two_spec(count, D),
        out_shape=jax.ShapeDtypeStruct((images, count, D), F32),
        compiler_params=pltpu.CompilerParams(vmem_limit_bytes=60 * MIB),
        cost_estimate=pl.CostEstimate(
            flops=images * count * D * 20, bytes_accessed=images * count * D * 11, transcendentals=0
        ),
        name="norm_one_back",
    )(normal, scale, d_low, d_branch, sums, params)


def adamw_update(weight_now, gradient, first_moment, second_moment, decay_rate, step_rate):
    first_new = 0.9 * first_moment + 0.1 * gradient
    second_new = 0.95 * second_moment + 0.05 * gradient * gradient
    direction = first_new / (1.0 - 0.9**STEP) / (jnp.sqrt(second_new / (1.0 - 0.95**STEP)) + 1e-08)
    return (weight_now - step_rate * (direction + decay_rate * weight_now), first_new, second_new)


def swap(value, axis, bit):
    size = lax.axis_size(axis)
    return lax.ppermute(value, axis, [(index, index ^ bit) for index in range(size)])


def to_rows(values):
    high = lax.reduce_precision(values, 8, 7)
    rows = jnp.concatenate([high, values - high], 1).reshape(-1, D).astype(BF16)
    return jnp.pad(rows, ((0, -rows.shape[0] % 16), (0, 0)))


def from_rows(rows, size):
    count = size // D
    return (rows[:count] + rows[count : 2 * count]).reshape(1, size)


def join(value):
    inner, outer = group_sizes(lax.axis_size("wide"))
    far = jnp.stack([value] + [swap(value, "wide", inner * step) for step in range(1, outer)])
    near = jnp.stack([far] + [swap(far, "wide", step) for step in range(1, inner)], 1)
    return near.reshape((inner * outer,) + value.shape)


def reorder(value, axis, dim=0):
    return jnp.take(value, lax.axis_index(axis) ^ jnp.arange(lax.axis_size(axis)), axis=dim)


def fetch_blocks(low_master, owners, means, whole_pieces):
    wide = lax.axis_size("wide")
    narrow = lax.axis_size("narrow")
    pieces = lax.all_to_all(low_master.reshape(wide, -1, D), "wide", 0, 0, tiled=True)
    mine = jnp.take(pieces, owners, axis=0)
    count, depth, _ = mine.shape
    joined = join(jnp.concatenate([mine.reshape(-1, D), means.reshape(-1, D)], 0))
    mean_all = joined[:, count * depth :].reshape((wide,) + means.shape).swapaxes(0, 1)
    mean_all = mean_all.reshape(means.shape[0], -1, D)
    if whole_pieces:
        return [joined] + [swap(joined, "narrow", step) for step in range(1, narrow)], mean_all
    rows = joined[:, : count * depth]
    halves = jnp.stack([rows] + [swap(rows, "narrow", step) for step in range(1, narrow)])
    halves = reorder(reorder(halves, "narrow"), "wide", 1).reshape(narrow, wide, count, depth, D)
    return [halves.transpose(2, 0, 1, 3, 4).reshape(count, D, D)], mean_all


def piece_lists(grads):
    if len(grads) > 1:
        return list(grads)
    (blocks,) = grads
    narrow = lax.axis_size("narrow")
    wide = lax.axis_size("wide")
    parts = blocks.reshape(blocks.shape[0], narrow, wide, -1, D).transpose(1, 2, 0, 3, 4)
    return list(reorder(parts, "narrow").reshape(narrow, wide, -1, D))


def by_group(pieces):
    inner, outer = group_sizes(lax.axis_size("wide"))
    return pieces.reshape((outer, inner) + pieces.shape[1:]).swapaxes(0, 1)


def sum_narrow(lists):
    total = lists[0].astype(F32)
    for step in range(1, len(lists)):
        total += swap(lists[step], "narrow", step).astype(F32)
    return total.astype(BF16)


def sum_group(pieces, stride):
    total = pieces[0].astype(F32)
    for step in range(1, len(pieces)):
        total += swap(pieces[step], "wide", step * stride).astype(F32)
    return total


def per_device(
    tokens, cotangent, owner_list, master, moment_one, moment_two, small_params, small_one, small_two
):
    images, count, _ = tokens.shape
    rows = count // ROW
    wide = lax.axis_size("wide")
    small = small_params.reshape(1, -1)
    low_master = master.astype(BF16)
    slots = lax.all_gather(low_master.reshape(-1, D), ("wide", "narrow"), axis=0, tiled=True)
    slots = slots.reshape(-1, D, D)
    narrow = lax.axis_size("narrow")
    inner, outer = group_sizes(wide)
    depth = D // narrow // wide
    groups = (narrow, wide) if depth % 16 == 0 and narrow > 1 else None
    me = lax.axis_index("wide")
    names = owner_list[None, :] == jnp.arange(wide, dtype=jnp.int32)[:, None]
    owned = jnp.any(names, 1)
    block_of = jnp.argmax(names, 1)
    place = jnp.stack([me, lax.axis_index("narrow")]).astype(jnp.int32)
    place, small, owned, block_of, tokens = lax.optimization_barrier((place, small, owned, block_of, tokens))
    normal, scale, means = norm_call(tokens)
    parts, mean_all = fetch_blocks(low_master, owner_list[:3], means, groups is not None)
    queries, keys, values, weights, attended, inverse, sum_k, sum_v = attend_call(
        place, normal, mean_all, small, parts
    )
    block_out, d_branch, d_out, late_small, *grads_late = ff_call(
        owner_list, place, groups, tokens, attended, cotangent, inverse, small, slots
    )

    tie = lax.optimization_barrier
    late, queries = tie((sum_narrow(piece_lists(grads_late)), queries))
    late = lax.all_to_all(late, "wide", 0, 0, tiled=True)
    operands = (queries, keys, values, attended, d_out, weights, normal, sum_k, sum_v, mean_all)
    d_joined, d_mean, early_small, *grads_early = back_call(
        owner_list, place, groups, operands, small, slots
    )
    late, early_small, *grads_early = tie((late, early_small, *grads_early))
    late = jnp.sum(late.astype(F32), 0)
    small_sums = jnp.concatenate([early_small, late_small], 1)
    size = small_sums.shape[1]
    bit = 1
    while bit < narrow:
        small_sums = small_sums + swap(small_sums, "narrow", bit)
        bit *= 2
    early = sum_narrow(piece_lists(grads_early))
    if groups is None:
        early = by_group(reorder(early, "wide"))
    early, small_sums, d_joined = tie((early, small_sums, d_joined))
    d_low = low_call(owner_list, d_joined, slots)

    cuts = (3 * depth, 3 * depth + images * rows)
    small_rows = to_rows(small_sums)
    near = jnp.concatenate([early, d_mean], 2).reshape(inner, outer * cuts[1], D)
    near = sum_group([jnp.concatenate([near[step], small_rows], 0) for step in range(inner)], 1)
    near, late, d_low = tie((near, late, d_low))
    small_rows = to_rows(from_rows(near[outer * cuts[1] :], size))
    far = near[: outer * cuts[1]].astype(BF16).reshape(outer, cuts[1], D)
    far = sum_group([jnp.concatenate([far[step], small_rows], 0) for step in range(outer)], inner)
    small_grad = from_rows(far[cuts[1] :], size).reshape(-1)
    shares = jnp.concatenate([far[: cuts[0]], late], 0).reshape(-1, depth, D).astype(BF16)

    moved = jnp.where(owned[:, None, None], jnp.take(shares, block_of, axis=0), jnp.zeros((), BF16))
    moved = lax.all_to_all(moved, "wide", 0, 0, tiled=True)
    grad_tokens = last_call(normal, scale, d_low, d_branch, far, cuts[0], small)
    moved, grad_tokens = tie((moved, grad_tokens))
    own_grad = moved.reshape(1, -1, D).astype(F32)
    owns_slot = owned[me]
    slot_weight, slot_first, slot_second = adamw_update(
        master, own_grad, moment_one, moment_two, 0.1, RATE
    )
    new_master = jnp.where(owns_slot, slot_weight, master)
    new_one = jnp.where(owns_slot, slot_first, moment_one)
    new_two = jnp.where(owns_slot, slot_second, moment_two)
    small_new, small_one_new, small_two_new = adamw_update(
        small_params, small_grad, small_one, small_two, 0.0, GAIN_RATE
    )
    return (block_out, grad_tokens, new_master, new_one, new_two, small_new, small_one_new, small_two_new)


def solution(mesh):
    split = P("narrow", "wide", None)
    slot = P("wide", "narrow", None)
    return jax.shard_map(
        per_device,
        mesh=mesh,
        in_specs=(split, split, P(), slot, slot, slot, P(), P(), P()),
        out_specs=(split, split, slot, slot, slot, P(), P(), P()),
        check_vma=False,
    )
```

```python
import functools
import functools
import itertools
import math

import jax
import jax.numpy as jnp
from jax import lax
from jax.experimental import pallas as pl
from jax.experimental.pallas import tpu as pltpu
from jax.sharding import PartitionSpec as P

D = 512
HEADS = 8
HD = 64
PAIR = 2 * HD
PAIRS = HEADS // 2
FF = 2048
NF = FF // D
ROW = 192
ROWS_IMG = 64
KEYS = ROW + ROWS_IMG
STEP = 10
RATE = 0.03
GAIN_RATE = 0.4
EPS = 1e-05
LOG2E = math.log2(math.e)
F32 = jnp.float32
BF16 = jnp.bfloat16
MIB = 1024 * 1024


def dot(left, right):
    return jnp.dot(left, right, preferred_element_type=F32)


def dot_nt(left, right):
    return lax.dot_general(left, right, (((1,), (1,)), ((), ())), preferred_element_type=F32)


def normalize(values):
    centred = values - jnp.mean(values, -1, keepdims=True)
    scale = lax.rsqrt(jnp.mean(centred * centred, -1, keepdims=True) + EPS)
    return centred * scale, scale


def head_masks(dtype):
    lane = lax.broadcasted_iota(jnp.int32, (1, PAIR), 1)
    first = (lane < HD).astype(F32)
    return first.astype(dtype), (1.0 - first).astype(dtype)


def tile_spec(*tail, buffers=None):
    zeros = (0,) * len(tail)
    return pl.BlockSpec((1,) + tail, lambda step, *_: (step,) + zeros)


def two_spec(*tail):
    zeros = (0,) * len(tail)
    return pl.BlockSpec((2,) + tail, lambda step, *_: (step,) + zeros)


def whole_spec(shape):
    zeros = (0,) * len(shape)
    return pl.BlockSpec(shape, lambda step, *_: zeros, pipeline_mode=pl.Buffered(1))


def weight_spec(block):
    return pl.BlockSpec(
        (1, D, D), lambda step, owner, *_: (owner[block], 0, 0), pipeline_mode=pl.Buffered(1)
    )


def out_whole(shape):
    zeros = (0,) * len(shape)
    return pl.BlockSpec(shape, lambda step, *_: zeros)


def with_ones(rows):
    return jnp.concatenate([rows, jnp.ones((16, rows.shape[1]), rows.dtype)], 0)


def norm_kernel(x_ref, xh_ref, scale_ref, mean_ref):
    normal, scale_ref[0] = normalize(x_ref[0].astype(F32))
    xh_ref[0] = normal.astype(BF16)
    for row in range(mean_ref.shape[1]):
        part = normal[row * ROW : (row + 1) * ROW]
        mean_ref[0, row : row + 1, :] = jnp.mean(part, 0, keepdims=True).astype(BF16)


def norm_call(tokens):
    images, count, _ = tokens.shape
    rows = count // ROW
    return pl.pallas_call(
        norm_kernel,
        grid=(images,),
        in_specs=[tile_spec(count, D)],
        out_specs=[tile_spec(count, D), tile_spec(count, 1), tile_spec(rows, D)],
        out_shape=[
            jax.ShapeDtypeStruct((images, count, D), BF16),
            jax.ShapeDtypeStruct((images, count, 1), F32),
            jax.ShapeDtypeStruct((images, rows, D), BF16),
        ],
        compiler_params=pltpu.CompilerParams(vmem_limit_bytes=60 * MIB),
        cost_estimate=pl.CostEstimate(
            flops=images * count * D * 10, bytes_accessed=images * count * D * 4, transcendentals=0
        ),
        name="norm_one",
    )(tokens)


def group_sizes(wide):
    inner = min(4, wide)
    return inner, wide // inner


def write_pieces(place, out_refs, read):
    narrow = len(out_refs)
    *lead, height, _ = out_refs[0].shape
    wide = math.prod(lead)
    depth = D // narrow // wide

    def one(number, carry):
        for step, out_ref in enumerate(out_refs):
            device = number if len(lead) == 1 else place[0] ^ number
            start = (place[1] ^ step) * (D // narrow) + device * depth
            here = pl.ds(pl.multiple_of(start, depth), depth)
            index = (number,) if len(lead) == 1 else (number % lead[0], number // lead[0])
            for block in range(height // depth):
                value = read(block, here).astype(BF16)
                out_ref[index + (slice(block * depth, (block + 1) * depth), slice(None))] = value
        return carry

    lax.fori_loop(0, wide, one, 0)


def attend_kernel(
    parts, place, xh_ref, mean_ref, params_ref, *refs
):
    g_ref, s_ref = params_ref.at[:, 0:D], params_ref.at[:, D : 2 * D]
    part_refs, refs = refs[:parts], refs[parts:]
    q_ref, k_ref, v_ref, e_ref, o_ref, li_ref, sk_ref, sv_ref, bias_ref, w_ref = refs
    rows = xh_ref.shape[1] // ROW
    first_row = place[0] * rows

    @pl.when(pl.program_id(0) == 0)
    def _():
        query = lax.broadcasted_iota(jnp.int32, (ROW, KEYS), 0)
        key = lax.broadcasted_iota(jnp.int32, (ROW, KEYS), 1)
        summary = jnp.maximum(key - ROW, 0)
        image_row = (place[0] ^ lax.div(summary, rows)) * rows + lax.rem(summary, rows)
        for row in range(rows):
            own = jnp.where(key <= query, 0.0, -1e30)
            earlier = jnp.where(image_row < first_row + row, math.log2(ROW), -1e30)
            bias_ref[row] = jnp.where(key < ROW, own, earlier)
        if parts == 1:
            w_ref[...] = part_refs[0][...]
            return
        wide, height, _ = part_refs[0].shape
        depth = D // parts // wide

        def one(distance, carry):
            for step, part_ref in enumerate(part_refs):
                start = (place[1] ^ step) * (D // parts) + (place[0] ^ distance) * depth
                here = pl.ds(pl.multiple_of(start, depth), depth)
                for block in range(3):
                    w_ref[block, here, :] = part_ref[distance, block * depth : (block + 1) * depth, :]
            return carry

        lax.fori_loop(0, wide, one, 0)

    a1 = (xh_ref[0].astype(F32) * g_ref[...] + s_ref[...]).astype(BF16)
    q_ref[0] = dot(a1, w_ref[0]).astype(BF16)
    k_ref[0] = dot(a1, w_ref[1]).astype(BF16)
    v_ref[0] = dot(a1, w_ref[2]).astype(BF16)
    mean_a = (mean_ref[0].astype(F32) * g_ref[...] + s_ref[...]).astype(BF16)
    sum_k = dot(mean_a, w_ref[1]).astype(BF16)
    sum_v = dot(mean_a, w_ref[2]).astype(BF16)
    sk_ref[0] = sum_k
    sv_ref[0] = sum_v
    masks = head_masks(BF16)
    ones = [jnp.broadcast_to(mask, (KEYS, PAIR)) for mask in masks]
    scale = LOG2E / math.sqrt(HD)

    for row in range(rows):
        here = slice(row * ROW, (row + 1) * ROW)
        for pair in range(PAIRS):
            lanes = slice(pair * PAIR, (pair + 1) * PAIR)
            query = q_ref[0, here, lanes]
            keys = jnp.concatenate([k_ref[0, here, lanes], sum_k[:, lanes]], 0)
            values = jnp.concatenate([v_ref[0, here, lanes], sum_v[:, lanes]], 0)
            total = None
            for half in range(2):
                score = dot_nt(query, keys * masks[half]) * scale + bias_ref[row]
                weight = jnp.exp2(score - jnp.max(score, -1, keepdims=True)).astype(BF16)
                e_ref[0, row, 2 * pair + half] = weight
                part = dot(weight, jnp.concatenate([values * masks[half], ones[half]], 1))
                total = part if total is None else total + part
            inverse = 1.0 / total[:, PAIR:]
            o_ref[0, here, lanes] = (total[:, :PAIR] * inverse).astype(BF16)
            li_ref[0, here, lanes] = inverse.astype(BF16)


def attend_call(place, normal, mean_all, params, parts):
    images, count, _ = normal.shape
    rows = count // ROW
    tokens_shape = jax.ShapeDtypeStruct((images, count, D), BF16)
    return pl.pallas_call(
        functools.partial(attend_kernel, len(parts)),
        grid_spec=pltpu.PrefetchScalarGridSpec(
            num_scalar_prefetch=1,
            grid=(images,),
            in_specs=[
                tile_spec(count, D), tile_spec(ROWS_IMG, D), whole_spec(params.shape),
            ]
            + [whole_spec(part.shape) for part in parts],
            out_specs=[tile_spec(count, D)] * 3
            + [tile_spec(rows, HEADS, ROW, KEYS)]
            + [tile_spec(count, D)] * 2
            + [tile_spec(ROWS_IMG, D)] * 2,
            scratch_shapes=[
                pltpu.VMEM((rows, ROW, KEYS), F32),
                pltpu.VMEM((3, D, D), BF16),
            ],
        ),
        out_shape=[tokens_shape] * 3
        + [jax.ShapeDtypeStruct((images, rows, HEADS, ROW, KEYS), BF16)]
        + [tokens_shape] * 2
        + [jax.ShapeDtypeStruct((images, ROWS_IMG, D), BF16)] * 2,
        compiler_params=pltpu.CompilerParams(vmem_limit_bytes=60 * MIB),
        cost_estimate=pl.CostEstimate(
            flops=images * count * D * D * 10, bytes_accessed=images * count * D * 20, transcendentals=0
        ),
        name="attend",
    )(place, normal, mean_all, params, *parts)


def ff_kernel(
    pieces, owner, place, x_ref, o_ref, cot_ref, li_ref, params_ref,
    wo_ref, u0_ref, u1_ref, u2_ref, u3_ref, d0_ref, d1_ref, d2_ref, d3_ref,
    out_ref, dr_ref, do_ref, small_ref, *refs
):
    grads_refs, (acc_ref, h_ref, xh_ref, act_ref, dp_ref) = refs[:-5], refs[-5:]
    gg_ref, gs_ref = small_ref.at[:, 0:D], small_ref.at[:, D : 2 * D]
    gbu_ref, gbd_ref = small_ref.at[:, 2 * D : 2 * D + FF], small_ref.at[:, 2 * D + FF :]
    g_ref, s_ref = params_ref.at[:, 2 * D : 3 * D], params_ref.at[:, 3 * D : 4 * D]
    bu_ref, bd_ref = params_ref.at[:, 4 * D : 4 * D + FF], params_ref.at[:, 4 * D + FF :]
    step = pl.program_id(0)
    ups = (u0_ref, u1_ref, u2_ref, u3_ref)
    downs = (d0_ref, d1_ref, d2_ref, d3_ref)

    @pl.when(step == 0)
    def _():
        acc_ref[...] = jnp.zeros_like(acc_ref)
        small_ref[...] = jnp.zeros_like(small_ref)

    hidden = x_ref[0].astype(F32) + dot(o_ref[0], wo_ref[0])
    normal, spread = normalize(hidden)
    xh_ref[...] = normal
    h_ref[...] = hidden + bd_ref[...]
    a2 = (normal * g_ref[...] + s_ref[...]).astype(BF16)
    a2_t = a2.T
    cot = cot_ref[0]
    cot_t = cot.T
    c_one = math.sqrt(2.0 / math.pi)
    c_two = c_one * 0.044715
    width = D // 2
    a2_ones = with_ones(a2_t)

    def first_products(start):
        block, inside = start // D, slice(start % D, start % D + width)
        pre = dot(a2, ups[block][0, :, inside]) + bu_ref[:, start : start + width]
        return pre, dot_nt(cot, downs[block][0, inside, :])

    following = first_products(0)
    for start in range(0, FF, width):
        block, inside, columns = start // D, slice(start % D, start % D + width), slice(start, start + width)
        pre, d_act = following
        if start + width < FF:
            following = first_products(start + width)
        square = pre * pre
        half = 0.5 + 0.5 * jnp.tanh(pre * (c_one + c_two * square))
        act = (pre * half).astype(BF16)
        rest = (1.0 - half).astype(BF16)
        half = half.astype(BF16)
        slope = half + act * rest * (2.0 * c_one + (6.0 * c_two) * square.astype(BF16))
        d_pre = d_act.astype(BF16) * slope
        act_ref[:, columns] = act
        dp_ref[:, columns] = d_pre
        part = dot(a2_ones, d_pre)
        acc_ref[1 + block, :, inside] += part[:D]
        gbu_ref[:, columns] += part[D : D + 1]
        acc_ref[1 + NF + block, :, inside] += dot(cot_t, act)
    d_a2 = dot_nt(dp_ref[:, 0:D], ups[0][0])
    for block in range(1, NF):
        d_a2 += dot_nt(dp_ref[:, block * D : (block + 1) * D], ups[block][0])
    normal = xh_ref[...]
    gs_ref[...] += jnp.sum(d_a2, 0, keepdims=True)
    gg_ref[...] += jnp.sum(d_a2 * normal, 0, keepdims=True)
    d_normal = d_a2 * g_ref[...]
    middle = jnp.mean(d_normal, -1, keepdims=True)
    along = jnp.mean(d_normal * normal, -1, keepdims=True)
    cot = cot.astype(F32)
    gbd_ref[...] += jnp.sum(cot, 0, keepdims=True)
    d_hidden = cot + spread * (d_normal - middle - normal * along)
    branch = d_hidden.astype(BF16)
    dr_ref[0] = branch
    total = h_ref[...]
    for block, down in enumerate(downs):
        total += dot(act_ref[:, block * D : (block + 1) * D], down[0])
    out_ref[0] = total.astype(BF16)
    acc_ref[0] += dot(o_ref[0].T, branch)
    do_ref[0] = (dot_nt(branch, wo_ref[0]) * li_ref[0].astype(F32)).astype(BF16)

    @pl.when(step == pl.num_programs(0) - 1)
    def _():
        for block in range(1 + NF, 1 + 2 * NF):
            acc_ref[block] = acc_ref[block].T
        if pieces:
            write_pieces(place, grads_refs, lambda block, here: acc_ref[block, here, :])
        else:
            grads_refs[0][...] = acc_ref[...].astype(BF16)


def grad_shapes(groups, blocks, lead):
    if groups is None:
        return [(blocks, D, D)]
    narrow, wide = groups
    return [lead + (blocks * (D // narrow // wide), D)] * narrow


def ff_call(owner, place, groups, tokens, attended, cotangent, inverse, params, slots):
    images, count, _ = tokens.shape
    tokens_shape = jax.ShapeDtypeStruct((images, count, D), BF16)
    blocks = 1 + 2 * NF
    grads = grad_shapes(groups, blocks, groups and groups[1:])
    return pl.pallas_call(
        functools.partial(ff_kernel, groups is not None),
        grid_spec=pltpu.PrefetchScalarGridSpec(
            num_scalar_prefetch=2,
            grid=(images,),
            in_specs=[tile_spec(count, D)] * 4
            + [whole_spec(params.shape)]
            + [weight_spec(3 + block) for block in range(blocks)],
            out_specs=[tile_spec(count, D)] * 3
            + [out_whole((1, 3 * D + FF))]
            + [out_whole(shape) for shape in grads],
            scratch_shapes=[
                pltpu.VMEM((blocks, D, D), F32),
                pltpu.VMEM((count, D), F32),
                pltpu.VMEM((count, D), F32),
                pltpu.VMEM((count, FF), BF16),
                pltpu.VMEM((count, FF), BF16),
            ],
        ),
        out_shape=[tokens_shape] * 3
        + [jax.ShapeDtypeStruct((1, 3 * D + FF), F32)]
        + [jax.ShapeDtypeStruct(shape, BF16) for shape in grads],
        compiler_params=pltpu.CompilerParams(vmem_limit_bytes=60 * MIB),
        cost_estimate=pl.CostEstimate(
            flops=images * count * D * D * 54, bytes_accessed=images * count * D * 14, transcendentals=0
        ),
        name="feed_forward",
    )(owner, place, tokens, attended, cotangent, inverse, params, *([slots] * blocks))


def back_kernel(pieces, owner, place, *refs):
    (q_ref, k_ref, v_ref, o_ref, do_ref, e_ref, xh_ref, sk_ref, sv_ref, mean_ref, params_ref) = refs[:11]
    weights = refs[11:14]
    grad_ref, dm_ref, small_ref, *grads_refs = refs[14:-3]
    acc_ref, dsk_ref, dsv_ref = refs[-3:]
    step = pl.program_id(0)
    rows = q_ref.shape[1] // ROW
    scale = 1.0 / math.sqrt(HD)

    @pl.when(step == 0)
    def _():
        acc_ref[...] = jnp.zeros_like(acc_ref)

    sum_k = sk_ref[0]
    sum_v = sv_ref[0]
    masks = head_masks(BF16)
    blank = jnp.zeros((HD, KEYS), BF16)
    minus = jnp.full((HD, KEYS), -1.0, BF16)
    d_sum_k = jnp.zeros((ROWS_IMG, D), F32)
    d_sum_v = jnp.zeros((ROWS_IMG, D), F32)
    for row in range(rows):
        here = slice(row * ROW, (row + 1) * ROW)
        d_out = do_ref[0, here, :]
        d_out_o = d_out * o_ref[0, here, :]
        q_t = (q_ref[0, here, :] * scale).T
        d_out_t = d_out.T
        v_t = jnp.concatenate([v_ref[0, here, :], sum_v], 0).T
        d_keys = []
        d_values = []
        for pair in range(PAIRS):
            lanes = slice(pair * PAIR, (pair + 1) * PAIR)
            keys = jnp.concatenate([k_ref[0, here, lanes], sum_k[:, lanes]], 0)
            left = jnp.concatenate([d_out[:, lanes], d_out_o[:, lanes]], 1)
            d_query = None
            for half in range(2):
                head = 2 * pair + half
                mine = slice(head * HD, (head + 1) * HD)
                own = v_t[mine]
                right = [own, blank, minus, blank] if half == 0 else [blank, own, blank, minus]
                weight = e_ref[0, row, head]
                d_score = weight * dot(left, jnp.concatenate(right, 0)).astype(BF16)
                d_values.append(dot(d_out_t[mine], weight).astype(BF16))
                d_keys.append(dot(q_t[mine], d_score).astype(BF16))
                part = dot(d_score, keys * masks[half])
                d_query = part if d_query is None else d_query + part
            grad_ref[0, here, lanes] = (d_query * scale).astype(BF16)
        d_key = jnp.concatenate(d_keys, 0).T
        d_value = jnp.concatenate(d_values, 0).T
        grad_ref[0, here, D : 2 * D] = d_key[:ROW]
        grad_ref[0, here, 2 * D :] = d_value[:ROW]
        d_sum_k += d_key[ROW:].astype(F32)
        d_sum_v += d_value[ROW:].astype(F32)
    dsk_ref[step] = d_sum_k.astype(BF16)
    dsv_ref[step] = d_sum_v.astype(BF16)
    acc_ref[...] += dot(with_ones(xh_ref[0].T), grad_ref[0])

    @pl.when(step == pl.num_programs(0) - 1)
    def _():
        mean_t = with_ones(mean_ref[...].reshape(-1, D).T)
        all_k = dsk_ref[...].reshape(-1, D)
        all_v = dsv_ref[...].reshape(-1, D)
        acc_ref[:, D : 2 * D] += dot(mean_t, all_k)
        acc_ref[:, 2 * D :] += dot(mean_t, all_v)
        d_mean = dot_nt(all_k, weights[1][0]) + dot_nt(all_v, weights[2][0])
        inner, outer, height, _ = dm_ref.shape
        for distance in range(inner * outer):
            first = range(distance * rows, d_mean.shape[0], ROWS_IMG)
            piece = jnp.concatenate([d_mean[row : row + rows] for row in first], 0)
            dm_ref[distance % inner, distance // inner] = piece.astype(BF16)
        gain_grad = jnp.zeros((D, 1), F32)
        shift_grad = jnp.zeros((1, D), F32)
        gain = jnp.broadcast_to(params_ref[:, 0:D], (8, D)).T[:, 0:1]
        shift = jnp.broadcast_to(params_ref[:, D : 2 * D], (8, D)).T[:, 0:1]
        for block, w_ref in enumerate(weights):
            columns = slice(block * D, (block + 1) * D)
            product = acc_ref[0:D, columns]
            sums = acc_ref[D : D + 1, columns]
            gain_grad += jnp.sum(product * w_ref[0].astype(F32), -1, keepdims=True)
            high = sums.astype(BF16)
            parts = jnp.concatenate([high, (sums - high.astype(F32)).astype(BF16)], 0)
            parts = jnp.concatenate([parts, jnp.zeros((14, D), BF16)], 0)
            shift_grad += jnp.sum(dot_nt(parts, w_ref[0]), 0, keepdims=True)
            acc_ref[0:D, columns] = product * gain + shift * sums
        small_ref[:, 0:D] = jnp.broadcast_to(gain_grad, (D, 128)).T[0:1]
        small_ref[:, D:] = shift_grad
        if pieces:
            write_pieces(place, grads_refs, lambda block, here: acc_ref[here, block * D : (block + 1) * D])
        else:
            for block in range(3):
                grads_refs[0][block] = acc_ref[0:D, block * D : (block + 1) * D].astype(BF16)


def back_call(owner, place, groups, operands, params, slots):
    images, count, _ = operands[0].shape
    rows = count // ROW
    grads = grad_shapes(groups, 3, groups and group_sizes(groups[1]))
    mean_shape = group_sizes(ROWS_IMG // rows) + (images * rows, D)
    return pl.pallas_call(
        functools.partial(back_kernel, groups is not None),
        grid_spec=pltpu.PrefetchScalarGridSpec(
            num_scalar_prefetch=2,
            grid=(images,),
            in_specs=[tile_spec(count, D)] * 5
            + [tile_spec(rows, HEADS, ROW, KEYS), tile_spec(count, D)]
            + [tile_spec(ROWS_IMG, D)] * 2
            + [whole_spec((images, ROWS_IMG, D)), whole_spec(params.shape)]
            + [weight_spec(block) for block in range(3)],
            out_specs=[tile_spec(count, 3 * D), out_whole(mean_shape), out_whole((1, 2 * D))]
            + [out_whole(shape) for shape in grads],
            scratch_shapes=[
                pltpu.VMEM((D + 16, 3 * D), F32),
                pltpu.VMEM((images, ROWS_IMG, D), BF16),
                pltpu.VMEM((images, ROWS_IMG, D), BF16),
            ],
        ),
        out_shape=[
            jax.ShapeDtypeStruct((images, count, 3 * D), BF16),
            jax.ShapeDtypeStruct(mean_shape, BF16),
            jax.ShapeDtypeStruct((1, 2 * D), F32),
        ]
        + [jax.ShapeDtypeStruct(shape, BF16) for shape in grads],
        compiler_params=pltpu.CompilerParams(vmem_limit_bytes=60 * MIB),
        cost_estimate=pl.CostEstimate(
            flops=images * count * D * D * 20, bytes_accessed=images * count * D * 24, transcendentals=0
        ),
        name="attend_back",
    )(owner, place, *operands, params, slots, slots, slots)


def low_kernel(owner, grad_ref, wq_ref, wk_ref, wv_ref, low_ref):
    joined = jnp.concatenate([wq_ref[0], wk_ref[0], wv_ref[0]], 1)
    low_ref[...] = dot_nt(grad_ref[...].reshape(-1, 3 * D), joined).astype(BF16).reshape(low_ref.shape)


def low_call(owner, grads, slots):
    images, count, _ = grads.shape
    return pl.pallas_call(
        low_kernel,
        grid_spec=pltpu.PrefetchScalarGridSpec(
            num_scalar_prefetch=1,
            grid=(images // 2,),
            in_specs=[two_spec(count, 3 * D)] + [weight_spec(block) for block in range(3)],
            out_specs=two_spec(count, D),
        ),
        out_shape=jax.ShapeDtypeStruct((images, count, D), BF16),
        compiler_params=pltpu.CompilerParams(vmem_limit_bytes=60 * MIB),
        cost_estimate=pl.CostEstimate(
            flops=images * count * D * D * 6, bytes_accessed=images * count * D * 8, transcendentals=0
        ),
        name="project_back",
    )(owner, grads, slots, slots, slots)


def last_kernel(start, rows, xh_ref, scale_ref, low_ref, dr_ref, sums_ref, params_ref, out_ref):
    g_ref = params_ref.at[:, 0:D]
    for image, row in itertools.product(range(2), range(rows)):
        mean_row = start + (2 * pl.program_id(0) + image) * rows + row
        here = slice(row * ROW, (row + 1) * ROW)
        normal, spread = xh_ref[image, here, :].astype(F32), scale_ref[image, here, :]
        total = low_ref[image, here, :].astype(F32) + sums_ref[pl.ds(mean_row, 1), :] * (1.0 / ROW)
        d_normal = total * g_ref[...]
        middle = jnp.mean(d_normal, -1, keepdims=True)
        along = jnp.mean(d_normal * normal, -1, keepdims=True)
        out_ref[image, here, :] = dr_ref[image, here, :].astype(F32) + spread * (d_normal - middle - normal * along)


def last_call(normal, scale, d_low, d_branch, sums, start, params):
    images, count, _ = normal.shape
    return pl.pallas_call(
        functools.partial(last_kernel, start, count // ROW),
        grid=(images // 2,),
        in_specs=[two_spec(count, D), two_spec(count, 1), two_spec(count, D), two_spec(count, D)]
        + [whole_spec(sums.shape), whole_spec(params.shape)],
        out_specs=two_spec(count, D),
        out_shape=jax.ShapeDtypeStruct((images, count, D), F32),
        compiler_params=pltpu.CompilerParams(vmem_limit_bytes=60 * MIB),
        cost_estimate=pl.CostEstimate(
            flops=images * count * D * 20, bytes_accessed=images * count * D * 11, transcendentals=0
        ),
        name="norm_one_back",
    )(normal, scale, d_low, d_branch, sums, params)


def adamw_update(weight_now, gradient, first_moment, second_moment, decay_rate, step_rate):
    first_new = 0.9 * first_moment + 0.1 * gradient
    second_new = 0.95 * second_moment + 0.05 * gradient * gradient
    direction = first_new / (1.0 - 0.9**STEP) / (jnp.sqrt(second_new / (1.0 - 0.95**STEP)) + 1e-08)
    return (weight_now - step_rate * (direction + decay_rate * weight_now), first_new, second_new)


def swap(value, axis, bit):
    size = lax.axis_size(axis)
    return lax.ppermute(value, axis, [(index, index ^ bit) for index in range(size)])


def to_rows(values):
    high = lax.reduce_precision(values, 8, 7)
    rows = jnp.concatenate([high, values - high], 1).reshape(-1, D).astype(BF16)
    return jnp.pad(rows, ((0, -rows.shape[0] % 16), (0, 0)))


def from_rows(rows, size):
    count = size // D
    return (rows[:count] + rows[count : 2 * count]).reshape(1, size)


def join(value):
    inner, outer = group_sizes(lax.axis_size("wide"))
    far = jnp.stack([value] + [swap(value, "wide", inner * step) for step in range(1, outer)])
    near = jnp.stack([far] + [swap(far, "wide", step) for step in range(1, inner)], 1)
    return near.reshape((inner * outer,) + value.shape)


def reorder(value, axis, dim=0):
    return jnp.take(value, lax.axis_index(axis) ^ jnp.arange(lax.axis_size(axis)), axis=dim)


def fetch_blocks(low_master, owners, means, whole_pieces):
    wide = lax.axis_size("wide")
    narrow = lax.axis_size("narrow")
    pieces = lax.all_to_all(low_master.reshape(wide, -1, D), "wide", 0, 0, tiled=True)
    mine = jnp.take(pieces, owners, axis=0)
    count, depth, _ = mine.shape
    joined = join(jnp.concatenate([mine.reshape(-1, D), means.reshape(-1, D)], 0))
    mean_all = joined[:, count * depth :].reshape((wide,) + means.shape).swapaxes(0, 1)
    mean_all = mean_all.reshape(means.shape[0], -1, D)
    if whole_pieces:
        return [joined] + [swap(joined, "narrow", step) for step in range(1, narrow)], mean_all
    rows = joined[:, : count * depth]
    halves = jnp.stack([rows] + [swap(rows, "narrow", step) for step in range(1, narrow)])
    halves = reorder(reorder(halves, "narrow"), "wide", 1).reshape(narrow, wide, count, depth, D)
    return [halves.transpose(2, 0, 1, 3, 4).reshape(count, D, D)], mean_all


def piece_lists(grads):
    if len(grads) > 1:
        return list(grads)
    (blocks,) = grads
    narrow = lax.axis_size("narrow")
    wide = lax.axis_size("wide")
    parts = blocks.reshape(blocks.shape[0], narrow, wide, -1, D).transpose(1, 2, 0, 3, 4)
    return list(reorder(parts, "narrow").reshape(narrow, wide, -1, D))


def by_group(pieces):
    inner, outer = group_sizes(lax.axis_size("wide"))
    return pieces.reshape((outer, inner) + pieces.shape[1:]).swapaxes(0, 1)


def sum_narrow(lists):
    total = lists[0].astype(F32)
    for step in range(1, len(lists)):
        total += swap(lists[step], "narrow", step).astype(F32)
    return total.astype(BF16)


def sum_group(pieces, stride):
    total = pieces[0].astype(F32)
    for step in range(1, len(pieces)):
        total += swap(pieces[step], "wide", step * stride).astype(F32)
    return total


def per_device(
    tokens, cotangent, owner_list, master, moment_one, moment_two, small_params, small_one, small_two
):
    images, count, _ = tokens.shape
    rows = count // ROW
    wide = lax.axis_size("wide")
    small = small_params.reshape(1, -1)
    low_master = master.astype(BF16)
    slots = lax.all_gather(low_master.reshape(-1, D), ("wide", "narrow"), axis=0, tiled=True)
    slots = slots.reshape(-1, D, D)
    narrow = lax.axis_size("narrow")
    inner, outer = group_sizes(wide)
    depth = D // narrow // wide
    groups = (narrow, wide) if depth % 16 == 0 and narrow > 1 else None
    me = lax.axis_index("wide")
    names = owner_list[None, :] == jnp.arange(wide, dtype=jnp.int32)[:, None]
    owned = jnp.any(names, 1)
    block_of = jnp.argmax(names, 1)
    place = jnp.stack([me, lax.axis_index("narrow")]).astype(jnp.int32)
    owns_slot = owned[me]
    place, small, owned, owns_slot, block_of, tokens = lax.optimization_barrier(
        (place, small, owned, owns_slot, block_of, tokens)
    )
    normal, scale, means = norm_call(tokens)
    parts, mean_all = fetch_blocks(low_master, owner_list[:3], means, groups is not None)
    queries, keys, values, weights, attended, inverse, sum_k, sum_v = attend_call(
        place, normal, mean_all, small, parts
    )
    block_out, d_branch, d_out, late_small, *grads_late = ff_call(
        owner_list, place, groups, tokens, attended, cotangent, inverse, small, slots
    )

    tie = lax.optimization_barrier
    late, queries = tie((sum_narrow(piece_lists(grads_late)), queries))
    late = lax.all_to_all(late, "wide", 0, 0, tiled=True)
    operands = (queries, keys, values, attended, d_out, weights, normal, sum_k, sum_v, mean_all)
    d_joined, d_mean, early_small, *grads_early = back_call(
        owner_list, place, groups, operands, small, slots
    )
    late, early_small, *grads_early = tie((late, early_small, *grads_early))
    late = jnp.sum(late.astype(F32), 0)
    small_sums = jnp.concatenate([early_small, late_small], 1)
    size = small_sums.shape[1]
    bit = 1
    while bit < narrow:
        small_sums = small_sums + swap(small_sums, "narrow", bit)
        bit *= 2
    early = sum_narrow(piece_lists(grads_early))
    if groups is None:
        early = by_group(reorder(early, "wide"))
    early, small_sums, d_joined = tie((early, small_sums, d_joined))
    d_low = low_call(owner_list, d_joined, slots)

    cuts = (3 * depth, 3 * depth + images * rows)
    small_rows = to_rows(small_sums)
    near = jnp.concatenate([early, d_mean], 2).reshape(inner, outer * cuts[1], D)
    near = sum_group([jnp.concatenate([near[step], small_rows], 0) for step in range(inner)], 1)
    near, late, d_low = tie((near, late, d_low))
    small_rows = to_rows(from_rows(near[outer * cuts[1] :], size))
    far = near[: outer * cuts[1]].astype(BF16).reshape(outer, cuts[1], D)
    far = sum_group([jnp.concatenate([far[step], small_rows], 0) for step in range(outer)], inner)
    small_grad = from_rows(far[cuts[1] :], size).reshape(-1)
    shares = jnp.concatenate([far[: cuts[0]], late], 0).reshape(-1, depth, D).astype(BF16)

    moved = jnp.where(owned[:, None, None], jnp.take(shares, block_of, axis=0), jnp.zeros((), BF16))
    moved = lax.all_to_all(moved, "wide", 0, 0, tiled=True)
    grad_tokens = last_call(normal, scale, d_low, d_branch, far, cuts[0], small)
    moved, grad_tokens = tie((moved, grad_tokens))
    own_grad = moved.reshape(1, -1, D).astype(F32)
    slot_weight, slot_first, slot_second = adamw_update(
        master, own_grad, moment_one, moment_two, 0.1, RATE
    )
    new_master = jnp.where(owns_slot, slot_weight, master)
    new_one = jnp.where(owns_slot, slot_first, moment_one)
    new_two = jnp.where(owns_slot, slot_second, moment_two)
    small_new, small_one_new, small_two_new = adamw_update(
        small_params, small_grad, small_one, small_two, 0.0, GAIN_RATE
    )
    return (block_out, grad_tokens, new_master, new_one, new_two, small_new, small_one_new, small_two_new)


def solution(mesh):
    split = P("narrow", "wide", None)
    slot = P("wide", "narrow", None)
    return jax.shard_map(
        per_device,
        mesh=mesh,
        in_specs=(split, split, P(), slot, slot, slot, P(), P(), P()),
        out_specs=(split, split, slot, slot, slot, P(), P(), P()),
        check_vma=False,
    )
```
